32 devices in a mesh: stream: 2 (over core), dp: 4 (over y, x), tensor: 4 (over z).
Axes of the slice: x: 2, y: 2, z: 4, core: 2. Of those that a mesh axis runs over, the one named last changes fastest.
Arguments:
- hidden: bfloat16 [2, 64, 8192], P('stream', 'tensor', 'dp'), may hold values from -3 to 3
- cached_rotated_keys: bfloat16 [2, 64, 8, 256, 128], P('stream', 'dp', 'tensor'), may hold values from -6 to 6
- cached_values: bfloat16 [2, 64, 8, 256, 128], P('stream', 'dp', 'tensor'), may hold values from -18 to 18
- cache_lengths: int32 [2, 64], P('stream', 'dp'), may hold values from 1 to 256, as said below
- recent_ids: int32 [64, 128], replicated, may hold values from 0 to 8191
- guidance: float32 [64], replicated, may hold values from 1 to 3
- w_query: bfloat16 [8192, 8192], P('dp', 'tensor'), may hold values from -0.0625 to 0.0625
- key_value_weight: bfloat16 [8192, 2, 1024], P('dp', None, 'tensor'), may hold values from -0.0625 to 0.0625
- w_output: bfloat16 [8192, 8192], P('tensor', 'dp'), may hold values from -0.0625 to 0.0625
- norm_gain: bfloat16 [8192], P('dp'), may hold values from 0.5 to 1.5
- w_head: bfloat16 [8192, 8192], P(None, ('dp', 'tensor')), may hold values from -0.16503906 to 0.16503906
Outputs:
- guided_logprobs: float32 [64, 8192], P('stream', ('dp', 'tensor'))
The draws below stay inside these ranges and needn't reach their ends.
Inputs may be any that keep to these rules, and one draw needn't show every extreme that they name: `cache_lengths`: every prompt has 1 to 256 filled slots in each stream; some prompt has all 256; lengths differ widely from one group of 16 prompts to the next.
All inputs are finite; a program needn't handle non-finite values.
Results may differ from the reference program's by a relative error of at most 0.0025.
Values may be sent and summed in bfloat16 or wider, within the bound.
No kernel may reach another device: no remote copies, remote signals or barrier semaphores. Data moves between devices by JAX's collectives and lax.ppermute only.
A program may use at most 64 MiB of HBM per device.

```python
import math
import jax
import jax.numpy as jnp
import numpy as np
from jax import lax

MODEL_WIDTH = 8192
QUERY_HEADS = 64
KEY_VALUE_HEADS = 8
HEAD_SIZE = 128
PROMPT_DEV = 16
CACHE_SLOTS = 256
RECENT = 128
PROMPT_COUNT = 64
VOCAB = 8192


def draw_cache_lengths(key, part):
    first_key, second_key = jax.random.split(jax.random.fold_in(key, 71))
    blocks = PROMPT_COUNT // PROMPT_DEV
    ceiling = jax.random.randint(first_key, (2, blocks, 1), CACHE_SLOTS // 4, CACHE_SLOTS + 1)
    ceiling = jnp.broadcast_to(ceiling, (2, blocks, PROMPT_DEV)).reshape(2, PROMPT_COUNT)
    raw_draw = jax.random.randint(second_key, (2, PROMPT_COUNT), 0, 1048576)
    lengths = 1 + raw_draw % ceiling
    lengths = lengths.at[:, 0].set(CACHE_SLOTS)
    return lengths.astype(jnp.int32)


def touch_ends(result, rng, low, top_value):
    extent = result.shape
    index_at = [jax.random.randint(jax.random.fold_in(rng, axis), (), 0, extent[axis]) for axis in range(len(extent))]
    result = result.at[tuple(index_at)].set(low)
    longest = extent.index(max(extent))
    index_at[longest] = (index_at[longest] + 1) % extent[longest]
    return result.at[tuple(index_at)].set(top_value)


def block_scale(own_key, extent, cuts, low, high):
    level, own = 1.0, jax.random.fold_in(own_key, 6)
    for axis_at, blocks in cuts:
        steps = jnp.exp(jax.random.uniform(jax.random.fold_in(own, axis_at), (blocks,), jnp.float32, low / len(cuts), high / len(cuts)))
        level = level * jnp.repeat(steps, extent[axis_at] // blocks).reshape([-1 if axis == axis_at else 1 for axis in range(len(extent))])
    return level


def rank_bounds(number_of, skew):
    weights = [(1 << 20) // math.isqrt(standing ** skew) + 1 for standing in range(1, number_of + 1)]
    scale = 1 + sum(weights) // (1 << 30)
    return np.cumsum(np.array([max(1, weight // scale) for weight in weights]))


def ranked(stream_key, extent, count, skew):
    table = rank_bounds(count, skew)
    ticket = jax.random.randint(jax.random.fold_in(stream_key, 1), extent, 0, int(table[count - 1]))
    standing = jnp.searchsorted(jnp.asarray(table, jnp.int32), ticket, side="right")
    return jax.random.permutation(jax.random.fold_in(stream_key, 2), count)[standing].astype(jnp.int32)


def scatter_about(stream_key, shape, width, most, pieces=(), kind=jnp.bfloat16):
    gain = block_scale(stream_key, shape, pieces, -0.22, 0.18) if pieces else 1.0
    result = jax.random.normal(stream_key, shape, jnp.float32) * width * gain
    return jnp.minimum(jnp.maximum(result, -most), most).astype(kind)


def setup_inputs(seed: int = 0) -> dict:
    key_of = jax.random.split(jax.random.key(seed), 12)
    return {
        "hidden": scatter_about(key_of[0], (2, PROMPT_COUNT, MODEL_WIDTH), 0.5, 3.0, ((0, 2), (1, 4), (2, 4))),
        "cached_rotated_keys": scatter_about(key_of[1], (2, PROMPT_COUNT, KEY_VALUE_HEADS, CACHE_SLOTS, HEAD_SIZE), 1.0, 6.0, ((0, 2), (1, 4), (2, 4))),
        "cached_values": scatter_about(key_of[2], (2, PROMPT_COUNT, KEY_VALUE_HEADS, CACHE_SLOTS, HEAD_SIZE), 3.0, 18.0, ((0, 2), (1, 4), (2, 4))),
        "cache_lengths": draw_cache_lengths(jax.random.fold_in(key_of[11], 71), 0),
        "recent_ids": touch_ends(ranked(key_of[4], (PROMPT_COUNT, RECENT), VOCAB, 4), jax.random.fold_in(key_of[4], 3), 0, VOCAB - 1).astype(jnp.int32),
        "guidance": jnp.clip(jnp.exp(jax.random.uniform(key_of[5], (PROMPT_COUNT,), jnp.float32, math.log(1.0), math.log(3.0))), 1.0, 3.0),
        "w_query": scatter_about(key_of[6], (MODEL_WIDTH, QUERY_HEADS * HEAD_SIZE), MODEL_WIDTH ** -0.5, 0.0625, ((0, 4), (1, 4))),
        "key_value_weight": scatter_about(key_of[7], (MODEL_WIDTH, 2, KEY_VALUE_HEADS * HEAD_SIZE), MODEL_WIDTH ** -0.5, 0.0625, ((0, 4), (2, 4))),
        "w_output": scatter_about(key_of[8], (QUERY_HEADS * HEAD_SIZE, MODEL_WIDTH), (QUERY_HEADS * HEAD_SIZE) ** -0.5, 0.0625, ((0, 4), (1, 4))),
        "norm_gain": jnp.clip(1.0 + 0.1 * jax.random.normal(key_of[9], (MODEL_WIDTH,), jnp.float32), 0.5, 1.5).astype(jnp.bfloat16),
        "w_head": scatter_about(key_of[10], (MODEL_WIDTH, VOCAB), (2.5 * MODEL_WIDTH ** -0.5), 0.16503906, ((1, 16),)),
    }


rope_theta = 500000.0
penalty_step = 1.5
norm_eps = 1e-05

def rotate(values, positions):
    halfway = values.shape[-1] // 2
    frequency = rope_theta ** (-(jnp.arange(halfway, dtype=jnp.float32) * 2.0 / values.shape[-1]))
    angles = positions.astype(jnp.float32)[:, None, None] * frequency
    cosine_term = jnp.cos(angles)
    sine_term = jnp.sin(angles)
    first_half = values[..., :halfway]
    second_half = values[..., halfway:]
    return jnp.concatenate([first_half * cosine_term - second_half * sine_term, second_half * cosine_term + first_half * sine_term], axis=-1)

def stream_logits(operands, w_query, key_value_weight, w_output, norm_gain, w_head):
    hidden_state_rows, key_cache, value_cache, lengths = operands
    batch_rows = hidden_state_rows.shape[0]
    queries = jnp.dot(hidden_state_rows, w_query, preferred_element_type=jnp.float32)
    key_value_rows = jnp.dot(hidden_state_rows, key_value_weight.reshape(MODEL_WIDTH, 2 * KEY_VALUE_HEADS * HEAD_SIZE), preferred_element_type=jnp.float32).reshape(batch_rows, 2, KEY_VALUE_HEADS, HEAD_SIZE)
    rotated_query = rotate(queries.reshape(batch_rows, QUERY_HEADS, HEAD_SIZE), lengths).astype(jnp.bfloat16)
    fresh_key = rotate(key_value_rows[:, 0], lengths).astype(jnp.bfloat16)
    value_new = key_value_rows[:, 1].astype(jnp.bfloat16)
    grouped_queries = rotated_query.reshape(batch_rows, KEY_VALUE_HEADS, QUERY_HEADS // KEY_VALUE_HEADS, HEAD_SIZE).astype(jnp.float32)
    attention_scale = HEAD_SIZE ** (-0.5)
    scores = jnp.einsum('bkgd,bksd->bkgs', grouped_queries, key_cache.astype(jnp.float32)) * attention_scale
    self_score = jnp.einsum('wxuz,wxz->wxu', grouped_queries, fresh_key.astype(jnp.float32)) * attention_scale
    valid = jnp.arange(CACHE_SLOTS, dtype=jnp.int32)[None, :] < lengths[:, None]
    exps = jnp.where(valid[:, None, None, :], jnp.exp(scores), 0.0)
    own_exp = jnp.exp(self_score)
    denominator = lax.optimization_barrier(jnp.sum(exps, -1)) + own_exp
    weights = (exps / denominator[..., None]).astype(jnp.bfloat16)
    own_weight = (own_exp / denominator).astype(jnp.bfloat16)
    attended = jnp.einsum('bkgs,bksd->bkgd', weights.astype(jnp.float32), value_cache.astype(jnp.float32))
    attended = attended + own_weight.astype(jnp.float32)[..., None] * value_new.astype(jnp.float32)[:, :, None, :]
    attended = attended.reshape(batch_rows, QUERY_HEADS * HEAD_SIZE).astype(jnp.bfloat16)
    projected = jnp.dot(attended, w_output, preferred_element_type=jnp.float32)
    residual = (hidden_state_rows.astype(jnp.float32) + projected).astype(jnp.bfloat16)
    widened = residual.astype(jnp.float32)
    squares = lax.optimization_barrier(jnp.sum(widened * widened, 1))
    inverse = lax.rsqrt(squares / MODEL_WIDTH + norm_eps)
    normed = (widened * inverse[:, None] * norm_gain.astype(jnp.float32)).astype(jnp.bfloat16)
    return jnp.dot(normed, w_head, preferred_element_type=jnp.float32)

def reference(hidden, cached_rotated_keys, cached_values, cache_lengths, recent_ids, guidance, w_query, key_value_weight, w_output, norm_gain, w_head):

    def per_stream(operands):
        return stream_logits(operands, w_query, key_value_weight, w_output, norm_gain, w_head)
    logits = lax.map(per_stream, (hidden, cached_rotated_keys, cached_values, cache_lengths))
    conditional = logits[0]
    unconditional = logits[1]
    guided = unconditional + guidance[:, None] * (conditional - unconditional)

    def add_counts(counts, column_ids):
        hits = (column_ids[:, None] == jnp.arange(VOCAB, dtype=jnp.int32)[None, :]).astype(jnp.float32)
        return (counts + hits, None)
    counts, unused = lax.scan(add_counts, jnp.zeros((PROMPT_COUNT, VOCAB), jnp.float32), recent_ids.T)
    guided = guided - penalty_step * counts
    totals = lax.optimization_barrier(jnp.sum(jnp.exp(guided), 1))
    return guided - jnp.log(totals)[:, None]
```

```python
import jax
import jax.numpy as jnp
from jax import lax
from jax.sharding import PartitionSpec as P

MODEL_WIDTH = 8192
HEAD_SIZE = 128


rope_theta = 500000.0
penalty_step = 1.5
norm_eps = 1e-05


def swap(value, axis, distance):
    if distance == 0:
        return value
    pairs = [(source, source ^ distance) for source in range(lax.axis_size(axis))]
    return lax.ppermute(value, axis, pairs)


def gather_swapped(value, axis):
    return [swap(value, axis, distance) for distance in range(lax.axis_size(axis))]


def rotate(values, positions):
    halfway = values.shape[-1] // 2
    frequency = rope_theta ** (-(jnp.arange(halfway, dtype=jnp.float32) * 2.0 / values.shape[-1]))
    angles = positions.astype(jnp.float32)[:, None, None] * frequency
    cosine_term = jnp.cos(angles)
    sine_term = jnp.sin(angles)
    first_half = values[..., :halfway]
    second_half = values[..., halfway:]
    return jnp.concatenate(
        [
            first_half * cosine_term - second_half * sine_term,
            second_half * cosine_term + first_half * sine_term,
        ],
        axis=-1,
    )


def repeat_counts(recent_ids, first_column, width):
    columns = first_column + jnp.arange(width, dtype=jnp.int32)
    return jnp.sum((recent_ids[:, :, None] == columns[None, None, :]).astype(jnp.float32), 1)


def body(
    hidden,
    cached_rotated_keys,
    cached_values,
    cache_lengths,
    recent_ids,
    guidance,
    w_query,
    key_value_weight,
    w_output,
    norm_gain,
    w_head,
):
    streams, dps, tensors = (lax.axis_size(axis) for axis in ("stream", "dp", "tensor"))
    stream, dp, tensor = (lax.axis_index(axis) for axis in ("stream", "dp", "tensor"))
    local_width = hidden.shape[2]
    query_cols = w_query.shape[1]
    kv_cols = key_value_weight.shape[2]
    local_prompts = cache_lengths.shape[1]
    hidden_prompts = hidden.shape[1]
    prompts = recent_ids.shape[0]
    lengths = cache_lengths[0]
    vocab_local = w_head.shape[1]

    all_rows = jnp.concatenate(gather_swapped(hidden[0], "tensor"), axis=0)
    kv_flat = key_value_weight.reshape(local_width, 2 * kv_cols)
    projected_parts = jnp.concatenate(
        [
            jnp.dot(all_rows, w_query, preferred_element_type=jnp.float32),
            jnp.dot(all_rows, kv_flat, preferred_element_type=jnp.float32),
        ],
        axis=1,
    )

    def hidden_place(prompt):
        block = prompt // hidden_prompts
        return (tensor ^ block) * hidden_prompts + prompt % hidden_prompts

    projected = lax.dynamic_slice_in_dim(
        projected_parts, hidden_place(dp * local_prompts), local_prompts, 0
    )
    for distance in range(1, dps):
        sending = lax.dynamic_slice_in_dim(
            projected_parts, hidden_place((dp ^ distance) * local_prompts), local_prompts, 0
        ).astype(jnp.bfloat16)
        projected = projected + swap(sending, "dp", distance).astype(jnp.float32)

    query_heads = query_cols // HEAD_SIZE
    kv_heads = kv_cols // HEAD_SIZE
    rotated_query = rotate(
        projected[:, :query_cols].reshape(local_prompts, query_heads, HEAD_SIZE), lengths
    ).astype(jnp.bfloat16)
    key_value_rows = projected[:, query_cols:].reshape(local_prompts, 2, kv_heads, HEAD_SIZE)
    fresh_key = rotate(key_value_rows[:, 0], lengths).astype(jnp.bfloat16)
    value_new = key_value_rows[:, 1].astype(jnp.bfloat16)
    grouped_queries = rotated_query.reshape(
        local_prompts, kv_heads, query_heads // kv_heads, HEAD_SIZE
    )
    attention_scale = HEAD_SIZE ** (-0.5)
    key_block = cached_rotated_keys[0]
    value_block = cached_values[0]
    scores = (
        jnp.einsum(
            "pkgd,pksd->pkgs", grouped_queries, key_block, preferred_element_type=jnp.float32
        )
        * attention_scale
    )
    self_score = (
        jnp.einsum("pkgd,pkd->pkg", grouped_queries, fresh_key, preferred_element_type=jnp.float32)
        * attention_scale
    )
    valid = jnp.arange(key_block.shape[2], dtype=jnp.int32)[None, :] < lengths[:, None]
    exps = jnp.where(valid[:, None, None, :], jnp.exp(scores), 0.0)
    own_exp = jnp.exp(self_score)
    denominator = jnp.sum(exps, -1) + own_exp
    weights = (exps / denominator[..., None]).astype(jnp.bfloat16)
    own_weight = (own_exp / denominator).astype(jnp.bfloat16)
    attended = jnp.einsum(
        "pkgs,pksd->pkgd", weights, value_block, preferred_element_type=jnp.float32
    )
    attended = (
        attended
        + own_weight.astype(jnp.float32)[..., None] * value_new.astype(jnp.float32)[:, :, None, :]
    )
    attended = attended.reshape(local_prompts, query_cols).astype(jnp.bfloat16)

    attended_rows = jnp.concatenate(gather_swapped(attended, "dp"), axis=0)
    partial_out = jnp.dot(attended_rows, w_output, preferred_element_type=jnp.float32)

    half = prompts // streams
    share = half // tensors

    def partial_rows(stream_to, tensor_to):
        prompt = stream_to * half + tensor_to * share
        place = (dp ^ (prompt // local_prompts)) * local_prompts + prompt % local_prompts
        return lax.dynamic_slice_in_dim(partial_out, place, share, 0)

    def hidden_rows(stream_to):
        place = hidden_place(stream_to * half + tensor * share)
        return lax.dynamic_slice_in_dim(all_rows, place, share, 0).astype(jnp.float32)

    sums = []
    for stream_distance in range(streams):
        total = None
        for distance in range(tensors):
            rows = partial_rows(stream ^ stream_distance, tensor ^ distance)
            if distance == 0:
                rows = rows + hidden_rows(stream ^ stream_distance)
            if distance or stream_distance:
                joint = stream_distance * tensors + distance
                rows = swap(rows.astype(jnp.bfloat16), ("stream", "tensor"), joint)
                rows = rows.astype(jnp.float32)
            total = rows if total is None else total + rows
        sums.append(total)
    residuals = jnp.stack(sums)
    squares = jnp.sum(residuals * residuals, 2)
    squares = sum(gather_swapped(squares, "dp"))
    inverse = lax.rsqrt(squares / MODEL_WIDTH + norm_eps)
    guide = lax.dynamic_slice_in_dim(guidance, stream * half + tensor * share, share, 0)
    own_guide = jnp.where(stream == 0, guide, 1.0 - guide)
    factors = inverse * jnp.stack([own_guide, 1.0 - own_guide])
    mixed = jnp.sum(residuals * factors[:, :, None], 0) * norm_gain.astype(jnp.float32)
    mixed = mixed.astype(jnp.bfloat16)

    rows = jnp.zeros((half, local_width), jnp.bfloat16)
    for distance, block in enumerate(gather_swapped(mixed, "tensor")):
        rows = lax.dynamic_update_slice_in_dim(rows, block, (tensor ^ distance) * share, 0)
    whole = jnp.zeros((half, local_width * dps), jnp.bfloat16)
    for distance, block in enumerate(gather_swapped(rows, "dp")):
        whole = lax.dynamic_update_slice_in_dim(whole, block, (dp ^ distance) * local_width, 1)
    guided = jnp.dot(whole, w_head, preferred_element_type=jnp.float32)

    column_base = lax.axis_index(("dp", "tensor")) * vocab_local
    recent_mine = lax.dynamic_slice_in_dim(recent_ids, stream * half, half, 0)
    guided = guided - penalty_step * repeat_counts(recent_mine, column_base, vocab_local)
    totals = jnp.sum(jnp.exp(guided), 1)
    totals = sum(gather_swapped(totals, "tensor"))
    totals = sum(gather_swapped(totals, "dp"))
    return guided - jnp.log(totals)[:, None]


def solution(mesh):
    return jax.shard_map(
        body,
        mesh=mesh,
        in_specs=(
            P("stream", "tensor", "dp"),
            P("stream", "dp", "tensor", None, None),
            P("stream", "dp", "tensor", None, None),
            P("stream", "dp"),
            P(),
            P(),
            P("dp", "tensor"),
            P("dp", None, "tensor"),
            P("tensor", "dp"),
            P("dp"),
            P(None, ("dp", "tensor")),
        ),
        out_specs=P("stream", ("dp", "tensor")),
        check_vma=False,
    )
```

```python
import jax
import jax.numpy as jnp
from jax import lax
from jax.sharding import PartitionSpec as P

MODEL_WIDTH = 8192
HEAD_SIZE = 128


rope_theta = 500000.0
penalty_step = 1.5
norm_eps = 1e-05


def exchange(parts, axis):
    return lax.all_to_all(parts, axis, 0, 0, tiled=True)


def gather(value, axis):
    count = lax.axis_size(axis)
    return exchange(jnp.broadcast_to(value[None], (count,) + value.shape), axis)


def rotate(values, positions):
    halfway = values.shape[-1] // 2
    frequency = rope_theta ** (-(jnp.arange(halfway, dtype=jnp.float32) * 2.0 / values.shape[-1]))
    angles = positions.astype(jnp.float32)[:, None, None] * frequency
    cosine_term = jnp.cos(angles)
    sine_term = jnp.sin(angles)
    first_half = values[..., :halfway]
    second_half = values[..., halfway:]
    return jnp.concatenate(
        [
            first_half * cosine_term - second_half * sine_term,
            second_half * cosine_term + first_half * sine_term,
        ],
        axis=-1,
    )


def repeat_counts(recent_ids, first_column, width):
    columns = first_column + jnp.arange(width, dtype=jnp.int32)
    return jnp.sum((recent_ids[:, :, None] == columns[None, None, :]).astype(jnp.float32), 1)


def body(
    hidden,
    cached_rotated_keys,
    cached_values,
    cache_lengths,
    recent_ids,
    guidance,
    w_query,
    key_value_weight,
    w_output,
    norm_gain,
    w_head,
):
    streams, dps, tensors = (lax.axis_size(axis) for axis in ("stream", "dp", "tensor"))
    stream, tensor = (lax.axis_index(axis) for axis in ("stream", "tensor"))
    local_width = hidden.shape[2]
    query_cols = w_query.shape[1]
    kv_cols = key_value_weight.shape[2]
    local_prompts = cache_lengths.shape[1]
    prompts = recent_ids.shape[0]
    lengths = cache_lengths[0]
    vocab_local = w_head.shape[1]

    all_rows = gather(hidden[0], "tensor").reshape(prompts, local_width)
    kv_flat = key_value_weight.reshape(local_width, 2 * kv_cols)
    projected_parts = jnp.concatenate(
        [
            jnp.dot(all_rows, w_query, preferred_element_type=jnp.float32),
            jnp.dot(all_rows, kv_flat, preferred_element_type=jnp.float32),
        ],
        axis=1,
    )

    sending = projected_parts.astype(jnp.bfloat16).reshape(dps, local_prompts, -1)
    projected = jnp.sum(exchange(sending, "dp").astype(jnp.float32), 0)

    query_heads = query_cols // HEAD_SIZE
    kv_heads = kv_cols // HEAD_SIZE
    rotated_query = rotate(
        projected[:, :query_cols].reshape(local_prompts, query_heads, HEAD_SIZE), lengths
    ).astype(jnp.bfloat16)
    key_value_rows = projected[:, query_cols:].reshape(local_prompts, 2, kv_heads, HEAD_SIZE)
    fresh_key = rotate(key_value_rows[:, 0], lengths).astype(jnp.bfloat16)
    value_new = key_value_rows[:, 1].astype(jnp.bfloat16)
    grouped_queries = rotated_query.reshape(
        local_prompts, kv_heads, query_heads // kv_heads, HEAD_SIZE
    )
    attention_scale = HEAD_SIZE ** (-0.5)
    key_block = cached_rotated_keys[0]
    value_block = cached_values[0]
    scores = (
        jnp.einsum(
            "pkgd,pksd->pkgs", grouped_queries, key_block, preferred_element_type=jnp.float32
        )
        * attention_scale
    )
    self_score = (
        jnp.einsum("pkgd,pkd->pkg", grouped_queries, fresh_key, preferred_element_type=jnp.float32)
        * attention_scale
    )
    valid = jnp.arange(key_block.shape[2], dtype=jnp.int32)[None, :] < lengths[:, None]
    exps = jnp.where(valid[:, None, None, :], jnp.exp(scores), 0.0)
    own_exp = jnp.exp(self_score)
    denominator = jnp.sum(exps, -1) + own_exp
    weights = (exps / denominator[..., None]).astype(jnp.bfloat16)
    own_weight = (own_exp / denominator).astype(jnp.bfloat16)
    attended = jnp.einsum(
        "pkgs,pksd->pkgd", weights, value_block, preferred_element_type=jnp.float32
    )
    attended = (
        attended
        + own_weight.astype(jnp.float32)[..., None] * value_new.astype(jnp.float32)[:, :, None, :]
    )
    attended = attended.reshape(local_prompts, query_cols).astype(jnp.bfloat16)

    attended_rows = gather(attended, "dp").reshape(prompts, query_cols)
    partial_out = jnp.dot(attended_rows, w_output, preferred_element_type=jnp.float32)

    half = prompts // streams
    share = half // tensors
    sending = partial_out.reshape(streams, tensors, share, local_width)
    same = (jnp.arange(tensors) == tensor)[None, :, None, None]
    hidden_parts = all_rows.reshape(sending.shape).astype(jnp.float32)
    sending = (sending + jnp.where(same, hidden_parts, 0.0)).astype(jnp.bfloat16)
    sending = sending.reshape(streams * tensors, share, local_width)
    arrived = exchange(sending, ("stream", "tensor"))
    arrived = arrived.reshape(streams, tensors, share, local_width)
    residuals = jnp.sum(arrived.astype(jnp.float32), 1)
    squares = jnp.sum(residuals * residuals, 2)
    squares = jnp.sum(gather(squares, "dp"), 0)
    inverse = lax.rsqrt(squares / MODEL_WIDTH + norm_eps)
    guide = lax.dynamic_slice_in_dim(guidance, stream * half + tensor * share, share, 0)
    factors = inverse * jnp.stack([guide, 1.0 - guide])
    mixed = jnp.sum(residuals * factors[:, :, None], 0) * norm_gain.astype(jnp.float32)
    mixed = mixed.astype(jnp.bfloat16)

    rows = gather(mixed, "tensor").reshape(half, local_width)
    whole = gather(rows, "dp").transpose(1, 0, 2).reshape(half, dps * local_width)
    guided = jnp.dot(whole, w_head, preferred_element_type=jnp.float32)

    column_base = lax.axis_index(("dp", "tensor")) * vocab_local
    recent_mine = lax.dynamic_slice_in_dim(recent_ids, stream * half, half, 0)
    guided = guided - penalty_step * repeat_counts(recent_mine, column_base, vocab_local)
    totals = jnp.sum(jnp.exp(guided), 1)
    totals = jnp.sum(gather(totals, ("dp", "tensor")), 0)
    return guided - jnp.log(totals)[:, None]


def solution(mesh):
    return jax.shard_map(
        body,
        mesh=mesh,
        in_specs=(
            P("stream", "tensor", "dp"),
            P("stream", "dp", "tensor", None, None),
            P("stream", "dp", "tensor", None, None),
            P("stream", "dp"),
            P(),
            P(),
            P("dp", "tensor"),
            P("dp", None, "tensor"),
            P("tensor", "dp"),
            P("dp"),
            P(None, ("dp", "tensor")),
        ),
        out_specs=P("stream", ("dp", "tensor")),
        check_vma=False,
    )
```

```python
import jax
import jax.numpy as jnp
from jax import lax
from jax.sharding import PartitionSpec as P

MODEL_WIDTH = 8192
HEAD_SIZE = 128


rope_theta = 500000.0
penalty_step = 1.5
norm_eps = 1e-05


def swap(value, axis, distance):
    if distance == 0:
        return value
    pairs = [(source, source ^ distance) for source in range(lax.axis_size(axis))]
    return lax.ppermute(value, axis, pairs)


def gather_swapped(value, axis):
    return [swap(value, axis, distance) for distance in range(lax.axis_size(axis))]


def halving_distances(axis):
    distances, size = [], lax.axis_size(axis)
    while size > 1:
        distances.append(size - 1)
        size //= 2
    return distances


def span(distances):
    offsets = [0]
    for distance in distances:
        offsets = offsets + [offset ^ distance for offset in offsets]
    return offsets


def gather_doubling(value, axis):
    for distance in halving_distances(axis):
        value = jnp.concatenate([value, swap(value, axis, distance)], axis=0)
    return value


def scatter_halving(blocks, axis):
    distances = halving_distances(axis)[::-1]
    blocks = dict(enumerate(blocks))
    for step, distance in enumerate(distances):
        kept = span(distances[step + 1 :])
        rows = blocks[0].shape[0]
        sending = jnp.concatenate([blocks[offset ^ distance] for offset in kept], axis=0)
        arrived = swap(sending.astype(jnp.bfloat16), axis, distance).astype(jnp.float32)
        blocks = {
            offset: blocks[offset] + arrived[place * rows : (place + 1) * rows]
            for place, offset in enumerate(kept)
        }
    return blocks[0]


def sum_doubling(value, axis):
    distance = 1
    while distance < lax.axis_size(axis):
        value = value + swap(value, axis, distance)
        distance *= 2
    return value


def rotate(values, positions):
    halfway = values.shape[-1] // 2
    frequency = rope_theta ** (-(jnp.arange(halfway, dtype=jnp.float32) * 2.0 / values.shape[-1]))
    angles = positions.astype(jnp.float32)[:, None, None] * frequency
    cosine_term = jnp.cos(angles)
    sine_term = jnp.sin(angles)
    first_half = values[..., :halfway]
    second_half = values[..., halfway:]
    return jnp.concatenate(
        [
            first_half * cosine_term - second_half * sine_term,
            second_half * cosine_term + first_half * sine_term,
        ],
        axis=-1,
    )


def repeat_counts(recent_ids, first_column, width):
    columns = first_column + jnp.arange(width, dtype=jnp.int32)
    return jnp.sum((recent_ids[:, :, None] == columns[None, None, :]).astype(jnp.float32), 1)


def body(
    hidden,
    cached_rotated_keys,
    cached_values,
    cache_lengths,
    recent_ids,
    guidance,
    w_query,
    key_value_weight,
    w_output,
    norm_gain,
    w_head,
):
    streams, dps, tensors = (lax.axis_size(axis) for axis in ("stream", "dp", "tensor"))
    stream, dp, tensor = (lax.axis_index(axis) for axis in ("stream", "dp", "tensor"))
    local_width = hidden.shape[2]
    query_cols = w_query.shape[1]
    kv_cols = key_value_weight.shape[2]
    local_prompts = cache_lengths.shape[1]
    hidden_prompts = hidden.shape[1]
    prompts = recent_ids.shape[0]
    lengths = cache_lengths[0]
    vocab_local = w_head.shape[1]

    all_rows = gather_doubling(hidden[0], "tensor")
    hidden_order = span(halving_distances("tensor"))
    kv_flat = key_value_weight.reshape(local_width, 2 * kv_cols)
    projected_parts = jnp.concatenate(
        [
            jnp.dot(all_rows, w_query, preferred_element_type=jnp.float32),
            jnp.dot(all_rows, kv_flat, preferred_element_type=jnp.float32),
        ],
        axis=1,
    )

    def hidden_place(prompt):
        block = prompt // hidden_prompts
        place = sum(jnp.where((tensor ^ block) == o, i, 0) for i, o in enumerate(hidden_order))
        return place * hidden_prompts + prompt % hidden_prompts

    projected = lax.dynamic_slice_in_dim(
        projected_parts, hidden_place(dp * local_prompts), local_prompts, 0
    )
    for distance in range(1, dps):
        sending = lax.dynamic_slice_in_dim(
            projected_parts, hidden_place((dp ^ distance) * local_prompts), local_prompts, 0
        ).astype(jnp.bfloat16)
        projected = projected + swap(sending, "dp", distance).astype(jnp.float32)

    query_heads = query_cols // HEAD_SIZE
    kv_heads = kv_cols // HEAD_SIZE
    rotated_query = rotate(
        projected[:, :query_cols].reshape(local_prompts, query_heads, HEAD_SIZE), lengths
    ).astype(jnp.bfloat16)
    key_value_rows = projected[:, query_cols:].reshape(local_prompts, 2, kv_heads, HEAD_SIZE)
    fresh_key = rotate(key_value_rows[:, 0], lengths).astype(jnp.bfloat16)
    value_new = key_value_rows[:, 1].astype(jnp.bfloat16)
    grouped_queries = rotated_query.reshape(
        local_prompts, kv_heads, query_heads // kv_heads, HEAD_SIZE
    )
    attention_scale = HEAD_SIZE ** (-0.5)
    key_block = cached_rotated_keys[0]
    value_block = cached_values[0]
    scores = (
        jnp.einsum(
            "pkgd,pksd->pkgs", grouped_queries, key_block, preferred_element_type=jnp.float32
        )
        * attention_scale
    )
    self_score = (
        jnp.einsum("pkgd,pkd->pkg", grouped_queries, fresh_key, preferred_element_type=jnp.float32)
        * attention_scale
    )
    valid = jnp.arange(key_block.shape[2], dtype=jnp.int32)[None, :] < lengths[:, None]
    exps = jnp.where(valid[:, None, None, :], jnp.exp(scores), 0.0)
    own_exp = jnp.exp(self_score)
    denominator = jnp.sum(exps, -1) + own_exp
    weights = (exps / denominator[..., None]).astype(jnp.bfloat16)
    own_weight = (own_exp / denominator).astype(jnp.bfloat16)
    attended = jnp.einsum(
        "pkgs,pksd->pkgd", weights, value_block, preferred_element_type=jnp.float32
    )
    attended = (
        attended
        + own_weight.astype(jnp.float32)[..., None] * value_new.astype(jnp.float32)[:, :, None, :]
    )
    attended = attended.reshape(local_prompts, query_cols).astype(jnp.bfloat16)

    attended_rows = jnp.concatenate(gather_swapped(attended, "dp"), axis=0)
    partial_out = jnp.dot(attended_rows, w_output, preferred_element_type=jnp.float32)

    half = prompts // streams
    share = half // tensors

    def partial_rows(stream_to, tensor_to):
        prompt = stream_to * half + tensor_to * share
        place = (dp ^ (prompt // local_prompts)) * local_prompts + prompt % local_prompts
        return lax.dynamic_slice_in_dim(partial_out, place, share, 0)

    def hidden_rows(stream_to):
        place = hidden_place(stream_to * half + tensor * share)
        return lax.dynamic_slice_in_dim(all_rows, place, share, 0).astype(jnp.float32)

    summed = scatter_halving(
        [
            jnp.concatenate(
                [partial_rows(stream ^ other, tensor ^ offset) for other in range(streams)], 0
            )
            for offset in range(tensors)
        ],
        "tensor",
    )
    summed = summed.reshape(streams, share, local_width)
    residuals = [
        (summed[other] + hidden_rows(stream ^ other)).astype(jnp.bfloat16)
        for other in range(streams)
    ]
    residuals = [swap(rows, "stream", other) for other, rows in enumerate(residuals)]
    residuals = jnp.stack(residuals).astype(jnp.float32)
    squares = sum_doubling(jnp.sum(residuals * residuals, 2), "dp")
    inverse = lax.rsqrt(squares / MODEL_WIDTH + norm_eps)
    guide = lax.dynamic_slice_in_dim(guidance, stream * half + tensor * share, share, 0)
    own_guide = jnp.where(stream == 0, guide, 1.0 - guide)
    factors = inverse * jnp.stack([own_guide, 1.0 - own_guide])
    mixed = jnp.sum(residuals * factors[:, :, None], 0) * norm_gain.astype(jnp.float32)
    mixed = mixed.astype(jnp.bfloat16)

    rows = jnp.zeros((half, local_width), jnp.bfloat16)
    gathered = gather_doubling(mixed, "tensor")
    for place, offset in enumerate(hidden_order):
        block = gathered[place * share : (place + 1) * share]
        rows = lax.dynamic_update_slice_in_dim(rows, block, (tensor ^ offset) * share, 0)
    whole = jnp.zeros((half, local_width * dps), jnp.bfloat16)
    for distance, block in enumerate(gather_swapped(rows, "dp")):
        whole = lax.dynamic_update_slice_in_dim(whole, block, (dp ^ distance) * local_width, 1)
    guided = jnp.dot(whole, w_head, preferred_element_type=jnp.float32)

    column_base = lax.axis_index(("dp", "tensor")) * vocab_local
    recent_mine = lax.dynamic_slice_in_dim(recent_ids, stream * half, half, 0)
    guided = guided - penalty_step * repeat_counts(recent_mine, column_base, vocab_local)
    totals = jnp.sum(jnp.exp(guided), 1)
    totals = sum_doubling(sum_doubling(totals, "dp"), "tensor")
    return guided - jnp.log(totals)[:, None]


def solution(mesh):
    return jax.shard_map(
        body,
        mesh=mesh,
        in_specs=(
            P("stream", "tensor", "dp"),
            P("stream", "dp", "tensor", None, None),
            P("stream", "dp", "tensor", None, None),
            P("stream", "dp"),
            P(),
            P(),
            P("dp", "tensor"),
            P("dp", None, "tensor"),
            P("tensor", "dp"),
            P("dp"),
            P(None, ("dp", "tensor")),
        ),
        out_specs=P("stream", ("dp", "tensor")),
        check_vma=False,
    )
```

```python
import jax
import jax.numpy as jnp
from jax import lax
from jax.sharding import PartitionSpec as P

MODEL_WIDTH = 8192
HEAD_SIZE = 128


rope_theta = 500000.0
penalty_step = 1.5
norm_eps = 1e-05


def swap(value, axis, distance, stream=None):
    if distance == 0:
        return value
    size = lax.axis_size(axis)
    if stream is None:
        return lax.ppermute(value, axis, [(i, i ^ distance) for i in range(size)])
    base = stream * size
    pairs = [(base + i, base + (i ^ distance)) for i in range(size)]
    return lax.ppermute(value, ("stream", axis), pairs)


def gather_swapped(value, axis, stream=None):
    return [swap(value, axis, distance, stream) for distance in range(lax.axis_size(axis))]


def sum_totals(value, axes):
    count = lax.axis_size(axes)
    copies = jnp.broadcast_to(value[None], (count,) + value.shape)
    return jnp.sum(lax.all_to_all(copies, axes, 0, 0, tiled=True), 0)


def rotate(values, positions):
    halfway = values.shape[-1] // 2
    frequency = rope_theta ** (-(jnp.arange(halfway, dtype=jnp.float32) * 2.0 / values.shape[-1]))
    angles = positions.astype(jnp.float32)[:, None, None] * frequency
    cosine_term = jnp.cos(angles)
    sine_term = jnp.sin(angles)
    first_half = values[..., :halfway]
    second_half = values[..., halfway:]
    return jnp.concatenate(
        [
            first_half * cosine_term - second_half * sine_term,
            second_half * cosine_term + first_half * sine_term,
        ],
        axis=-1,
    )


def repeat_counts(recent_ids, first_column, width):
    columns = first_column + jnp.arange(width, dtype=jnp.int32)
    return jnp.sum((recent_ids[:, :, None] == columns[None, None, :]).astype(jnp.float32), 1)


def body(
    hidden,
    cached_rotated_keys,
    cached_values,
    cache_lengths,
    recent_ids,
    guidance,
    w_query,
    key_value_weight,
    w_output,
    norm_gain,
    w_head,
):
    streams, dps, tensors = (lax.axis_size(axis) for axis in ("stream", "dp", "tensor"))
    stream, dp, tensor = (lax.axis_index(axis) for axis in ("stream", "dp", "tensor"))
    local_width = hidden.shape[2]
    query_cols = w_query.shape[1]
    kv_cols = key_value_weight.shape[2]
    local_prompts = cache_lengths.shape[1]
    hidden_prompts = hidden.shape[1]
    lead = streams - 1
    prompts = recent_ids.shape[0]
    lengths = cache_lengths[0]
    vocab_local = w_head.shape[1]

    all_rows = jnp.concatenate(gather_swapped(hidden[0], "tensor"), axis=0)
    kv_flat = key_value_weight.reshape(local_width, 2 * kv_cols)
    projected_parts = jnp.concatenate(
        [
            jnp.dot(all_rows, w_query, preferred_element_type=jnp.float32),
            jnp.dot(all_rows, kv_flat, preferred_element_type=jnp.float32),
        ],
        axis=1,
    )

    def hidden_place(prompt):
        block = prompt // hidden_prompts
        return (tensor ^ block) * hidden_prompts + prompt % hidden_prompts

    projected = lax.dynamic_slice_in_dim(
        projected_parts, hidden_place(dp * local_prompts), local_prompts, 0
    )
    for distance in range(1, dps):
        sending = lax.dynamic_slice_in_dim(
            projected_parts, hidden_place((dp ^ distance) * local_prompts), local_prompts, 0
        ).astype(jnp.bfloat16)
        projected = projected + swap(sending, "dp", distance).astype(jnp.float32)

    query_heads = query_cols // HEAD_SIZE
    kv_heads = kv_cols // HEAD_SIZE
    rotated_query = rotate(
        projected[:, :query_cols].reshape(local_prompts, query_heads, HEAD_SIZE), lengths
    ).astype(jnp.bfloat16)
    key_value_rows = projected[:, query_cols:].reshape(local_prompts, 2, kv_heads, HEAD_SIZE)
    fresh_key = rotate(key_value_rows[:, 0], lengths).astype(jnp.bfloat16)
    value_new = key_value_rows[:, 1].astype(jnp.bfloat16)
    grouped_queries = rotated_query.reshape(
        local_prompts, kv_heads, query_heads // kv_heads, HEAD_SIZE
    )
    attention_scale = HEAD_SIZE ** (-0.5)
    key_block = cached_rotated_keys[0]
    value_block = cached_values[0]
    scores = (
        jnp.einsum(
            "pkgd,pksd->pkgs", grouped_queries, key_block, preferred_element_type=jnp.float32
        )
        * attention_scale
    )
    self_score = (
        jnp.einsum("pkgd,pkd->pkg", grouped_queries, fresh_key, preferred_element_type=jnp.float32)
        * attention_scale
    )
    valid = jnp.arange(key_block.shape[2], dtype=jnp.int32)[None, :] < lengths[:, None]
    exps = jnp.where(valid[:, None, None, :], jnp.exp(scores), 0.0)
    own_exp = jnp.exp(self_score)
    denominator = jnp.sum(exps, -1) + own_exp
    weights = (exps / denominator[..., None]).astype(jnp.bfloat16)
    own_weight = (own_exp / denominator).astype(jnp.bfloat16)
    attended = jnp.einsum(
        "pkgs,pksd->pkgd", weights, value_block, preferred_element_type=jnp.float32
    )
    attended = (
        attended
        + own_weight.astype(jnp.float32)[..., None] * value_new.astype(jnp.float32)[:, :, None, :]
    )
    attended = attended.reshape(local_prompts, query_cols).astype(jnp.bfloat16)

    handed = lax.ppermute(attended, "stream", [(0, lead)])
    hidden_first = lax.ppermute(hidden[0], "stream", [(0, lead)])
    attended_pair = jnp.concatenate([handed, attended], axis=0)

    attended_rows = jnp.concatenate(gather_swapped(attended_pair, "dp", lead), axis=0)
    partial_out = jnp.dot(attended_rows, w_output, preferred_element_type=jnp.float32)
    partial_out = partial_out.reshape(dps, streams, local_prompts, local_width)

    pieces = hidden_prompts // local_prompts

    def partial_rows(tensor_to):
        return jnp.concatenate(
            [
                lax.dynamic_slice_in_dim(partial_out, dp ^ (tensor_to * pieces + i), 1, 0)
                for i in range(pieces)
            ],
            axis=0,
        )

    summed = partial_rows(tensor)
    for distance in range(1, tensors):
        sending = partial_rows(tensor ^ distance).astype(jnp.bfloat16)
        summed = summed + swap(sending, "tensor", distance, lead).astype(jnp.float32)
    hidden_pair = jnp.stack([hidden_first, hidden[0]])
    hidden_pair = hidden_pair.reshape(streams, pieces, local_prompts, local_width)
    summed = summed.transpose(1, 0, 2, 3) + hidden_pair.astype(jnp.float32)
    residuals = summed.reshape(streams, hidden_prompts, local_width)
    squares = jnp.sum(residuals * residuals, 2)
    squares = sum(gather_swapped(squares, "dp", lead))
    inverse = lax.rsqrt(squares / MODEL_WIDTH + norm_eps)
    guide = lax.dynamic_slice_in_dim(guidance, tensor * hidden_prompts, hidden_prompts, 0)
    factors = inverse * jnp.stack([guide, 1.0 - guide])
    mixed = jnp.sum(residuals * factors[:, :, None], 0) * norm_gain.astype(jnp.float32)
    mixed = mixed.astype(jnp.bfloat16)

    rows = jnp.zeros((prompts, local_width), jnp.bfloat16)
    for distance, block in enumerate(gather_swapped(mixed, "tensor", lead)):
        place = (tensor ^ distance) * hidden_prompts
        rows = lax.dynamic_update_slice_in_dim(rows, block, place, 0)
    whole = jnp.zeros((prompts, local_width * dps), jnp.bfloat16)
    for distance, block in enumerate(gather_swapped(rows, "dp", lead)):
        whole = lax.dynamic_update_slice_in_dim(whole, block, (dp ^ distance) * local_width, 1)
    guided = jnp.dot(whole, w_head, preferred_element_type=jnp.float32)

    column_base = lax.axis_index(("dp", "tensor")) * vocab_local
    guided = guided - penalty_step * repeat_counts(recent_ids, column_base, vocab_local)
    totals = sum_totals(jnp.sum(jnp.exp(guided), 1), ("dp", "tensor"))
    result = guided - jnp.log(totals)[:, None]
    half = prompts // streams
    returned = lax.ppermute(result[:half], "stream", [(lead, 0)])
    return jnp.where(stream == lead, result[lead * half :], returned)


def solution(mesh):
    return jax.shard_map(
        body,
        mesh=mesh,
        in_specs=(
            P("stream", "tensor", "dp"),
            P("stream", "dp", "tensor", None, None),
            P("stream", "dp", "tensor", None, None),
            P("stream", "dp"),
            P(),
            P(),
            P("dp", "tensor"),
            P("dp", None, "tensor"),
            P("tensor", "dp"),
            P("dp"),
            P(None, ("dp", "tensor")),
        ),
        out_specs=P("stream", ("dp", "tensor")),
        check_vma=False,
    )
```

```python
import jax
import jax.numpy as jnp
from jax import lax
from jax.sharding import PartitionSpec as P

MODEL_WIDTH = 8192
HEAD_SIZE = 128


rope_theta = 500000.0
penalty_step = 1.5
norm_eps = 1e-05


def swap(value, axis, distance, stream=None):
    if distance == 0:
        return value
    size = lax.axis_size(axis)
    if stream is None:
        return lax.ppermute(value, axis, [(i, i ^ distance) for i in range(size)])
    base = stream * size
    pairs = [(i, i) for i in range(size * lax.axis_size("stream"))]
    pairs[base : base + size] = [(base + i, base + (i ^ distance)) for i in range(size)]
    return lax.ppermute(value, ("stream", axis), pairs)


def gather_swapped(value, axis, stream=None):
    return [swap(value, axis, distance, stream) for distance in range(lax.axis_size(axis))]


def sum_totals(value, axes):
    count = lax.axis_size(axes)
    copies = jnp.broadcast_to(value[None], (count,) + value.shape)
    return jnp.sum(lax.all_to_all(copies, axes, 0, 0, tiled=True), 0)


def rotate(values, positions):
    halfway = values.shape[-1] // 2
    frequency = rope_theta ** (-(jnp.arange(halfway, dtype=jnp.float32) * 2.0 / values.shape[-1]))
    angles = positions.astype(jnp.float32)[:, None, None] * frequency
    cosine_term = jnp.cos(angles)
    sine_term = jnp.sin(angles)
    first_half = values[..., :halfway]
    second_half = values[..., halfway:]
    return jnp.concatenate(
        [
            first_half * cosine_term - second_half * sine_term,
            second_half * cosine_term + first_half * sine_term,
        ],
        axis=-1,
    )


def repeat_counts(recent_ids, first_column, width):
    columns = first_column + jnp.arange(width, dtype=jnp.int32)
    return jnp.sum((recent_ids[:, :, None] == columns[None, None, :]).astype(jnp.float32), 1)


def body(
    hidden,
    cached_rotated_keys,
    cached_values,
    cache_lengths,
    recent_ids,
    guidance,
    w_query,
    key_value_weight,
    w_output,
    norm_gain,
    w_head,
):
    streams, dps, tensors = (lax.axis_size(axis) for axis in ("stream", "dp", "tensor"))
    stream, dp, tensor = (lax.axis_index(axis) for axis in ("stream", "dp", "tensor"))
    local_width = hidden.shape[2]
    query_cols = w_query.shape[1]
    kv_cols = key_value_weight.shape[2]
    local_prompts = cache_lengths.shape[1]
    hidden_prompts = hidden.shape[1]
    lead = streams - 1
    prompts = recent_ids.shape[0]
    lengths = cache_lengths[0]
    vocab_local = w_head.shape[1]

    all_rows = jnp.concatenate(gather_swapped(hidden[0], "tensor"), axis=0)
    kv_flat = key_value_weight.reshape(local_width, 2 * kv_cols)
    projected_parts = jnp.concatenate(
        [
            jnp.dot(all_rows, w_query, preferred_element_type=jnp.float32),
            jnp.dot(all_rows, kv_flat, preferred_element_type=jnp.float32),
        ],
        axis=1,
    )

    def hidden_place(prompt):
        block = prompt // hidden_prompts
        return (tensor ^ block) * hidden_prompts + prompt % hidden_prompts

    projected = lax.dynamic_slice_in_dim(
        projected_parts, hidden_place(dp * local_prompts), local_prompts, 0
    )
    for distance in range(1, dps):
        sending = lax.dynamic_slice_in_dim(
            projected_parts, hidden_place((dp ^ distance) * local_prompts), local_prompts, 0
        ).astype(jnp.bfloat16)
        projected = projected + swap(sending, "dp", distance).astype(jnp.float32)

    query_heads = query_cols // HEAD_SIZE
    kv_heads = kv_cols // HEAD_SIZE
    rotated_query = rotate(
        projected[:, :query_cols].reshape(local_prompts, query_heads, HEAD_SIZE), lengths
    ).astype(jnp.bfloat16)
    key_value_rows = projected[:, query_cols:].reshape(local_prompts, 2, kv_heads, HEAD_SIZE)
    fresh_key = rotate(key_value_rows[:, 0], lengths).astype(jnp.bfloat16)
    value_new = key_value_rows[:, 1].astype(jnp.bfloat16)
    grouped_queries = rotated_query.reshape(
        local_prompts, kv_heads, query_heads // kv_heads, HEAD_SIZE
    )
    attention_scale = HEAD_SIZE ** (-0.5)
    key_block = cached_rotated_keys[0]
    value_block = cached_values[0]
    scores = (
        jnp.einsum(
            "pkgd,pksd->pkgs", grouped_queries, key_block, preferred_element_type=jnp.float32
        )
        * attention_scale
    )
    self_score = (
        jnp.einsum("pkgd,pkd->pkg", grouped_queries, fresh_key, preferred_element_type=jnp.float32)
        * attention_scale
    )
    valid = jnp.arange(key_block.shape[2], dtype=jnp.int32)[None, :] < lengths[:, None]
    exps = jnp.where(valid[:, None, None, :], jnp.exp(scores), 0.0)
    own_exp = jnp.exp(self_score)
    denominator = jnp.sum(exps, -1) + own_exp
    weights = (exps / denominator[..., None]).astype(jnp.bfloat16)
    own_weight = (own_exp / denominator).astype(jnp.bfloat16)
    attended = jnp.einsum(
        "pkgs,pksd->pkgd", weights, value_block, preferred_element_type=jnp.float32
    )
    attended = (
        attended
        + own_weight.astype(jnp.float32)[..., None] * value_new.astype(jnp.float32)[:, :, None, :]
    )
    attended = attended.reshape(local_prompts, query_cols).astype(jnp.bfloat16)

    handed = swap(attended, "stream", lead)
    hidden_first = swap(hidden[0], "stream", lead)
    attended_pair = jnp.concatenate([handed, attended], axis=0)

    attended_rows = jnp.concatenate(gather_swapped(attended_pair, "dp", lead), axis=0)
    partial_out = jnp.dot(attended_rows, w_output, preferred_element_type=jnp.float32)
    partial_out = partial_out.reshape(dps, streams, local_prompts, local_width)

    pieces = hidden_prompts // local_prompts

    def partial_rows(tensor_to):
        return jnp.concatenate(
            [
                lax.dynamic_slice_in_dim(partial_out, dp ^ (tensor_to * pieces + i), 1, 0)
                for i in range(pieces)
            ],
            axis=0,
        )

    summed = partial_rows(tensor)
    for distance in range(1, tensors):
        sending = partial_rows(tensor ^ distance).astype(jnp.bfloat16)
        summed = summed + swap(sending, "tensor", distance, lead).astype(jnp.float32)
    hidden_pair = jnp.stack([hidden_first, hidden[0]])
    hidden_pair = hidden_pair.reshape(streams, pieces, local_prompts, local_width)
    summed = summed.transpose(1, 0, 2, 3) + hidden_pair.astype(jnp.float32)
    residuals = summed.reshape(streams, hidden_prompts, local_width)
    squares = jnp.sum(residuals * residuals, 2)
    squares = sum(gather_swapped(squares, "dp", lead))
    inverse = lax.rsqrt(squares / MODEL_WIDTH + norm_eps)
    guide = lax.dynamic_slice_in_dim(guidance, tensor * hidden_prompts, hidden_prompts, 0)
    factors = inverse * jnp.stack([guide, 1.0 - guide])
    mixed = jnp.sum(residuals * factors[:, :, None], 0) * norm_gain.astype(jnp.float32)
    mixed = mixed.astype(jnp.bfloat16)

    rows = jnp.zeros((prompts, local_width), jnp.bfloat16)
    for distance, block in enumerate(gather_swapped(mixed, "tensor", lead)):
        place = (tensor ^ distance) * hidden_prompts
        rows = lax.dynamic_update_slice_in_dim(rows, block, place, 0)
    whole = jnp.zeros((prompts, local_width * dps), jnp.bfloat16)
    for distance, block in enumerate(gather_swapped(rows, "dp", lead)):
        whole = lax.dynamic_update_slice_in_dim(whole, block, (dp ^ distance) * local_width, 1)
    guided = jnp.dot(whole, w_head, preferred_element_type=jnp.float32)

    column_base = lax.axis_index(("dp", "tensor")) * vocab_local
    guided = guided - penalty_step * repeat_counts(recent_ids, column_base, vocab_local)
    totals = sum_totals(jnp.sum(jnp.exp(guided), 1), ("dp", "tensor"))
    result = guided - jnp.log(totals)[:, None]
    half = prompts // streams
    returned = swap(result[:half], "stream", lead)
    return jnp.where(stream == lead, result[lead * half :], returned)


def solution(mesh):
    return jax.shard_map(
        body,
        mesh=mesh,
        in_specs=(
            P("stream", "tensor", "dp"),
            P("stream", "dp", "tensor", None, None),
            P("stream", "dp", "tensor", None, None),
            P("stream", "dp"),
            P(),
            P(),
            P("dp", "tensor"),
            P("dp", None, "tensor"),
            P("tensor", "dp"),
            P("dp"),
            P(None, ("dp", "tensor")),
        ),
        out_specs=P("stream", ("dp", "tensor")),
        check_vma=False,
    )
```

```python
import jax
import jax.numpy as jnp
from jax import lax
from jax.experimental import pallas as pl
from jax.experimental.pallas import tpu as pltpu
from jax.sharding import PartitionSpec as P

MODEL_WIDTH = 8192
HEAD_SIZE = 128


rope_theta = 500000.0
penalty_step = 1.5
norm_eps = 1e-05


def swap(value, axis, distance):
    if distance == 0:
        return value
    pairs = [(source, source ^ distance) for source in range(lax.axis_size(axis))]
    return lax.ppermute(value, axis, pairs)


def gather_swapped(value, axis):
    return [swap(value, axis, distance) for distance in range(lax.axis_size(axis))]


def sum_totals(value, axes):
    count = lax.axis_size(axes)
    copies = jnp.broadcast_to(value[None], (count,) + value.shape)
    return jnp.sum(lax.all_to_all(copies, axes, 0, 0, tiled=True), 0)


def matmul_kernel(row_blocks, *refs):
    blocks, weights, out_ref = refs[:row_blocks], refs[row_blocks:-1], refs[-1]
    rows = jnp.concatenate([block[...] for block in blocks], axis=0)
    first = 0
    for weight in weights:
        last = first + weight.shape[1]
        product = jnp.dot(rows, weight[...], preferred_element_type=jnp.float32)
        out_ref[:, first:last] = product.astype(out_ref.dtype)
        first = last


def matmul(blocks, weights, dtype):
    rows = sum(block.shape[0] for block in blocks)
    cols = sum(weight.shape[1] for weight in weights)
    depth = weights[0].shape[0]
    whole = pl.BlockSpec(memory_space=pltpu.VMEM)
    return pl.pallas_call(
        lambda *refs: matmul_kernel(len(blocks), *refs),
        out_shape=jax.ShapeDtypeStruct((rows, cols), dtype),
        in_specs=[whole] * (len(blocks) + len(weights)),
        out_specs=whole,
        compiler_params=pltpu.CompilerParams(vmem_limit_bytes=8 * 1024 * 1024),
        cost_estimate=pl.CostEstimate(
            flops=2 * rows * cols * depth,
            bytes_accessed=2 * (depth * (rows + cols) + rows * cols),
            transcendentals=0,
        ),
    )(*blocks, *[pltpu.with_memory_space_constraint(weight, pltpu.VMEM) for weight in weights])


def load_kernel(weight_ref, out_ref, sems):
    pieces = sems.shape[0]
    rows = weight_ref.shape[0] // pieces
    copies = []
    for piece in range(pieces):
        part = pl.ds(piece * rows, rows)
        copy = pltpu.make_async_copy(weight_ref.at[part], out_ref.at[part], sems.at[piece])
        copy.start()
        copies.append(copy)
    for copy in copies:
        copy.wait()


def load_to_vmem(weight):
    return pl.pallas_call(
        load_kernel,
        out_shape=pltpu.VMEM(weight.shape, weight.dtype),
        in_specs=[pl.BlockSpec(memory_space=pltpu.HBM)],
        out_specs=pl.BlockSpec(memory_space=pltpu.VMEM),
        scratch_shapes=[pltpu.SemaphoreType.DMA((4,))],
        compiler_params=pltpu.CompilerParams(vmem_limit_bytes=8 * 1024 * 1024),
        cost_estimate=pl.CostEstimate(
            flops=0, bytes_accessed=2 * weight.size * weight.dtype.itemsize, transcendentals=0
        ),
    )(pltpu.with_memory_space_constraint(weight, pltpu.HBM))


def rotate(values, positions):
    halfway = values.shape[-1] // 2
    frequency = rope_theta ** (-(jnp.arange(halfway, dtype=jnp.float32) * 2.0 / values.shape[-1]))
    angles = positions.astype(jnp.float32)[:, None, None] * frequency
    cosine_term = jnp.cos(angles)
    sine_term = jnp.sin(angles)
    first_half = values[..., :halfway]
    second_half = values[..., halfway:]
    return jnp.concatenate(
        [
            first_half * cosine_term - second_half * sine_term,
            second_half * cosine_term + first_half * sine_term,
        ],
        axis=-1,
    )


def repeat_counts(recent_ids, first_column, width):
    columns = first_column + jnp.arange(width, dtype=jnp.int32)
    return jnp.sum((recent_ids[:, :, None] == columns[None, None, :]).astype(jnp.float32), 1)


def body(
    hidden,
    cached_rotated_keys,
    cached_values,
    cache_lengths,
    recent_ids,
    guidance,
    w_query,
    key_value_weight,
    w_output,
    norm_gain,
    w_head,
):
    streams, dps, tensors = (lax.axis_size(axis) for axis in ("stream", "dp", "tensor"))
    stream, dp, tensor = (lax.axis_index(axis) for axis in ("stream", "dp", "tensor"))
    local_width = hidden.shape[2]
    query_cols = w_query.shape[1]
    kv_cols = key_value_weight.shape[2]
    local_prompts = cache_lengths.shape[1]
    hidden_prompts = hidden.shape[1]
    prompts = recent_ids.shape[0]
    lengths = cache_lengths[0]
    vocab_local = w_head.shape[1]

    hidden_blocks = gather_swapped(hidden[0], "tensor")
    all_rows = jnp.concatenate(hidden_blocks, axis=0)
    w_query = load_to_vmem(w_query)
    kv_flat = key_value_weight.reshape(local_width, 2 * kv_cols)
    projected_parts = matmul(hidden_blocks, [w_query, kv_flat], jnp.bfloat16)

    def hidden_place(prompt):
        block = prompt // hidden_prompts
        return (tensor ^ block) * hidden_prompts + prompt % hidden_prompts

    gain_rows = norm_gain.reshape(local_prompts, -1)
    total_cols = query_cols + 2 * kv_cols
    projected, gain_blocks = 0.0, []
    for distance in range(dps):
        sending = lax.dynamic_slice_in_dim(
            projected_parts, hidden_place((dp ^ distance) * local_prompts), local_prompts, 0
        )
        arrived = swap(jnp.concatenate([sending, gain_rows], axis=1), "dp", distance)
        projected = projected + arrived[:, :total_cols].astype(jnp.float32)
        gain_blocks.append(arrived[:, total_cols:].reshape(local_width))
    gain = jnp.zeros((local_width * dps,), norm_gain.dtype)
    for distance, block in enumerate(gain_blocks):
        gain = lax.dynamic_update_slice_in_dim(gain, block, (dp ^ distance) * local_width, 0)

    query_heads = query_cols // HEAD_SIZE
    kv_heads = kv_cols // HEAD_SIZE
    rotated_query = rotate(
        projected[:, :query_cols].reshape(local_prompts, query_heads, HEAD_SIZE), lengths
    ).astype(jnp.bfloat16)
    key_value_rows = projected[:, query_cols:].reshape(local_prompts, 2, kv_heads, HEAD_SIZE)
    fresh_key = rotate(key_value_rows[:, 0], lengths).astype(jnp.bfloat16)
    value_new = key_value_rows[:, 1].astype(jnp.bfloat16)
    grouped_queries = rotated_query.reshape(
        local_prompts, kv_heads, query_heads // kv_heads, HEAD_SIZE
    )
    attention_scale = HEAD_SIZE ** (-0.5)
    key_block = cached_rotated_keys[0]
    value_block = cached_values[0]
    scores = (
        jnp.einsum(
            "pkgd,pksd->pkgs", grouped_queries, key_block, preferred_element_type=jnp.float32
        )
        * attention_scale
    )
    self_score = (
        jnp.einsum("pkgd,pkd->pkg", grouped_queries, fresh_key, preferred_element_type=jnp.float32)
        * attention_scale
    )
    valid = jnp.arange(key_block.shape[2], dtype=jnp.int32)[None, :] < lengths[:, None]
    exps = jnp.where(valid[:, None, None, :], jnp.exp(scores), 0.0)
    own_exp = jnp.exp(self_score)
    denominator = jnp.sum(exps, -1) + own_exp
    weights = (exps / denominator[..., None]).astype(jnp.bfloat16)
    own_weight = (own_exp / denominator).astype(jnp.bfloat16)
    attended = jnp.einsum(
        "pkgs,pksd->pkgd", weights, value_block, preferred_element_type=jnp.float32
    )
    attended = (
        attended
        + own_weight.astype(jnp.float32)[..., None] * value_new.astype(jnp.float32)[:, :, None, :]
    )
    attended = attended.reshape(local_prompts, query_cols).astype(jnp.bfloat16)

    partial_out = matmul(gather_swapped(attended, "dp"), [w_output], jnp.bfloat16)

    half = prompts // streams
    share = half // tensors

    def partial_rows(tensor_to):
        parts = []
        for other in range(streams):
            prompt = (stream ^ other) * half + tensor_to * share
            place = (dp ^ (prompt // local_prompts)) * local_prompts + prompt % local_prompts
            parts.append(lax.dynamic_slice_in_dim(partial_out, place, share, 0))
        return jnp.concatenate(parts, axis=0)

    def hidden_rows(stream_to):
        place = hidden_place(stream_to * half + tensor * share)
        return lax.dynamic_slice_in_dim(all_rows, place, share, 0).astype(jnp.float32)

    summed = jnp.concatenate([hidden_rows(stream ^ other) for other in range(streams)], axis=0)
    for distance in range(tensors):
        arrived = swap(partial_rows(tensor ^ distance), "tensor", distance)
        summed = summed + arrived.astype(jnp.float32)
    residuals = summed.astype(jnp.bfloat16).reshape(streams, share, local_width)
    pair = [swap(residuals[other], "stream", other) for other in range(streams)]
    pair = jnp.concatenate(pair, axis=0)

    whole = jnp.zeros((streams * share, local_width * dps), jnp.bfloat16)
    for distance, block in enumerate(gather_swapped(pair, "dp")):
        whole = lax.dynamic_update_slice_in_dim(whole, block, (dp ^ distance) * local_width, 1)
    whole = whole.reshape(streams, share, -1).astype(jnp.float32)
    inverse = lax.rsqrt(jnp.sum(whole * whole, 2) / MODEL_WIDTH + norm_eps)
    guide = lax.dynamic_slice_in_dim(guidance, stream * half + tensor * share, share, 0)
    own_guide = jnp.where(stream == 0, guide, 1.0 - guide)
    factors = inverse * jnp.stack([own_guide, 1.0 - own_guide])
    mixed = jnp.sum(whole * factors[:, :, None], 0) * gain.astype(jnp.float32)
    mixed = mixed.astype(jnp.bfloat16)

    rows = jnp.zeros((half, local_width * dps), jnp.bfloat16)
    for distance, block in enumerate(gather_swapped(mixed, "tensor")):
        rows = lax.dynamic_update_slice_in_dim(rows, block, (tensor ^ distance) * share, 0)
    guided = matmul([rows], [w_head], jnp.float32)

    column_base = lax.axis_index(("dp", "tensor")) * vocab_local
    recent_mine = lax.dynamic_slice_in_dim(recent_ids, stream * half, half, 0)
    guided = guided - penalty_step * repeat_counts(recent_mine, column_base, vocab_local)
    totals = sum_totals(jnp.sum(jnp.exp(guided), 1), ("dp", "tensor"))
    return guided - jnp.log(totals)[:, None]


def solution(mesh):
    return jax.shard_map(
        body,
        mesh=mesh,
        in_specs=(
            P("stream", "tensor", "dp"),
            P("stream", "dp", "tensor", None, None),
            P("stream", "dp", "tensor", None, None),
            P("stream", "dp"),
            P(),
            P(),
            P("dp", "tensor"),
            P("dp", None, "tensor"),
            P("tensor", "dp"),
            P("dp"),
            P(None, ("dp", "tensor")),
        ),
        out_specs=P("stream", ("dp", "tensor")),
        check_vma=False,
    )
```

```python
import jax
import jax.numpy as jnp
from jax import lax
from jax.experimental import pallas as pl
from jax.experimental.pallas import tpu as pltpu
from jax.sharding import PartitionSpec as P

MODEL_WIDTH = 8192
HEAD_SIZE = 128


rope_theta = 500000.0
penalty_step = 1.5
norm_eps = 1e-05


def swap(value, axis, distance):
    if distance == 0:
        return value
    pairs = [(source, source ^ distance) for source in range(lax.axis_size(axis))]
    return lax.ppermute(value, axis, pairs)


def gather_swapped(value, axis):
    return [swap(value, axis, distance) for distance in range(lax.axis_size(axis))]


def sum_totals(value, axes):
    count = lax.axis_size(axes)
    copies = jnp.broadcast_to(value[None], (count,) + value.shape)
    return jnp.sum(lax.all_to_all(copies, axes, 0, 0, tiled=True), 0)


def matmul_kernel(row_blocks, *refs):
    blocks, weights, out_ref = refs[:row_blocks], refs[row_blocks:-1], refs[-1]
    rows = jnp.concatenate([block[...] for block in blocks], axis=0)
    first = 0
    for weight in weights:
        last = first + weight.shape[1]
        product = jnp.dot(rows, weight[...], preferred_element_type=jnp.float32)
        out_ref[:, first:last] = product.astype(out_ref.dtype)
        first = last


def matmul(blocks, weights, dtype):
    rows = sum(block.shape[0] for block in blocks)
    cols = sum(weight.shape[1] for weight in weights)
    depth = weights[0].shape[0]
    whole = pl.BlockSpec(memory_space=pltpu.VMEM)
    return pl.pallas_call(
        lambda *refs: matmul_kernel(len(blocks), *refs),
        out_shape=jax.ShapeDtypeStruct((rows, cols), dtype),
        in_specs=[whole] * (len(blocks) + len(weights)),
        out_specs=whole,
        compiler_params=pltpu.CompilerParams(vmem_limit_bytes=8 * 1024 * 1024),
        cost_estimate=pl.CostEstimate(
            flops=2 * rows * cols * depth,
            bytes_accessed=2 * (depth * (rows + cols) + rows * cols),
            transcendentals=0,
        ),
    )(*blocks, *[pltpu.with_memory_space_constraint(weight, pltpu.VMEM) for weight in weights])


def head_kernel(places_ref, *refs):
    blocks, (weight_ref, penalty_ref, out_ref) = refs[:-3], refs[-3:]
    rows = jnp.concatenate([block[...] for block in blocks], axis=0)
    logits = jnp.dot(rows, weight_ref[...], preferred_element_type=jnp.float32)
    share = blocks[0].shape[0]
    for i in range(len(blocks)):
        place = pl.ds(pl.multiple_of(places_ref[i], 8), share)
        out_ref[place, :] = logits[i * share : (i + 1) * share] - penalty_ref[place, :]


def head(places, blocks, weight, penalty):
    whole = pl.BlockSpec(memory_space=pltpu.VMEM)
    rows, cols = penalty.shape
    depth = weight.shape[0]
    return pl.pallas_call(
        head_kernel,
        out_shape=jax.ShapeDtypeStruct((rows, cols), jnp.float32),
        in_specs=[pl.BlockSpec(memory_space=pltpu.SMEM)] + [whole] * (len(blocks) + 2),
        out_specs=whole,
        compiler_params=pltpu.CompilerParams(vmem_limit_bytes=8 * 1024 * 1024),
        cost_estimate=pl.CostEstimate(
            flops=2 * rows * cols * depth,
            bytes_accessed=2 * depth * (rows + cols) + 8 * rows * cols,
            transcendentals=0,
        ),
    )(places, *blocks, pltpu.with_memory_space_constraint(weight, pltpu.VMEM), penalty)


def load_kernel(weight_ref, out_ref, sems):
    pieces = sems.shape[0]
    rows = weight_ref.shape[0] // pieces
    copies = []
    for piece in range(pieces):
        part = pl.ds(piece * rows, rows)
        copy = pltpu.make_async_copy(weight_ref.at[part], out_ref.at[part], sems.at[piece])
        copy.start()
        copies.append(copy)
    for copy in copies:
        copy.wait()


def load_to_vmem(weight):
    return pl.pallas_call(
        load_kernel,
        out_shape=pltpu.VMEM(weight.shape, weight.dtype),
        in_specs=[pl.BlockSpec(memory_space=pltpu.HBM)],
        out_specs=pl.BlockSpec(memory_space=pltpu.VMEM),
        scratch_shapes=[pltpu.SemaphoreType.DMA((4,))],
        compiler_params=pltpu.CompilerParams(vmem_limit_bytes=8 * 1024 * 1024),
        cost_estimate=pl.CostEstimate(
            flops=0, bytes_accessed=2 * weight.size * weight.dtype.itemsize, transcendentals=0
        ),
    )(pltpu.with_memory_space_constraint(weight, pltpu.HBM))


def rotation(positions):
    halfway = HEAD_SIZE // 2
    frequency = rope_theta ** (-(jnp.arange(halfway, dtype=jnp.float32) * 2.0 / HEAD_SIZE))
    angles = positions.astype(jnp.float32)[:, None, None] * frequency
    return jnp.cos(angles), jnp.sin(angles)


def rotate(values, cosine_term, sine_term):
    halfway = values.shape[-1] // 2
    first_half = values[..., :halfway]
    second_half = values[..., halfway:]
    return jnp.concatenate(
        [
            first_half * cosine_term - second_half * sine_term,
            second_half * cosine_term + first_half * sine_term,
        ],
        axis=-1,
    )


def repeat_counts(recent_ids, first_column, width):
    columns = first_column + jnp.arange(width, dtype=jnp.int32)
    return jnp.sum((recent_ids[:, :, None] == columns[None, None, :]).astype(jnp.float32), 1)


def body(
    hidden,
    cached_rotated_keys,
    cached_values,
    cache_lengths,
    recent_ids,
    guidance,
    w_query,
    key_value_weight,
    w_output,
    norm_gain,
    w_head,
):
    streams, dps, tensors = (lax.axis_size(axis) for axis in ("stream", "dp", "tensor"))
    stream, dp, tensor = (lax.axis_index(axis) for axis in ("stream", "dp", "tensor"))
    local_width = hidden.shape[2]
    query_cols = w_query.shape[1]
    kv_cols = key_value_weight.shape[2]
    local_prompts = cache_lengths.shape[1]
    hidden_prompts = hidden.shape[1]
    prompts = recent_ids.shape[0]
    lengths = cache_lengths[0]
    vocab_local = w_head.shape[1]

    hidden_blocks = gather_swapped(hidden[0], "tensor")
    all_rows = jnp.concatenate(hidden_blocks, axis=0)
    kv_flat = key_value_weight.reshape(local_width, 2 * kv_cols)
    cosine_term, sine_term = rotation(lengths)
    kv_flat, w_query, cosine_term, sine_term = lax.optimization_barrier(
        (kv_flat, w_query, cosine_term, sine_term)
    )
    w_query = load_to_vmem(w_query)
    projected_parts = matmul(hidden_blocks, [w_query, kv_flat], jnp.bfloat16)
    column_base = lax.axis_index(("dp", "tensor")) * vocab_local
    projected_parts, lengths, recent_ids, guidance, column_base = lax.optimization_barrier(
        (projected_parts, lengths, recent_ids, guidance, column_base)
    )

    def hidden_place(prompt):
        block = prompt // hidden_prompts
        return (tensor ^ block) * hidden_prompts + prompt % hidden_prompts

    gain_rows = norm_gain.reshape(local_prompts, -1)
    total_cols = query_cols + 2 * kv_cols
    projected, gain_blocks = 0.0, []
    for distance in range(dps):
        sending = lax.dynamic_slice_in_dim(
            projected_parts, hidden_place((dp ^ distance) * local_prompts), local_prompts, 0
        )
        arrived = swap(jnp.concatenate([sending, gain_rows], axis=1), "dp", distance)
        projected = projected + arrived[:, :total_cols].astype(jnp.float32)
        gain_blocks.append(arrived[:, total_cols:].reshape(local_width))
    gain = jnp.zeros((local_width * dps,), norm_gain.dtype)
    for distance, block in enumerate(gain_blocks):
        gain = lax.dynamic_update_slice_in_dim(gain, block, (dp ^ distance) * local_width, 0)

    query_heads = query_cols // HEAD_SIZE
    kv_heads = kv_cols // HEAD_SIZE
    rotated_query = rotate(
        projected[:, :query_cols].reshape(local_prompts, query_heads, HEAD_SIZE),
        cosine_term,
        sine_term,
    ).astype(jnp.bfloat16)
    key_value_rows = projected[:, query_cols:].reshape(local_prompts, 2, kv_heads, HEAD_SIZE)
    fresh_key = rotate(key_value_rows[:, 0], cosine_term, sine_term).astype(jnp.bfloat16)
    value_new = key_value_rows[:, 1].astype(jnp.bfloat16)
    grouped_queries = rotated_query.reshape(
        local_prompts, kv_heads, query_heads // kv_heads, HEAD_SIZE
    )
    attention_scale = HEAD_SIZE ** (-0.5)
    key_block = cached_rotated_keys[0]
    value_block = cached_values[0]
    scores = (
        jnp.einsum(
            "pkgd,pksd->pkgs", grouped_queries, key_block, preferred_element_type=jnp.float32
        )
        * attention_scale
    )
    self_score = (
        jnp.einsum("pkgd,pkd->pkg", grouped_queries, fresh_key, preferred_element_type=jnp.float32)
        * attention_scale
    )
    valid = jnp.arange(key_block.shape[2], dtype=jnp.int32)[None, :] < lengths[:, None]
    exps = jnp.where(valid[:, None, None, :], jnp.exp(scores), 0.0)
    own_exp = jnp.exp(self_score)
    denominator = jnp.sum(exps, -1) + own_exp
    weights = (exps / denominator[..., None]).astype(jnp.bfloat16)
    own_weight = (own_exp / denominator).astype(jnp.bfloat16)
    attended = jnp.einsum(
        "pkgs,pksd->pkgd", weights, value_block, preferred_element_type=jnp.float32
    )
    attended = (
        attended
        + own_weight.astype(jnp.float32)[..., None] * value_new.astype(jnp.float32)[:, :, None, :]
    )
    attended = attended.reshape(local_prompts, query_cols).astype(jnp.bfloat16)

    half = prompts // streams
    recent_mine = lax.dynamic_slice_in_dim(recent_ids, stream * half, half, 0)
    penalty = penalty_step * repeat_counts(recent_mine, column_base, vocab_local)
    attended, penalty = lax.optimization_barrier((attended, penalty))

    attended_blocks = gather_swapped(attended, "dp")
    w_output, _ = lax.optimization_barrier((w_output, attended))
    partial_out = matmul(attended_blocks, [load_to_vmem(w_output)], jnp.bfloat16)

    share = half // tensors

    def partial_rows(tensor_to):
        parts = []
        for other in range(streams):
            prompt = (stream ^ other) * half + tensor_to * share
            place = (dp ^ (prompt // local_prompts)) * local_prompts + prompt % local_prompts
            parts.append(lax.dynamic_slice_in_dim(partial_out, place, share, 0))
        return jnp.concatenate(parts, axis=0)

    def hidden_rows(stream_to):
        place = hidden_place(stream_to * half + tensor * share)
        return lax.dynamic_slice_in_dim(all_rows, place, share, 0).astype(jnp.float32)

    summed = jnp.concatenate([hidden_rows(stream ^ other) for other in range(streams)], axis=0)
    for distance in range(tensors):
        arrived = swap(partial_rows(tensor ^ distance), "tensor", distance)
        summed = summed + arrived.astype(jnp.float32)
    residuals = summed.astype(jnp.bfloat16).reshape(streams, share, local_width)
    pair = [swap(residuals[other], "stream", other) for other in range(streams)]
    pair = jnp.concatenate(pair, axis=0)

    whole = jnp.zeros((streams * share, local_width * dps), jnp.bfloat16)
    for distance, block in enumerate(gather_swapped(pair, "dp")):
        whole = lax.dynamic_update_slice_in_dim(whole, block, (dp ^ distance) * local_width, 1)
    whole = whole.reshape(streams, share, -1).astype(jnp.float32)
    inverse = lax.rsqrt(jnp.sum(whole * whole, 2) / MODEL_WIDTH + norm_eps)
    guide = lax.dynamic_slice_in_dim(guidance, stream * half + tensor * share, share, 0)
    own_guide = jnp.where(stream == 0, guide, 1.0 - guide)
    factors = inverse * jnp.stack([own_guide, 1.0 - own_guide])
    mixed = jnp.sum(whole * factors[:, :, None], 0) * gain.astype(jnp.float32)
    mixed = mixed.astype(jnp.bfloat16)

    mixed_blocks = gather_swapped(mixed, "tensor")
    w_head, _ = lax.optimization_barrier((w_head, mixed))
    places = jnp.stack([(tensor ^ distance) * share for distance in range(tensors)])
    guided = head(places.astype(jnp.int32), mixed_blocks, load_to_vmem(w_head), penalty)
    totals = sum_totals(jnp.sum(jnp.exp(guided), 1), ("dp", "tensor"))
    return guided - jnp.log(totals)[:, None]


def solution(mesh):
    return jax.shard_map(
        body,
        mesh=mesh,
        in_specs=(
            P("stream", "tensor", "dp"),
            P("stream", "dp", "tensor", None, None),
            P("stream", "dp", "tensor", None, None),
            P("stream", "dp"),
            P(),
            P(),
            P("dp", "tensor"),
            P("dp", None, "tensor"),
            P("tensor", "dp"),
            P("dp"),
            P(None, ("dp", "tensor")),
        ),
        out_specs=P("stream", ("dp", "tensor")),
        check_vma=False,
    )
```

```python
import math

import jax
import jax.numpy as jnp
from jax import lax
from jax.experimental import pallas as pl
from jax.experimental.pallas import tpu as pltpu
from jax.sharding import PartitionSpec as P

MODEL_WIDTH = 8192
HEAD_SIZE = 128


rope_theta = 500000.0
penalty_step = 1.5
norm_eps = 1e-05


def swap(value, axis, distance):
    if distance == 0:
        return value
    pairs = [(source, source ^ distance) for source in range(lax.axis_size(axis))]
    return lax.ppermute(value, axis, pairs)


def gather_swapped(value, axis):
    return [swap(value, axis, distance) for distance in range(lax.axis_size(axis))]


def sum_totals(value, axes):
    count = lax.axis_size(axes)
    copies = jnp.broadcast_to(value[None], (count,) + value.shape)
    return jnp.sum(lax.all_to_all(copies, axes, 0, 0, tiled=True), 0)


def matmul_kernel(row_blocks, *refs):
    blocks, weights, out_ref = refs[:row_blocks], refs[row_blocks:-1], refs[-1]
    rows = jnp.concatenate([block[...] for block in blocks], axis=0)
    first = 0
    for weight in weights:
        last = first + weight.shape[1]
        product = jnp.dot(rows, weight[...], preferred_element_type=jnp.float32)
        out_ref[:, first:last] = product.astype(out_ref.dtype)
        first = last


def matmul(blocks, weights, dtype):
    rows = sum(block.shape[0] for block in blocks)
    cols = sum(weight.shape[1] for weight in weights)
    depth = weights[0].shape[0]
    whole = pl.BlockSpec(memory_space=pltpu.VMEM)
    return pl.pallas_call(
        lambda *refs: matmul_kernel(len(blocks), *refs),
        out_shape=jax.ShapeDtypeStruct((rows, cols), dtype),
        in_specs=[whole] * (len(blocks) + len(weights)),
        out_specs=whole,
        compiler_params=pltpu.CompilerParams(vmem_limit_bytes=8 * 1024 * 1024),
        cost_estimate=pl.CostEstimate(
            flops=2 * rows * cols * depth,
            bytes_accessed=2 * (depth * (rows + cols) + rows * cols),
            transcendentals=0,
        ),
    )(*blocks, *[pltpu.with_memory_space_constraint(weight, pltpu.VMEM) for weight in weights])


def head_kernel(places_ref, *refs):
    blocks, (weight_ref, penalty_ref, out_ref) = refs[:-3], refs[-3:]
    rows = jnp.concatenate([block[...] for block in blocks], axis=0)
    logits = jnp.dot(rows, weight_ref[...], preferred_element_type=jnp.float32)
    share = blocks[0].shape[0]
    for i in range(len(blocks)):
        place = pl.ds(pl.multiple_of(places_ref[i], 8), share)
        out_ref[place, :] = logits[i * share : (i + 1) * share] - penalty_ref[place, :]


def head(places, blocks, weight, penalty):
    whole = pl.BlockSpec(memory_space=pltpu.VMEM)
    rows, cols = penalty.shape
    depth = weight.shape[0]
    return pl.pallas_call(
        head_kernel,
        out_shape=jax.ShapeDtypeStruct((rows, cols), jnp.float32),
        in_specs=[pl.BlockSpec(memory_space=pltpu.SMEM)] + [whole] * (len(blocks) + 2),
        out_specs=whole,
        compiler_params=pltpu.CompilerParams(vmem_limit_bytes=8 * 1024 * 1024),
        cost_estimate=pl.CostEstimate(
            flops=2 * rows * cols * depth,
            bytes_accessed=2 * depth * (rows + cols) + 8 * rows * cols,
            transcendentals=0,
        ),
    )(places, *blocks, pltpu.with_memory_space_constraint(weight, pltpu.VMEM), penalty)


def load_kernel(weight_ref, out_ref, sems):
    pieces = sems.shape[0]
    rows = weight_ref.shape[0] // pieces
    copies = []
    for piece in range(pieces):
        part = pl.ds(piece * rows, rows)
        copy = pltpu.make_async_copy(weight_ref.at[part], out_ref.at[part], sems.at[piece])
        copy.start()
        copies.append(copy)
    for copy in copies:
        copy.wait()


def load_to_vmem(weight):
    return pl.pallas_call(
        load_kernel,
        out_shape=pltpu.VMEM(weight.shape, weight.dtype),
        in_specs=[pl.BlockSpec(memory_space=pltpu.HBM)],
        out_specs=pl.BlockSpec(memory_space=pltpu.VMEM),
        scratch_shapes=[pltpu.SemaphoreType.DMA((4,))],
        compiler_params=pltpu.CompilerParams(vmem_limit_bytes=8 * 1024 * 1024),
        cost_estimate=pl.CostEstimate(
            flops=0, bytes_accessed=2 * weight.size * weight.dtype.itemsize, transcendentals=0
        ),
    )(pltpu.with_memory_space_constraint(weight, pltpu.HBM))


def load_projections_kernel(query_ref, pair_ref, query_out, pair_out, pair_raw, sems):
    first = pltpu.make_async_copy(pair_ref, pair_raw, sems.at[0])
    first.start()
    second = pltpu.make_async_copy(query_ref, query_out, sems.at[1])
    second.start()
    first.wait()
    depth, pair, cols = pair_raw.shape
    step = math.gcd(depth, 256)

    def relayout(index, carry):
        rows = pl.ds(pl.multiple_of(index * step, step), step)
        for member in range(pair):
            pair_out[rows, member * cols : (member + 1) * cols] = pair_raw[rows, member, :]
        return carry

    lax.fori_loop(0, depth // step, relayout, 0)
    second.wait()


def load_projections(query, pair):
    depth, members, cols = pair.shape
    arrays = [pltpu.with_memory_space_constraint(array, pltpu.HBM) for array in (query, pair)]
    return pl.pallas_call(
        load_projections_kernel,
        out_shape=(
            pltpu.VMEM(query.shape, query.dtype),
            pltpu.VMEM((depth, members * cols), pair.dtype),
        ),
        in_specs=[pl.BlockSpec(memory_space=pltpu.HBM)] * 2,
        out_specs=[pl.BlockSpec(memory_space=pltpu.VMEM)] * 2,
        scratch_shapes=[pltpu.VMEM(pair.shape, pair.dtype), pltpu.SemaphoreType.DMA((2,))],
        compiler_params=pltpu.CompilerParams(vmem_limit_bytes=16 * 1024 * 1024),
        cost_estimate=pl.CostEstimate(
            flops=0, bytes_accessed=4 * (query.size + pair.size), transcendentals=0
        ),
    )(*arrays)


def rotation(positions):
    halfway = HEAD_SIZE // 2
    frequency = rope_theta ** (-(jnp.arange(halfway, dtype=jnp.float32) * 2.0 / HEAD_SIZE))
    angles = positions.astype(jnp.float32)[:, None, None] * frequency
    return jnp.cos(angles), jnp.sin(angles)


def rotate(values, cosine_term, sine_term):
    halfway = values.shape[-1] // 2
    first_half = values[..., :halfway]
    second_half = values[..., halfway:]
    return jnp.concatenate(
        [
            first_half * cosine_term - second_half * sine_term,
            second_half * cosine_term + first_half * sine_term,
        ],
        axis=-1,
    )


def repeat_counts(recent_ids, first_column, width):
    columns = first_column + jnp.arange(width, dtype=jnp.int32)
    return jnp.sum((recent_ids[:, :, None] == columns[None, None, :]).astype(jnp.float32), 1)


def body(
    hidden,
    cached_rotated_keys,
    cached_values,
    cache_lengths,
    recent_ids,
    guidance,
    w_query,
    key_value_weight,
    w_output,
    norm_gain,
    w_head,
):
    streams, dps, tensors = (lax.axis_size(axis) for axis in ("stream", "dp", "tensor"))
    stream, dp, tensor = (lax.axis_index(axis) for axis in ("stream", "dp", "tensor"))
    local_width = hidden.shape[2]
    query_cols = w_query.shape[1]
    kv_cols = key_value_weight.shape[2]
    local_prompts = cache_lengths.shape[1]
    hidden_prompts = hidden.shape[1]
    prompts = recent_ids.shape[0]
    lengths = cache_lengths[0]
    vocab_local = w_head.shape[1]

    hidden_blocks = gather_swapped(hidden[0], "tensor")
    all_rows = jnp.concatenate(hidden_blocks, axis=0)
    projected_parts = matmul(
        hidden_blocks, load_projections(w_query, key_value_weight), jnp.bfloat16
    )
    column_base = lax.axis_index(("dp", "tensor")) * vocab_local
    projected_parts, lengths, recent_ids, guidance, column_base, norm_gain = (
        lax.optimization_barrier(
            (projected_parts, lengths, recent_ids, guidance, column_base, norm_gain)
        )
    )
    cosine_term, sine_term = rotation(lengths)

    def hidden_place(prompt):
        block = prompt // hidden_prompts
        return (tensor ^ block) * hidden_prompts + prompt % hidden_prompts

    gain_rows = norm_gain.reshape(local_prompts, -1)
    total_cols = query_cols + 2 * kv_cols
    projected, gain_blocks = 0.0, []
    for distance in range(dps):
        sending = lax.dynamic_slice_in_dim(
            projected_parts, hidden_place((dp ^ distance) * local_prompts), local_prompts, 0
        )
        arrived = swap(jnp.concatenate([sending, gain_rows], axis=1), "dp", distance)
        projected = projected + arrived[:, :total_cols].astype(jnp.float32)
        gain_blocks.append(arrived[:, total_cols:].reshape(local_width))
    gain = jnp.zeros((local_width * dps,), norm_gain.dtype)
    for distance, block in enumerate(gain_blocks):
        gain = lax.dynamic_update_slice_in_dim(gain, block, (dp ^ distance) * local_width, 0)

    query_heads = query_cols // HEAD_SIZE
    kv_heads = kv_cols // HEAD_SIZE
    rotated_query = rotate(
        projected[:, :query_cols].reshape(local_prompts, query_heads, HEAD_SIZE),
        cosine_term,
        sine_term,
    ).astype(jnp.bfloat16)
    key_value_rows = projected[:, query_cols:].reshape(local_prompts, 2, kv_heads, HEAD_SIZE)
    fresh_key = rotate(key_value_rows[:, 0], cosine_term, sine_term).astype(jnp.bfloat16)
    value_new = key_value_rows[:, 1].astype(jnp.bfloat16)
    grouped_queries = rotated_query.reshape(
        local_prompts, kv_heads, query_heads // kv_heads, HEAD_SIZE
    )
    attention_scale = HEAD_SIZE ** (-0.5)
    key_block = cached_rotated_keys[0]
    value_block = cached_values[0]
    scores = (
        jnp.einsum(
            "pkgd,pksd->pkgs", grouped_queries, key_block, preferred_element_type=jnp.float32
        )
        * attention_scale
    )
    self_score = (
        jnp.einsum("pkgd,pkd->pkg", grouped_queries, fresh_key, preferred_element_type=jnp.float32)
        * attention_scale
    )
    valid = jnp.arange(key_block.shape[2], dtype=jnp.int32)[None, :] < lengths[:, None]
    exps = jnp.where(valid[:, None, None, :], jnp.exp(scores), 0.0)
    own_exp = jnp.exp(self_score)
    denominator = jnp.sum(exps, -1) + own_exp
    weights = (exps / denominator[..., None]).astype(jnp.bfloat16)
    own_weight = (own_exp / denominator).astype(jnp.bfloat16)
    attended = jnp.einsum(
        "pkgs,pksd->pkgd", weights, value_block, preferred_element_type=jnp.float32
    )
    attended = (
        attended
        + own_weight.astype(jnp.float32)[..., None] * value_new.astype(jnp.float32)[:, :, None, :]
    )
    attended = attended.reshape(local_prompts, query_cols).astype(jnp.bfloat16)

    half = prompts // streams
    recent_mine = lax.dynamic_slice_in_dim(recent_ids, stream * half, half, 0)
    penalty = penalty_step * repeat_counts(recent_mine, column_base, vocab_local)
    attended, penalty = lax.optimization_barrier((attended, penalty))

    attended_blocks = gather_swapped(attended, "dp")
    w_output, _ = lax.optimization_barrier((w_output, attended))
    partial_out = matmul(attended_blocks, [load_to_vmem(w_output)], jnp.bfloat16)

    share = half // tensors

    def partial_rows(tensor_to):
        parts = []
        for other in range(streams):
            prompt = (stream ^ other) * half + tensor_to * share
            place = (dp ^ (prompt // local_prompts)) * local_prompts + prompt % local_prompts
            parts.append(lax.dynamic_slice_in_dim(partial_out, place, share, 0))
        return jnp.concatenate(parts, axis=0)

    def hidden_rows(stream_to):
        place = hidden_place(stream_to * half + tensor * share)
        return lax.dynamic_slice_in_dim(all_rows, place, share, 0).astype(jnp.float32)

    summed = jnp.concatenate([hidden_rows(stream ^ other) for other in range(streams)], axis=0)
    for distance in range(tensors):
        arrived = swap(partial_rows(tensor ^ distance), "tensor", distance)
        summed = summed + arrived.astype(jnp.float32)
    residuals = summed.astype(jnp.bfloat16).reshape(streams, share, local_width)
    pair = [swap(residuals[other], "stream", other) for other in range(streams)]
    pair = jnp.concatenate(pair, axis=0)

    whole = jnp.zeros((streams * share, local_width * dps), jnp.bfloat16)
    for distance, block in enumerate(gather_swapped(pair, "dp")):
        whole = lax.dynamic_update_slice_in_dim(whole, block, (dp ^ distance) * local_width, 1)
    whole = whole.reshape(streams, share, -1).astype(jnp.float32)
    inverse = lax.rsqrt(jnp.sum(whole * whole, 2) / MODEL_WIDTH + norm_eps)
    guide = lax.dynamic_slice_in_dim(guidance, stream * half + tensor * share, share, 0)
    own_guide = jnp.where(stream == 0, guide, 1.0 - guide)
    factors = inverse * jnp.stack([own_guide, 1.0 - own_guide])
    mixed = jnp.sum(whole * factors[:, :, None], 0) * gain.astype(jnp.float32)
    mixed = mixed.astype(jnp.bfloat16)

    mixed_blocks = gather_swapped(mixed, "tensor")
    w_head, _ = lax.optimization_barrier((w_head, mixed))
    places = jnp.stack([(tensor ^ distance) * share for distance in range(tensors)])
    guided = head(places.astype(jnp.int32), mixed_blocks, load_to_vmem(w_head), penalty)
    totals = sum_totals(jnp.sum(jnp.exp(guided), 1), ("dp", "tensor"))
    return guided - jnp.log(totals)[:, None]


def solution(mesh):
    return jax.shard_map(
        body,
        mesh=mesh,
        in_specs=(
            P("stream", "tensor", "dp"),
            P("stream", "dp", "tensor", None, None),
            P("stream", "dp", "tensor", None, None),
            P("stream", "dp"),
            P(),
            P(),
            P("dp", "tensor"),
            P("dp", None, "tensor"),
            P("tensor", "dp"),
            P("dp"),
            P(None, ("dp", "tensor")),
        ),
        out_specs=P("stream", ("dp", "tensor")),
        check_vma=False,
    )
```

```python
import math

import jax
import jax.numpy as jnp
import numpy as np
from jax import lax
from jax.experimental import pallas as pl
from jax.experimental.pallas import tpu as pltpu
from jax.sharding import PartitionSpec as P

MODEL_WIDTH = 8192
HEAD_SIZE = 128


rope_theta = 500000.0
penalty_step = 1.5
norm_eps = 1e-05


def swap(value, axis, distance):
    if distance == 0:
        return value
    pairs = [(source, source ^ distance) for source in range(lax.axis_size(axis))]
    return lax.ppermute(value, axis, pairs)


def gather_swapped(value, axis):
    return [swap(value, axis, distance) for distance in range(lax.axis_size(axis))]


def sum_totals(value, axes):
    count = lax.axis_size(axes)
    copies = jnp.broadcast_to(value[None], (count,) + value.shape)
    return jnp.sum(lax.all_to_all(copies, axes, 0, 0, tiled=True), 0)


def matmul_kernel(row_blocks, *refs):
    blocks, weights, out_ref = refs[:row_blocks], refs[row_blocks:-1], refs[-1]
    rows = jnp.concatenate([block[...] for block in blocks], axis=0)
    first = 0
    for weight in weights:
        last = first + weight.shape[1]
        product = jnp.dot(rows, weight[...], preferred_element_type=jnp.float32)
        out_ref[:, first:last] = product.astype(out_ref.dtype)
        first = last


def matmul(blocks, weights, dtype):
    rows = sum(block.shape[0] for block in blocks)
    cols = sum(weight.shape[1] for weight in weights)
    depth = weights[0].shape[0]
    whole = pl.BlockSpec(memory_space=pltpu.VMEM)
    return pl.pallas_call(
        lambda *refs: matmul_kernel(len(blocks), *refs),
        out_shape=jax.ShapeDtypeStruct((rows, cols), dtype),
        in_specs=[whole] * (len(blocks) + len(weights)),
        out_specs=whole,
        compiler_params=pltpu.CompilerParams(vmem_limit_bytes=8 * 1024 * 1024),
        cost_estimate=pl.CostEstimate(
            flops=2 * rows * cols * depth,
            bytes_accessed=2 * (depth * (rows + cols) + rows * cols),
            transcendentals=0,
        ),
    )(*blocks, *[pltpu.with_memory_space_constraint(weight, pltpu.VMEM) for weight in weights])


def head_kernel(places_ref, *refs):
    blocks, (weight_ref, penalty_ref, out_ref) = refs[:-3], refs[-3:]
    rows = jnp.concatenate([block[...] for block in blocks], axis=0)
    logits = jnp.dot(rows, weight_ref[...], preferred_element_type=jnp.float32)
    share = blocks[0].shape[0]
    for i in range(len(blocks)):
        place = pl.ds(pl.multiple_of(places_ref[i], 8), share)
        out_ref[place, :] = logits[i * share : (i + 1) * share] - penalty_ref[place, :]


def head(places, blocks, weight, penalty):
    whole = pl.BlockSpec(memory_space=pltpu.VMEM)
    rows, cols = penalty.shape
    depth = weight.shape[0]
    return pl.pallas_call(
        head_kernel,
        out_shape=jax.ShapeDtypeStruct((rows, cols), jnp.float32),
        in_specs=[pl.BlockSpec(memory_space=pltpu.SMEM)] + [whole] * (len(blocks) + 2),
        out_specs=whole,
        compiler_params=pltpu.CompilerParams(vmem_limit_bytes=8 * 1024 * 1024),
        cost_estimate=pl.CostEstimate(
            flops=2 * rows * cols * depth,
            bytes_accessed=2 * depth * (rows + cols) + 8 * rows * cols,
            transcendentals=0,
        ),
    )(places, *blocks, pltpu.with_memory_space_constraint(weight, pltpu.VMEM), penalty)


def load_kernel(weight_ref, out_ref, sems):
    pieces = sems.shape[0]
    rows = weight_ref.shape[0] // pieces
    copies = []
    for piece in range(pieces):
        part = pl.ds(piece * rows, rows)
        copy = pltpu.make_async_copy(weight_ref.at[part], out_ref.at[part], sems.at[piece])
        copy.start()
        copies.append(copy)
    for copy in copies:
        copy.wait()


def load_to_vmem(weight):
    return pl.pallas_call(
        load_kernel,
        out_shape=pltpu.VMEM(weight.shape, weight.dtype),
        in_specs=[pl.BlockSpec(memory_space=pltpu.HBM)],
        out_specs=pl.BlockSpec(memory_space=pltpu.VMEM),
        scratch_shapes=[pltpu.SemaphoreType.DMA((4,))],
        compiler_params=pltpu.CompilerParams(vmem_limit_bytes=8 * 1024 * 1024),
        cost_estimate=pl.CostEstimate(
            flops=0, bytes_accessed=2 * weight.size * weight.dtype.itemsize, transcendentals=0
        ),
    )(pltpu.with_memory_space_constraint(weight, pltpu.HBM))


def load_projections_kernel(query_ref, pair_ref, query_out, pair_out, pair_raw, sems):
    first = pltpu.make_async_copy(pair_ref, pair_raw, sems.at[0])
    first.start()
    second = pltpu.make_async_copy(query_ref, query_out, sems.at[1])
    second.start()
    first.wait()
    depth, pair, cols = pair_raw.shape
    step = math.gcd(depth, 256)

    def relayout(index, carry):
        rows = pl.ds(pl.multiple_of(index * step, step), step)
        for member in range(pair):
            pair_out[rows, member * cols : (member + 1) * cols] = pair_raw[rows, member, :]
        return carry

    lax.fori_loop(0, depth // step, relayout, 0)
    second.wait()


def load_projections(query, pair):
    depth, members, cols = pair.shape
    arrays = [pltpu.with_memory_space_constraint(array, pltpu.HBM) for array in (query, pair)]
    return pl.pallas_call(
        load_projections_kernel,
        out_shape=(
            pltpu.VMEM(query.shape, query.dtype),
            pltpu.VMEM((depth, members * cols), pair.dtype),
        ),
        in_specs=[pl.BlockSpec(memory_space=pltpu.HBM)] * 2,
        out_specs=[pl.BlockSpec(memory_space=pltpu.VMEM)] * 2,
        scratch_shapes=[pltpu.VMEM(pair.shape, pair.dtype), pltpu.SemaphoreType.DMA((2,))],
        compiler_params=pltpu.CompilerParams(vmem_limit_bytes=16 * 1024 * 1024),
        cost_estimate=pl.CostEstimate(
            flops=0, bytes_accessed=4 * (query.size + pair.size), transcendentals=0
        ),
    )(*arrays)


def rotation(positions):
    halfway = HEAD_SIZE // 2
    frequency = np.asarray(rope_theta ** (-np.arange(halfway) * 2.0 / HEAD_SIZE), np.float32)
    angles = positions.astype(jnp.float32)[:, None, None] * frequency
    return jnp.cos(angles), jnp.sin(angles)


def rotate(values, cosine_term, sine_term):
    halfway = values.shape[-1] // 2
    first_half = values[..., :halfway]
    second_half = values[..., halfway:]
    return jnp.concatenate(
        [
            first_half * cosine_term - second_half * sine_term,
            second_half * cosine_term + first_half * sine_term,
        ],
        axis=-1,
    )


def repeat_counts(recent_ids, first_column, width):
    columns = first_column + jnp.arange(width, dtype=jnp.int32)
    return jnp.sum((recent_ids[:, :, None] == columns[None, None, :]).astype(jnp.float32), 1)


def body(
    hidden,
    cached_rotated_keys,
    cached_values,
    cache_lengths,
    recent_ids,
    guidance,
    w_query,
    key_value_weight,
    w_output,
    norm_gain,
    w_head,
):
    streams, dps, tensors = (lax.axis_size(axis) for axis in ("stream", "dp", "tensor"))
    stream, dp, tensor = (lax.axis_index(axis) for axis in ("stream", "dp", "tensor"))
    local_width = hidden.shape[2]
    query_cols = w_query.shape[1]
    kv_cols = key_value_weight.shape[2]
    local_prompts = cache_lengths.shape[1]
    hidden_prompts = hidden.shape[1]
    prompts = recent_ids.shape[0]
    lengths = cache_lengths[0]
    vocab_local = w_head.shape[1]

    hidden_blocks = gather_swapped(hidden[0], "tensor")
    all_rows = jnp.concatenate(hidden_blocks, axis=0)
    projected_parts = matmul(
        hidden_blocks, load_projections(w_query, key_value_weight), jnp.bfloat16
    )
    column_base = lax.axis_index(("dp", "tensor")) * vocab_local
    projected_parts, lengths, recent_ids, guidance, column_base, norm_gain = (
        lax.optimization_barrier(
            (projected_parts, lengths, recent_ids, guidance, column_base, norm_gain)
        )
    )
    cosine_term, sine_term = rotation(lengths)

    def hidden_place(prompt):
        block = prompt // hidden_prompts
        return (tensor ^ block) * hidden_prompts + prompt % hidden_prompts

    gain_rows = norm_gain.reshape(local_prompts, -1)
    total_cols = query_cols + 2 * kv_cols
    projected, gain_blocks = 0.0, []
    for distance in range(dps):
        sending = lax.dynamic_slice_in_dim(
            projected_parts, hidden_place((dp ^ distance) * local_prompts), local_prompts, 0
        )
        arrived = swap(jnp.concatenate([sending, gain_rows], axis=1), "dp", distance)
        projected = projected + arrived[:, :total_cols].astype(jnp.float32)
        gain_blocks.append(arrived[:, total_cols:].reshape(local_width))
    gain = jnp.zeros((local_width * dps,), norm_gain.dtype)
    for distance, block in enumerate(gain_blocks):
        gain = lax.dynamic_update_slice_in_dim(gain, block, (dp ^ distance) * local_width, 0)

    query_heads = query_cols // HEAD_SIZE
    kv_heads = kv_cols // HEAD_SIZE
    rotated_query = rotate(
        projected[:, :query_cols].reshape(local_prompts, query_heads, HEAD_SIZE),
        cosine_term,
        sine_term,
    ).astype(jnp.bfloat16)
    key_value_rows = projected[:, query_cols:].reshape(local_prompts, 2, kv_heads, HEAD_SIZE)
    fresh_key = rotate(key_value_rows[:, 0], cosine_term, sine_term).astype(jnp.bfloat16)
    value_new = key_value_rows[:, 1].astype(jnp.bfloat16)
    grouped_queries = rotated_query.reshape(
        local_prompts, kv_heads, query_heads // kv_heads, HEAD_SIZE
    )
    attention_scale = HEAD_SIZE ** (-0.5)
    key_block = cached_rotated_keys[0]
    value_block = cached_values[0]
    scores = (
        jnp.einsum(
            "pkgd,pksd->pkgs", grouped_queries, key_block, preferred_element_type=jnp.float32
        )
        * attention_scale
    )
    self_score = (
        jnp.einsum("pkgd,pkd->pkg", grouped_queries, fresh_key, preferred_element_type=jnp.float32)
        * attention_scale
    )
    valid = jnp.arange(key_block.shape[2], dtype=jnp.int32)[None, :] < lengths[:, None]
    exps = jnp.where(valid[:, None, None, :], jnp.exp(scores), 0.0)
    own_exp = jnp.exp(self_score)
    denominator = jnp.sum(exps, -1) + own_exp
    weights = (exps / denominator[..., None]).astype(jnp.bfloat16)
    own_weight = (own_exp / denominator).astype(jnp.bfloat16)
    attended = jnp.einsum(
        "pkgs,pksd->pkgd", weights, value_block, preferred_element_type=jnp.float32
    )
    attended = (
        attended
        + own_weight.astype(jnp.float32)[..., None] * value_new.astype(jnp.float32)[:, :, None, :]
    )
    attended = attended.reshape(local_prompts, query_cols).astype(jnp.bfloat16)

    half = prompts // streams
    recent_mine = lax.dynamic_slice_in_dim(recent_ids, stream * half, half, 0)
    penalty = penalty_step * repeat_counts(recent_mine, column_base, vocab_local)
    attended, penalty = lax.optimization_barrier((attended, penalty))

    attended_blocks = gather_swapped(attended, "dp")
    w_output, _ = lax.optimization_barrier((w_output, attended))
    partial_out = matmul(attended_blocks, [load_to_vmem(w_output)], jnp.bfloat16)

    share = half // tensors

    def partial_rows(tensor_to):
        parts = []
        for other in range(streams):
            prompt = (stream ^ other) * half + tensor_to * share
            place = (dp ^ (prompt // local_prompts)) * local_prompts + prompt % local_prompts
            parts.append(lax.dynamic_slice_in_dim(partial_out, place, share, 0))
        return jnp.concatenate(parts, axis=0)

    def hidden_rows(stream_to):
        place = hidden_place(stream_to * half + tensor * share)
        return lax.dynamic_slice_in_dim(all_rows, place, share, 0).astype(jnp.float32)

    summed = jnp.concatenate([hidden_rows(stream ^ other) for other in range(streams)], axis=0)
    for distance in range(tensors):
        arrived = swap(partial_rows(tensor ^ distance), "tensor", distance)
        summed = summed + arrived.astype(jnp.float32)
    residuals = summed.astype(jnp.bfloat16).reshape(streams, share, local_width)
    pair = [swap(residuals[other], "stream", other) for other in range(streams)]
    pair = jnp.concatenate(pair, axis=0)

    whole = jnp.zeros((streams * share, local_width * dps), jnp.bfloat16)
    for distance, block in enumerate(gather_swapped(pair, "dp")):
        whole = lax.dynamic_update_slice_in_dim(whole, block, (dp ^ distance) * local_width, 1)
    whole = whole.reshape(streams, share, -1).astype(jnp.float32)
    inverse = lax.rsqrt(jnp.sum(whole * whole, 2) / MODEL_WIDTH + norm_eps)
    guide = lax.dynamic_slice_in_dim(guidance, stream * half + tensor * share, share, 0)
    own_guide = jnp.where(stream == 0, guide, 1.0 - guide)
    factors = inverse * jnp.stack([own_guide, 1.0 - own_guide])
    mixed = jnp.sum(whole * factors[:, :, None], 0) * gain.astype(jnp.float32)
    mixed = mixed.astype(jnp.bfloat16)

    mixed_blocks = gather_swapped(mixed, "tensor")
    w_head, _ = lax.optimization_barrier((w_head, mixed))
    places = jnp.stack([(tensor ^ distance) * share for distance in range(tensors)])
    guided = head(places.astype(jnp.int32), mixed_blocks, load_to_vmem(w_head), penalty)
    totals = sum_totals(jnp.sum(jnp.exp(guided), 1), ("dp", "tensor"))
    return guided - jnp.log(totals)[:, None]


def solution(mesh):
    return jax.shard_map(
        body,
        mesh=mesh,
        in_specs=(
            P("stream", "tensor", "dp"),
            P("stream", "dp", "tensor", None, None),
            P("stream", "dp", "tensor", None, None),
            P("stream", "dp"),
            P(),
            P(),
            P("dp", "tensor"),
            P("dp", None, "tensor"),
            P("tensor", "dp"),
            P("dp"),
            P(None, ("dp", "tensor")),
        ),
        out_specs=P("stream", ("dp", "tensor")),
        check_vma=False,
    )
```

```python
import math

import jax
import jax.numpy as jnp
import numpy as np
from jax import lax
from jax.experimental import pallas as pl
from jax.experimental.pallas import tpu as pltpu
from jax.sharding import PartitionSpec as P

MODEL_WIDTH = 8192
HEAD_SIZE = 128


rope_theta = 500000.0
penalty_step = 1.5
norm_eps = 1e-05


def swap(value, axis, distance):
    if distance == 0:
        return value
    pairs = [(source, source ^ distance) for source in range(lax.axis_size(axis))]
    return lax.ppermute(value, axis, pairs)


def gather_swapped(value, axis):
    return [swap(value, axis, distance) for distance in range(lax.axis_size(axis))]


def sum_totals(value, axes):
    count = lax.axis_size(axes)
    copies = jnp.broadcast_to(value[None], (count,) + value.shape)
    return jnp.sum(lax.all_to_all(copies, axes, 0, 0, tiled=True), 0)


def matmul_kernel(row_blocks, *refs):
    blocks, weights, out_ref = refs[:row_blocks], refs[row_blocks:-1], refs[-1]
    rows = jnp.concatenate([block[...] for block in blocks], axis=0)
    first = 0
    for weight in weights:
        last = first + weight.shape[1]
        product = jnp.dot(rows, weight[...], preferred_element_type=jnp.float32)
        out_ref[:, first:last] = product.astype(out_ref.dtype)
        first = last


def matmul(blocks, weights, dtype):
    rows = sum(block.shape[0] for block in blocks)
    cols = sum(weight.shape[1] for weight in weights)
    depth = weights[0].shape[0]
    whole = pl.BlockSpec(memory_space=pltpu.VMEM)
    return pl.pallas_call(
        lambda *refs: matmul_kernel(len(blocks), *refs),
        out_shape=jax.ShapeDtypeStruct((rows, cols), dtype),
        in_specs=[whole] * (len(blocks) + len(weights)),
        out_specs=whole,
        compiler_params=pltpu.CompilerParams(vmem_limit_bytes=8 * 1024 * 1024),
        cost_estimate=pl.CostEstimate(
            flops=2 * rows * cols * depth,
            bytes_accessed=2 * (depth * (rows + cols) + rows * cols),
            transcendentals=0,
        ),
    )(*blocks, *[pltpu.with_memory_space_constraint(weight, pltpu.VMEM) for weight in weights])


def head_kernel(places_ref, *refs):
    blocks, (weight_ref, penalty_ref, out_ref) = refs[:-3], refs[-3:]
    rows = jnp.concatenate([block[...] for block in blocks], axis=0)
    logits = jnp.dot(rows, weight_ref[...], preferred_element_type=jnp.float32)
    share = blocks[0].shape[0]
    for i in range(len(blocks)):
        place = pl.ds(pl.multiple_of(places_ref[i], 8), share)
        out_ref[place, :] = logits[i * share : (i + 1) * share] - penalty_ref[place, :]


def head(places, blocks, weight, penalty):
    whole = pl.BlockSpec(memory_space=pltpu.VMEM)
    rows, cols = penalty.shape
    depth = weight.shape[0]
    return pl.pallas_call(
        head_kernel,
        out_shape=jax.ShapeDtypeStruct((rows, cols), jnp.float32),
        in_specs=[pl.BlockSpec(memory_space=pltpu.SMEM)] + [whole] * (len(blocks) + 2),
        out_specs=whole,
        compiler_params=pltpu.CompilerParams(vmem_limit_bytes=8 * 1024 * 1024),
        cost_estimate=pl.CostEstimate(
            flops=2 * rows * cols * depth,
            bytes_accessed=2 * depth * (rows + cols) + 8 * rows * cols,
            transcendentals=0,
        ),
    )(places, *blocks, pltpu.with_memory_space_constraint(weight, pltpu.VMEM), penalty)


def load_kernel(weight_ref, out_ref, sems):
    pieces = sems.shape[0]
    rows = weight_ref.shape[0] // pieces
    copies = []
    for piece in range(pieces):
        part = pl.ds(piece * rows, rows)
        copy = pltpu.make_async_copy(weight_ref.at[part], out_ref.at[part], sems.at[piece])
        copy.start()
        copies.append(copy)
    for copy in copies:
        copy.wait()


def load_to_vmem(weight):
    return pl.pallas_call(
        load_kernel,
        out_shape=pltpu.VMEM(weight.shape, weight.dtype),
        in_specs=[pl.BlockSpec(memory_space=pltpu.HBM)],
        out_specs=pl.BlockSpec(memory_space=pltpu.VMEM),
        scratch_shapes=[pltpu.SemaphoreType.DMA((4,))],
        compiler_params=pltpu.CompilerParams(vmem_limit_bytes=8 * 1024 * 1024),
        cost_estimate=pl.CostEstimate(
            flops=0, bytes_accessed=2 * weight.size * weight.dtype.itemsize, transcendentals=0
        ),
    )(pltpu.with_memory_space_constraint(weight, pltpu.HBM))


def load_projections_kernel(query_ref, pair_ref, query_out, pair_out, pair_raw, sems):
    first = pltpu.make_async_copy(pair_ref, pair_raw, sems.at[0])
    first.start()
    early = pl.ds(0, query_out.shape[1])
    second = pltpu.make_async_copy(query_ref.at[:, early], query_out, sems.at[1])
    second.start()
    first.wait()
    depth, pair, cols = pair_raw.shape
    step = math.gcd(depth, 256)

    def relayout(index, carry):
        rows = pl.ds(pl.multiple_of(index * step, step), step)
        for member in range(pair):
            pair_out[rows, member * cols : (member + 1) * cols] = pair_raw[rows, member, :]
        return carry

    lax.fori_loop(0, depth // step, relayout, 0)
    second.wait()


def load_projections(query, pair):
    depth, members, cols = pair.shape
    arrays = [pltpu.with_memory_space_constraint(array, pltpu.HBM) for array in (query, pair)]
    return pl.pallas_call(
        load_projections_kernel,
        out_shape=(
            pltpu.VMEM((depth, query.shape[1] // 2), query.dtype),
            pltpu.VMEM((depth, members * cols), pair.dtype),
        ),
        in_specs=[pl.BlockSpec(memory_space=pltpu.HBM)] * 2,
        out_specs=[pl.BlockSpec(memory_space=pltpu.VMEM)] * 2,
        scratch_shapes=[pltpu.VMEM(pair.shape, pair.dtype), pltpu.SemaphoreType.DMA((2,))],
        compiler_params=pltpu.CompilerParams(vmem_limit_bytes=16 * 1024 * 1024),
        cost_estimate=pl.CostEstimate(
            flops=0, bytes_accessed=2 * query.size + 4 * pair.size, transcendentals=0
        ),
    )(*arrays)


def project_kernel(*refs):
    blocks, (early_ref, pair_ref, query_ref, out_ref, late, sems) = refs[:-6], refs[-6:]
    early_cols, query_cols = early_ref.shape[1], query_ref.shape[1]
    pieces, _, piece_cols = late.shape
    copies = []
    for piece in range(pieces):
        part = pl.ds(early_cols + piece * piece_cols, piece_cols)
        copy = pltpu.make_async_copy(query_ref.at[:, part], late.at[piece], sems.at[piece])
        copy.start()
        copies.append(copy)
    rows = jnp.concatenate([block[...] for block in blocks], axis=0)

    def store(first, weight):
        product = jnp.dot(rows, weight, preferred_element_type=jnp.float32)
        out_ref[:, first : first + weight.shape[1]] = product.astype(out_ref.dtype)

    store(0, early_ref[...])
    store(query_cols, pair_ref[...])
    for piece in range(pieces):
        copies[piece].wait()
        store(early_cols + piece * piece_cols, late[piece])


def project(blocks, query, pair):
    early, flat = load_projections(query, pair)
    rows = sum(block.shape[0] for block in blocks)
    depth, query_cols = query.shape
    cols = query_cols + flat.shape[1]
    piece_cols = query_cols // 4
    whole = pl.BlockSpec(memory_space=pltpu.VMEM)
    held = [pltpu.with_memory_space_constraint(array, pltpu.VMEM) for array in (early, flat)]
    return pl.pallas_call(
        project_kernel,
        out_shape=jax.ShapeDtypeStruct((rows, cols), blocks[0].dtype),
        in_specs=[whole] * (len(blocks) + 2) + [pl.BlockSpec(memory_space=pltpu.HBM)],
        out_specs=whole,
        scratch_shapes=[
            pltpu.VMEM((2, depth, piece_cols), query.dtype),
            pltpu.SemaphoreType.DMA((2,)),
        ],
        compiler_params=pltpu.CompilerParams(vmem_limit_bytes=16 * 1024 * 1024),
        cost_estimate=pl.CostEstimate(
            flops=2 * rows * cols * depth,
            bytes_accessed=2 * depth * (rows + cols),
            transcendentals=0,
        ),
    )(*blocks, *held, pltpu.with_memory_space_constraint(query, pltpu.HBM))


def rotation(positions):
    halfway = HEAD_SIZE // 2
    frequency = np.asarray(rope_theta ** (-np.arange(halfway) * 2.0 / HEAD_SIZE), np.float32)
    angles = positions.astype(jnp.float32)[:, None, None] * frequency
    return jnp.cos(angles), jnp.sin(angles)


def rotate(values, cosine_term, sine_term):
    halfway = values.shape[-1] // 2
    first_half = values[..., :halfway]
    second_half = values[..., halfway:]
    return jnp.concatenate(
        [
            first_half * cosine_term - second_half * sine_term,
            second_half * cosine_term + first_half * sine_term,
        ],
        axis=-1,
    )


def repeat_counts(recent_ids, first_column, width):
    columns = first_column + jnp.arange(width, dtype=jnp.int32)
    return jnp.sum((recent_ids[:, :, None] == columns[None, None, :]).astype(jnp.float32), 1)


def body(
    hidden,
    cached_rotated_keys,
    cached_values,
    cache_lengths,
    recent_ids,
    guidance,
    w_query,
    key_value_weight,
    w_output,
    norm_gain,
    w_head,
):
    streams, dps, tensors = (lax.axis_size(axis) for axis in ("stream", "dp", "tensor"))
    stream, dp, tensor = (lax.axis_index(axis) for axis in ("stream", "dp", "tensor"))
    local_width = hidden.shape[2]
    query_cols = w_query.shape[1]
    kv_cols = key_value_weight.shape[2]
    local_prompts = cache_lengths.shape[1]
    hidden_prompts = hidden.shape[1]
    prompts = recent_ids.shape[0]
    lengths = cache_lengths[0]
    vocab_local = w_head.shape[1]

    hidden_blocks = gather_swapped(hidden[0], "tensor")
    all_rows = jnp.concatenate(hidden_blocks, axis=0)
    projected_parts = project(hidden_blocks, w_query, key_value_weight)
    column_base = lax.axis_index(("dp", "tensor")) * vocab_local
    projected_parts, lengths, recent_ids, guidance, column_base, norm_gain = (
        lax.optimization_barrier(
            (projected_parts, lengths, recent_ids, guidance, column_base, norm_gain)
        )
    )
    cosine_term, sine_term = rotation(lengths)

    def hidden_place(prompt):
        block = prompt // hidden_prompts
        return (tensor ^ block) * hidden_prompts + prompt % hidden_prompts

    gain_rows = norm_gain.reshape(local_prompts, -1)
    total_cols = query_cols + 2 * kv_cols
    projected, gain_blocks = 0.0, []
    for distance in range(dps):
        sending = lax.dynamic_slice_in_dim(
            projected_parts, hidden_place((dp ^ distance) * local_prompts), local_prompts, 0
        )
        arrived = swap(jnp.concatenate([sending, gain_rows], axis=1), "dp", distance)
        projected = projected + arrived[:, :total_cols].astype(jnp.float32)
        gain_blocks.append(arrived[:, total_cols:].reshape(local_width))
    gain = jnp.zeros((local_width * dps,), norm_gain.dtype)
    for distance, block in enumerate(gain_blocks):
        gain = lax.dynamic_update_slice_in_dim(gain, block, (dp ^ distance) * local_width, 0)

    query_heads = query_cols // HEAD_SIZE
    kv_heads = kv_cols // HEAD_SIZE
    rotated_query = rotate(
        projected[:, :query_cols].reshape(local_prompts, query_heads, HEAD_SIZE),
        cosine_term,
        sine_term,
    ).astype(jnp.bfloat16)
    key_value_rows = projected[:, query_cols:].reshape(local_prompts, 2, kv_heads, HEAD_SIZE)
    fresh_key = rotate(key_value_rows[:, 0], cosine_term, sine_term).astype(jnp.bfloat16)
    value_new = key_value_rows[:, 1].astype(jnp.bfloat16)
    grouped_queries = rotated_query.reshape(
        local_prompts, kv_heads, query_heads // kv_heads, HEAD_SIZE
    )
    attention_scale = HEAD_SIZE ** (-0.5)
    key_block = cached_rotated_keys[0]
    value_block = cached_values[0]
    scores = (
        jnp.einsum(
            "pkgd,pksd->pkgs", grouped_queries, key_block, preferred_element_type=jnp.float32
        )
        * attention_scale
    )
    self_score = (
        jnp.einsum("pkgd,pkd->pkg", grouped_queries, fresh_key, preferred_element_type=jnp.float32)
        * attention_scale
    )
    valid = jnp.arange(key_block.shape[2], dtype=jnp.int32)[None, :] < lengths[:, None]
    exps = jnp.where(valid[:, None, None, :], jnp.exp(scores), 0.0)
    own_exp = jnp.exp(self_score)
    denominator = jnp.sum(exps, -1) + own_exp
    weights = (exps / denominator[..., None]).astype(jnp.bfloat16)
    own_weight = (own_exp / denominator).astype(jnp.bfloat16)
    attended = jnp.einsum(
        "pkgs,pksd->pkgd", weights, value_block, preferred_element_type=jnp.float32
    )
    attended = (
        attended
        + own_weight.astype(jnp.float32)[..., None] * value_new.astype(jnp.float32)[:, :, None, :]
    )
    attended = attended.reshape(local_prompts, query_cols).astype(jnp.bfloat16)

    half = prompts // streams
    recent_mine = lax.dynamic_slice_in_dim(recent_ids, stream * half, half, 0)
    penalty = penalty_step * repeat_counts(recent_mine, column_base, vocab_local)
    attended, penalty = lax.optimization_barrier((attended, penalty))

    attended_blocks = gather_swapped(attended, "dp")
    w_output, _ = lax.optimization_barrier((w_output, attended))
    partial_out = matmul(attended_blocks, [load_to_vmem(w_output)], jnp.bfloat16)

    share = half // tensors

    def partial_rows(tensor_to):
        parts = []
        for other in range(streams):
            prompt = (stream ^ other) * half + tensor_to * share
            place = (dp ^ (prompt // local_prompts)) * local_prompts + prompt % local_prompts
            parts.append(lax.dynamic_slice_in_dim(partial_out, place, share, 0))
        return jnp.concatenate(parts, axis=0)

    def hidden_rows(stream_to):
        place = hidden_place(stream_to * half + tensor * share)
        return lax.dynamic_slice_in_dim(all_rows, place, share, 0).astype(jnp.float32)

    summed = jnp.concatenate([hidden_rows(stream ^ other) for other in range(streams)], axis=0)
    for distance in range(tensors):
        arrived = swap(partial_rows(tensor ^ distance), "tensor", distance)
        summed = summed + arrived.astype(jnp.float32)
    residuals = summed.astype(jnp.bfloat16).reshape(streams, share, local_width)
    pair = [swap(residuals[other], "stream", other) for other in range(streams)]
    pair = jnp.concatenate(pair, axis=0)

    whole = jnp.zeros((streams * share, local_width * dps), jnp.bfloat16)
    for distance, block in enumerate(gather_swapped(pair, "dp")):
        whole = lax.dynamic_update_slice_in_dim(whole, block, (dp ^ distance) * local_width, 1)
    whole = whole.reshape(streams, share, -1).astype(jnp.float32)
    inverse = lax.rsqrt(jnp.sum(whole * whole, 2) / MODEL_WIDTH + norm_eps)
    guide = lax.dynamic_slice_in_dim(guidance, stream * half + tensor * share, share, 0)
    own_guide = jnp.where(stream == 0, guide, 1.0 - guide)
    factors = inverse * jnp.stack([own_guide, 1.0 - own_guide])
    mixed = jnp.sum(whole * factors[:, :, None], 0) * gain.astype(jnp.float32)
    mixed = mixed.astype(jnp.bfloat16)

    mixed_blocks = gather_swapped(mixed, "tensor")
    w_head, _ = lax.optimization_barrier((w_head, mixed))
    places = jnp.stack([(tensor ^ distance) * share for distance in range(tensors)])
    guided = head(places.astype(jnp.int32), mixed_blocks, load_to_vmem(w_head), penalty)
    totals = sum_totals(jnp.sum(jnp.exp(guided), 1), ("dp", "tensor"))
    return guided - jnp.log(totals)[:, None]


def solution(mesh):
    return jax.shard_map(
        body,
        mesh=mesh,
        in_specs=(
            P("stream", "tensor", "dp"),
            P("stream", "dp", "tensor", None, None),
            P("stream", "dp", "tensor", None, None),
            P("stream", "dp"),
            P(),
            P(),
            P("dp", "tensor"),
            P("dp", None, "tensor"),
            P("tensor", "dp"),
            P("dp"),
            P(None, ("dp", "tensor")),
        ),
        out_specs=P("stream", ("dp", "tensor")),
        check_vma=False,
    )
```

```python
import math

import jax
import jax.numpy as jnp
import numpy as np
from jax import lax
from jax.experimental import pallas as pl
from jax.experimental.pallas import tpu as pltpu
from jax.sharding import PartitionSpec as P

MODEL_WIDTH = 8192
HEAD_SIZE = 128


rope_theta = 500000.0
penalty_step = 1.5
norm_eps = 1e-05


def swap(value, axis, distance):
    if distance == 0:
        return value
    pairs = [(source, source ^ distance) for source in range(lax.axis_size(axis))]
    return lax.ppermute(value, axis, pairs)


def gather_swapped(value, axis):
    return [swap(value, axis, distance) for distance in range(lax.axis_size(axis))]


def sum_totals(value, axes):
    count = lax.axis_size(axes)
    copies = jnp.broadcast_to(value[None], (count,) + value.shape)
    return jnp.sum(lax.all_to_all(copies, axes, 0, 0, tiled=True), 0)


def matmul_kernel(row_blocks, *refs):
    blocks, weights, out_ref = refs[:row_blocks], refs[row_blocks:-1], refs[-1]
    rows = jnp.concatenate([block[...] for block in blocks], axis=0)
    first = 0
    for weight in weights:
        last = first + weight.shape[1]
        product = jnp.dot(rows, weight[...], preferred_element_type=jnp.float32)
        out_ref[:, first:last] = product.astype(out_ref.dtype)
        first = last


def matmul(blocks, weights, dtype):
    rows = sum(block.shape[0] for block in blocks)
    cols = sum(weight.shape[1] for weight in weights)
    depth = weights[0].shape[0]
    whole = pl.BlockSpec(memory_space=pltpu.VMEM)
    return pl.pallas_call(
        lambda *refs: matmul_kernel(len(blocks), *refs),
        out_shape=jax.ShapeDtypeStruct((rows, cols), dtype),
        in_specs=[whole] * (len(blocks) + len(weights)),
        out_specs=whole,
        compiler_params=pltpu.CompilerParams(vmem_limit_bytes=8 * 1024 * 1024),
        cost_estimate=pl.CostEstimate(
            flops=2 * rows * cols * depth,
            bytes_accessed=2 * (depth * (rows + cols) + rows * cols),
            transcendentals=0,
        ),
    )(*blocks, *[pltpu.with_memory_space_constraint(weight, pltpu.VMEM) for weight in weights])


def head_kernel(places_ref, *refs):
    blocks, (weight_ref, penalty_ref, out_ref) = refs[:-3], refs[-3:]
    rows = jnp.concatenate([block[...] for block in blocks], axis=0)
    logits = jnp.dot(rows, weight_ref[...], preferred_element_type=jnp.float32)
    share = blocks[0].shape[0]
    for i in range(len(blocks)):
        place = pl.ds(pl.multiple_of(places_ref[i], 8), share)
        out_ref[place, :] = logits[i * share : (i + 1) * share] - penalty_ref[place, :]


def head(places, blocks, weight, penalty):
    whole = pl.BlockSpec(memory_space=pltpu.VMEM)
    rows, cols = penalty.shape
    depth = weight.shape[0]
    return pl.pallas_call(
        head_kernel,
        out_shape=jax.ShapeDtypeStruct((rows, cols), jnp.float32),
        in_specs=[pl.BlockSpec(memory_space=pltpu.SMEM)] + [whole] * (len(blocks) + 2),
        out_specs=whole,
        compiler_params=pltpu.CompilerParams(vmem_limit_bytes=8 * 1024 * 1024),
        cost_estimate=pl.CostEstimate(
            flops=2 * rows * cols * depth,
            bytes_accessed=2 * depth * (rows + cols) + 8 * rows * cols,
            transcendentals=0,
        ),
    )(places, *blocks, pltpu.with_memory_space_constraint(weight, pltpu.VMEM), penalty)


def load_kernel(weight_ref, out_ref, sems):
    pieces = sems.shape[0]
    rows = weight_ref.shape[0] // pieces
    copies = []
    for piece in range(pieces):
        part = pl.ds(piece * rows, rows)
        copy = pltpu.make_async_copy(weight_ref.at[part], out_ref.at[part], sems.at[piece])
        copy.start()
        copies.append(copy)
    for copy in copies:
        copy.wait()


def load_to_vmem(weight):
    return pl.pallas_call(
        load_kernel,
        out_shape=pltpu.VMEM(weight.shape, weight.dtype),
        in_specs=[pl.BlockSpec(memory_space=pltpu.HBM)],
        out_specs=pl.BlockSpec(memory_space=pltpu.VMEM),
        scratch_shapes=[pltpu.SemaphoreType.DMA((4,))],
        compiler_params=pltpu.CompilerParams(vmem_limit_bytes=8 * 1024 * 1024),
        cost_estimate=pl.CostEstimate(
            flops=0, bytes_accessed=2 * weight.size * weight.dtype.itemsize, transcendentals=0
        ),
    )(pltpu.with_memory_space_constraint(weight, pltpu.HBM))


def load_projections_kernel(query_ref, pair_ref, query_out, pair_out, pair_raw, sems):
    first = pltpu.make_async_copy(pair_ref, pair_raw, sems.at[0])
    first.start()
    second = pltpu.make_async_copy(query_ref, query_out, sems.at[1])
    second.start()
    first.wait()
    depth, pair, cols = pair_raw.shape
    step = math.gcd(depth, 256)

    def relayout(index, carry):
        rows = pl.ds(pl.multiple_of(index * step, step), step)
        for member in range(pair):
            pair_out[rows, member * cols : (member + 1) * cols] = pair_raw[rows, member, :]
        return carry

    lax.fori_loop(0, depth // step, relayout, 0)
    second.wait()


def load_projections(query, pair):
    depth, members, cols = pair.shape
    arrays = [pltpu.with_memory_space_constraint(array, pltpu.HBM) for array in (query, pair)]
    return pl.pallas_call(
        load_projections_kernel,
        out_shape=(
            pltpu.VMEM(query.shape, query.dtype),
            pltpu.VMEM((depth, members * cols), pair.dtype),
        ),
        in_specs=[pl.BlockSpec(memory_space=pltpu.HBM)] * 2,
        out_specs=[pl.BlockSpec(memory_space=pltpu.VMEM)] * 2,
        scratch_shapes=[pltpu.VMEM(pair.shape, pair.dtype), pltpu.SemaphoreType.DMA((2,))],
        compiler_params=pltpu.CompilerParams(vmem_limit_bytes=16 * 1024 * 1024),
        cost_estimate=pl.CostEstimate(
            flops=0, bytes_accessed=4 * (query.size + pair.size), transcendentals=0
        ),
    )(*arrays)


def rotation(positions):
    halfway = HEAD_SIZE // 2
    frequency = np.asarray(rope_theta ** (-np.arange(halfway) * 2.0 / HEAD_SIZE), np.float32)
    angles = positions.astype(jnp.float32)[:, None, None] * frequency
    return jnp.cos(angles), jnp.sin(angles)


def rotate(values, cosine_term, sine_term):
    halfway = values.shape[-1] // 2
    first_half = values[..., :halfway]
    second_half = values[..., halfway:]
    return jnp.concatenate(
        [
            first_half * cosine_term - second_half * sine_term,
            second_half * cosine_term + first_half * sine_term,
        ],
        axis=-1,
    )


def repeat_counts(recent_ids, first_column, width):
    columns = first_column + jnp.arange(width, dtype=jnp.int32)
    return jnp.sum((recent_ids[:, :, None] == columns[None, None, :]).astype(jnp.float32), 1)


def body(
    hidden,
    cached_rotated_keys,
    cached_values,
    cache_lengths,
    recent_ids,
    guidance,
    w_query,
    key_value_weight,
    w_output,
    norm_gain,
    w_head,
):
    streams, dps, tensors = (lax.axis_size(axis) for axis in ("stream", "dp", "tensor"))
    stream, dp, tensor = (lax.axis_index(axis) for axis in ("stream", "dp", "tensor"))
    local_width = hidden.shape[2]
    query_cols = w_query.shape[1]
    kv_cols = key_value_weight.shape[2]
    local_prompts = cache_lengths.shape[1]
    hidden_prompts = hidden.shape[1]
    prompts = recent_ids.shape[0]
    lengths = cache_lengths[0]
    vocab_local = w_head.shape[1]

    hidden_blocks = gather_swapped(hidden[0], "tensor")
    all_rows = jnp.concatenate(hidden_blocks, axis=0)
    w_query, key_value_weight, stream, dp, tensor = lax.optimization_barrier(
        (w_query, key_value_weight, stream, dp, tensor)
    )
    projected_parts = matmul(
        hidden_blocks, load_projections(w_query, key_value_weight), jnp.bfloat16
    )
    (projected_parts, lengths, recent_ids, guidance, norm_gain, stream, dp, tensor) = (
        lax.optimization_barrier(
            (projected_parts, lengths, recent_ids, guidance, norm_gain, stream, dp, tensor)
        )
    )
    column_base = (dp * tensors + tensor) * vocab_local
    cosine_term, sine_term = rotation(lengths)

    def hidden_place(prompt):
        block = prompt // hidden_prompts
        return (tensor ^ block) * hidden_prompts + prompt % hidden_prompts

    gain_rows = norm_gain.reshape(local_prompts, -1)
    total_cols = query_cols + 2 * kv_cols
    projected, gain_blocks = 0.0, []
    for distance in range(dps):
        sending = lax.dynamic_slice_in_dim(
            projected_parts, hidden_place((dp ^ distance) * local_prompts), local_prompts, 0
        )
        arrived = swap(jnp.concatenate([sending, gain_rows], axis=1), "dp", distance)
        projected = projected + arrived[:, :total_cols].astype(jnp.float32)
        gain_blocks.append(arrived[:, total_cols:].reshape(local_width))
    gain = jnp.zeros((local_width * dps,), norm_gain.dtype)
    for distance, block in enumerate(gain_blocks):
        gain = lax.dynamic_update_slice_in_dim(gain, block, (dp ^ distance) * local_width, 0)

    query_heads = query_cols // HEAD_SIZE
    kv_heads = kv_cols // HEAD_SIZE
    rotated_query = rotate(
        projected[:, :query_cols].reshape(local_prompts, query_heads, HEAD_SIZE),
        cosine_term,
        sine_term,
    ).astype(jnp.bfloat16)
    key_value_rows = projected[:, query_cols:].reshape(local_prompts, 2, kv_heads, HEAD_SIZE)
    fresh_key = rotate(key_value_rows[:, 0], cosine_term, sine_term).astype(jnp.bfloat16)
    value_new = key_value_rows[:, 1].astype(jnp.bfloat16)
    grouped_queries = rotated_query.reshape(
        local_prompts, kv_heads, query_heads // kv_heads, HEAD_SIZE
    )
    attention_scale = HEAD_SIZE ** (-0.5)
    key_block = cached_rotated_keys[0]
    value_block = cached_values[0]
    scores = (
        jnp.einsum(
            "pkgd,pksd->pkgs", grouped_queries, key_block, preferred_element_type=jnp.float32
        )
        * attention_scale
    )
    self_score = (
        jnp.einsum("pkgd,pkd->pkg", grouped_queries, fresh_key, preferred_element_type=jnp.float32)
        * attention_scale
    )
    valid = jnp.arange(key_block.shape[2], dtype=jnp.int32)[None, :] < lengths[:, None]
    exps = jnp.where(valid[:, None, None, :], jnp.exp(scores), 0.0)
    own_exp = jnp.exp(self_score)
    denominator = jnp.sum(exps, -1) + own_exp
    weights = (exps / denominator[..., None]).astype(jnp.bfloat16)
    own_weight = (own_exp / denominator).astype(jnp.bfloat16)
    attended = jnp.einsum(
        "pkgs,pksd->pkgd", weights, value_block, preferred_element_type=jnp.float32
    )
    attended = (
        attended
        + own_weight.astype(jnp.float32)[..., None] * value_new.astype(jnp.float32)[:, :, None, :]
    )
    attended = attended.reshape(local_prompts, query_cols).astype(jnp.bfloat16)

    half = prompts // streams
    recent_mine = lax.dynamic_slice_in_dim(recent_ids, stream * half, half, 0)
    penalty = penalty_step * repeat_counts(recent_mine, column_base, vocab_local)
    attended, penalty = lax.optimization_barrier((attended, penalty))

    attended_blocks = gather_swapped(attended, "dp")
    w_output, _ = lax.optimization_barrier((w_output, attended))
    partial_out = matmul(attended_blocks, [load_to_vmem(w_output)], jnp.bfloat16)

    share = half // tensors

    def partial_rows(tensor_to):
        parts = []
        for other in range(streams):
            prompt = (stream ^ other) * half + tensor_to * share
            place = (dp ^ (prompt // local_prompts)) * local_prompts + prompt % local_prompts
            parts.append(lax.dynamic_slice_in_dim(partial_out, place, share, 0))
        return jnp.concatenate(parts, axis=0)

    def hidden_rows(stream_to):
        place = hidden_place(stream_to * half + tensor * share)
        return lax.dynamic_slice_in_dim(all_rows, place, share, 0).astype(jnp.float32)

    summed = jnp.concatenate([hidden_rows(stream ^ other) for other in range(streams)], axis=0)
    for distance in range(tensors):
        arrived = swap(partial_rows(tensor ^ distance), "tensor", distance)
        summed = summed + arrived.astype(jnp.float32)
    residuals = summed.astype(jnp.bfloat16).reshape(streams, share, local_width)
    pair = [swap(residuals[other], "stream", other) for other in range(streams)]
    pair = jnp.concatenate(pair, axis=0)

    whole = jnp.zeros((streams * share, local_width * dps), jnp.bfloat16)
    for distance, block in enumerate(gather_swapped(pair, "dp")):
        whole = lax.dynamic_update_slice_in_dim(whole, block, (dp ^ distance) * local_width, 1)
    whole = whole.reshape(streams, share, -1).astype(jnp.float32)
    inverse = lax.rsqrt(jnp.sum(whole * whole, 2) / MODEL_WIDTH + norm_eps)
    guide = lax.dynamic_slice_in_dim(guidance, stream * half + tensor * share, share, 0)
    own_guide = jnp.where(stream == 0, guide, 1.0 - guide)
    factors = inverse * jnp.stack([own_guide, 1.0 - own_guide])
    mixed = jnp.sum(whole * factors[:, :, None], 0) * gain.astype(jnp.float32)
    mixed = mixed.astype(jnp.bfloat16)

    mixed_blocks = gather_swapped(mixed, "tensor")
    w_head, _ = lax.optimization_barrier((w_head, mixed))
    places = jnp.stack([(tensor ^ distance) * share for distance in range(tensors)])
    guided = head(places.astype(jnp.int32), mixed_blocks, load_to_vmem(w_head), penalty)
    totals = sum_totals(jnp.sum(jnp.exp(guided), 1), ("dp", "tensor"))
    return guided - jnp.log(totals)[:, None]


def solution(mesh):
    return jax.shard_map(
        body,
        mesh=mesh,
        in_specs=(
            P("stream", "tensor", "dp"),
            P("stream", "dp", "tensor", None, None),
            P("stream", "dp", "tensor", None, None),
            P("stream", "dp"),
            P(),
            P(),
            P("dp", "tensor"),
            P("dp", None, "tensor"),
            P("tensor", "dp"),
            P("dp"),
            P(None, ("dp", "tensor")),
        ),
        out_specs=P("stream", ("dp", "tensor")),
        check_vma=False,
    )
```

```python
import math

import jax
import jax.numpy as jnp
import numpy as np
from jax import lax
from jax.experimental import pallas as pl
from jax.experimental.pallas import tpu as pltpu
from jax.sharding import PartitionSpec as P

MODEL_WIDTH = 8192
HEAD_SIZE = 128


rope_theta = 500000.0
penalty_step = 1.5
norm_eps = 1e-05


def swap(value, axis, distance):
    if distance == 0:
        return value
    pairs = [(source, source ^ distance) for source in range(lax.axis_size(axis))]
    return lax.ppermute(value, axis, pairs)


def far_first(axis):
    return range(lax.axis_size(axis) - 1, -1, -1)


def gather_swapped(value, axis):
    return [swap(value, axis, distance) for distance in far_first(axis)]


def sum_totals(value, axes):
    count = lax.axis_size(axes)
    copies = jnp.broadcast_to(value[None], (count,) + value.shape)
    return jnp.sum(lax.all_to_all(copies, axes, 0, 0, tiled=True), 0)


def matmul_kernel(row_blocks, *refs):
    blocks, weights, out_ref = refs[:row_blocks], refs[row_blocks:-1], refs[-1]
    rows = jnp.concatenate([block[...] for block in blocks], axis=0)
    first = 0
    for weight in weights:
        last = first + weight.shape[1]
        product = jnp.dot(rows, weight[...], preferred_element_type=jnp.float32)
        out_ref[:, first:last] = product.astype(out_ref.dtype)
        first = last


def matmul(blocks, weights, dtype):
    rows = sum(block.shape[0] for block in blocks)
    cols = sum(weight.shape[1] for weight in weights)
    depth = weights[0].shape[0]
    whole = pl.BlockSpec(memory_space=pltpu.VMEM)
    return pl.pallas_call(
        lambda *refs: matmul_kernel(len(blocks), *refs),
        out_shape=jax.ShapeDtypeStruct((rows, cols), dtype),
        in_specs=[whole] * (len(blocks) + len(weights)),
        out_specs=whole,
        compiler_params=pltpu.CompilerParams(vmem_limit_bytes=8 * 1024 * 1024),
        cost_estimate=pl.CostEstimate(
            flops=2 * rows * cols * depth,
            bytes_accessed=2 * (depth * (rows + cols) + rows * cols),
            transcendentals=0,
        ),
    )(*blocks, *[pltpu.with_memory_space_constraint(weight, pltpu.VMEM) for weight in weights])


def head_kernel(places_ref, *refs):
    blocks, (weight_ref, penalty_ref, out_ref) = refs[:-3], refs[-3:]
    rows = jnp.concatenate([block[...] for block in blocks], axis=0)
    logits = jnp.dot(rows, weight_ref[...], preferred_element_type=jnp.float32)
    share = blocks[0].shape[0]
    for i in range(len(blocks)):
        place = pl.ds(pl.multiple_of(places_ref[i], 8), share)
        out_ref[place, :] = logits[i * share : (i + 1) * share] - penalty_ref[place, :]


def head(places, blocks, weight, penalty):
    whole = pl.BlockSpec(memory_space=pltpu.VMEM)
    rows, cols = penalty.shape
    depth = weight.shape[0]
    return pl.pallas_call(
        head_kernel,
        out_shape=jax.ShapeDtypeStruct((rows, cols), jnp.float32),
        in_specs=[pl.BlockSpec(memory_space=pltpu.SMEM)] + [whole] * (len(blocks) + 2),
        out_specs=whole,
        compiler_params=pltpu.CompilerParams(vmem_limit_bytes=8 * 1024 * 1024),
        cost_estimate=pl.CostEstimate(
            flops=2 * rows * cols * depth,
            bytes_accessed=2 * depth * (rows + cols) + 8 * rows * cols,
            transcendentals=0,
        ),
    )(places, *blocks, pltpu.with_memory_space_constraint(weight, pltpu.VMEM), penalty)


def load_kernel(weight_ref, out_ref, sems):
    pieces = sems.shape[0]
    rows = out_ref.shape[0] // pieces
    copies = []
    for piece in range(pieces):
        part = pl.ds(piece * rows, rows)
        copy = pltpu.make_async_copy(weight_ref.at[part], out_ref.at[part], sems.at[piece])
        copy.start()
        copies.append(copy)
    for copy in copies:
        copy.wait()


def load_to_vmem(weight, rows):
    return pl.pallas_call(
        load_kernel,
        out_shape=pltpu.VMEM((rows, weight.shape[1]), weight.dtype),
        in_specs=[pl.BlockSpec(memory_space=pltpu.HBM)],
        out_specs=pl.BlockSpec(memory_space=pltpu.VMEM),
        scratch_shapes=[pltpu.SemaphoreType.DMA((4,))],
        compiler_params=pltpu.CompilerParams(vmem_limit_bytes=8 * 1024 * 1024),
        cost_estimate=pl.CostEstimate(
            flops=0, bytes_accessed=4 * rows * weight.shape[1], transcendentals=0
        ),
    )(pltpu.with_memory_space_constraint(weight, pltpu.HBM))


def split_matmul_kernel(*refs):
    blocks, (early_ref, weight_ref, out_ref, late, sem) = refs[:-5], refs[-5:]
    early = early_ref.shape[0]
    copy = pltpu.make_async_copy(weight_ref.at[pl.ds(early, late.shape[0])], late, sem)
    copy.start()
    rows = jnp.concatenate([block[...] for block in blocks], axis=0)
    total = jnp.dot(rows[:, :early], early_ref[...], preferred_element_type=jnp.float32)
    copy.wait()
    total += jnp.dot(rows[:, early:], late[...], preferred_element_type=jnp.float32)
    out_ref[...] = total.astype(out_ref.dtype)


def split_matmul(blocks, weight, dtype):
    rows = sum(block.shape[0] for block in blocks)
    depth, cols = weight.shape
    early = load_to_vmem(weight, depth - depth // 4)
    whole = pl.BlockSpec(memory_space=pltpu.VMEM)
    return pl.pallas_call(
        split_matmul_kernel,
        out_shape=jax.ShapeDtypeStruct((rows, cols), dtype),
        in_specs=[whole] * (len(blocks) + 1) + [pl.BlockSpec(memory_space=pltpu.HBM)],
        out_specs=whole,
        scratch_shapes=[pltpu.VMEM((depth // 4, cols), weight.dtype), pltpu.SemaphoreType.DMA],
        compiler_params=pltpu.CompilerParams(vmem_limit_bytes=16 * 1024 * 1024),
        cost_estimate=pl.CostEstimate(
            flops=2 * rows * cols * depth,
            bytes_accessed=2 * (depth * (rows + cols) + rows * cols),
            transcendentals=0,
        ),
    )(
        *blocks,
        pltpu.with_memory_space_constraint(early, pltpu.VMEM),
        pltpu.with_memory_space_constraint(weight, pltpu.HBM),
    )


def load_projections_kernel(query_ref, pair_ref, query_out, pair_out, pair_raw, sems):
    first = pltpu.make_async_copy(pair_ref, pair_raw, sems.at[0])
    first.start()
    second = pltpu.make_async_copy(query_ref, query_out, sems.at[1])
    second.start()
    first.wait()
    depth, pair, cols = pair_raw.shape
    step = math.gcd(depth, 256)

    def relayout(index, carry):
        rows = pl.ds(pl.multiple_of(index * step, step), step)
        for member in range(pair):
            pair_out[rows, member * cols : (member + 1) * cols] = pair_raw[rows, member, :]
        return carry

    lax.fori_loop(0, depth // step, relayout, 0)
    second.wait()


def load_projections(query, pair):
    depth, members, cols = pair.shape
    arrays = [pltpu.with_memory_space_constraint(array, pltpu.HBM) for array in (query, pair)]
    return pl.pallas_call(
        load_projections_kernel,
        out_shape=(
            pltpu.VMEM(query.shape, query.dtype),
            pltpu.VMEM((depth, members * cols), pair.dtype),
        ),
        in_specs=[pl.BlockSpec(memory_space=pltpu.HBM)] * 2,
        out_specs=[pl.BlockSpec(memory_space=pltpu.VMEM)] * 2,
        scratch_shapes=[pltpu.VMEM(pair.shape, pair.dtype), pltpu.SemaphoreType.DMA((2,))],
        compiler_params=pltpu.CompilerParams(vmem_limit_bytes=16 * 1024 * 1024),
        cost_estimate=pl.CostEstimate(
            flops=0, bytes_accessed=4 * (query.size + pair.size), transcendentals=0
        ),
    )(*arrays)


def rotation(positions):
    halfway = HEAD_SIZE // 2
    frequency = np.asarray(rope_theta ** (-np.arange(halfway) * 2.0 / HEAD_SIZE), np.float32)
    angles = positions.astype(jnp.float32)[:, None, None] * frequency
    return jnp.cos(angles), jnp.sin(angles)


def rotate(values, cosine_term, sine_term):
    halfway = values.shape[-1] // 2
    first_half = values[..., :halfway]
    second_half = values[..., halfway:]
    return jnp.concatenate(
        [
            first_half * cosine_term - second_half * sine_term,
            second_half * cosine_term + first_half * sine_term,
        ],
        axis=-1,
    )


def repeat_counts(recent_ids, first_column, width):
    columns = first_column + jnp.arange(width, dtype=jnp.int32)
    return jnp.sum((recent_ids[:, :, None] == columns[None, None, :]).astype(jnp.float32), 1)


def body(
    hidden,
    cached_rotated_keys,
    cached_values,
    cache_lengths,
    recent_ids,
    guidance,
    w_query,
    key_value_weight,
    w_output,
    norm_gain,
    w_head,
):
    streams, dps, tensors = (lax.axis_size(axis) for axis in ("stream", "dp", "tensor"))
    stream, dp, tensor = (lax.axis_index(axis) for axis in ("stream", "dp", "tensor"))
    local_width = hidden.shape[2]
    query_cols = w_query.shape[1]
    kv_cols = key_value_weight.shape[2]
    local_prompts = cache_lengths.shape[1]
    hidden_prompts = hidden.shape[1]
    prompts = recent_ids.shape[0]
    lengths = cache_lengths[0]
    vocab_local = w_head.shape[1]

    hidden_blocks = gather_swapped(hidden[0], "tensor")
    all_rows = jnp.concatenate(hidden_blocks, axis=0)
    w_query, key_value_weight, stream, dp, tensor = lax.optimization_barrier(
        (w_query, key_value_weight, stream, dp, tensor)
    )
    projected_parts = matmul(
        hidden_blocks, load_projections(w_query, key_value_weight), jnp.bfloat16
    )
    (projected_parts, lengths, recent_ids, guidance, norm_gain, stream, dp, tensor) = (
        lax.optimization_barrier(
            (projected_parts, lengths, recent_ids, guidance, norm_gain, stream, dp, tensor)
        )
    )
    column_base = (dp * tensors + tensor) * vocab_local
    cosine_term, sine_term = rotation(lengths)

    def hidden_place(prompt):
        block = prompt // hidden_prompts
        return (tensors - 1 - (tensor ^ block)) * hidden_prompts + prompt % hidden_prompts

    gain_rows = norm_gain.reshape(local_prompts, -1)
    total_cols = query_cols + 2 * kv_cols
    projected, gain_blocks = 0.0, []
    for distance in far_first("dp"):
        sending = lax.dynamic_slice_in_dim(
            projected_parts, hidden_place((dp ^ distance) * local_prompts), local_prompts, 0
        )
        arrived = swap(jnp.concatenate([sending, gain_rows], axis=1), "dp", distance)
        projected = projected + arrived[:, :total_cols].astype(jnp.float32)
        gain_blocks.append(arrived[:, total_cols:].reshape(local_width))
    gain = jnp.zeros((local_width * dps,), norm_gain.dtype)
    for distance, block in zip(far_first("dp"), gain_blocks):
        gain = lax.dynamic_update_slice_in_dim(gain, block, (dp ^ distance) * local_width, 0)

    query_heads = query_cols // HEAD_SIZE
    kv_heads = kv_cols // HEAD_SIZE
    rotated_query = rotate(
        projected[:, :query_cols].reshape(local_prompts, query_heads, HEAD_SIZE),
        cosine_term,
        sine_term,
    ).astype(jnp.bfloat16)
    key_value_rows = projected[:, query_cols:].reshape(local_prompts, 2, kv_heads, HEAD_SIZE)
    fresh_key = rotate(key_value_rows[:, 0], cosine_term, sine_term).astype(jnp.bfloat16)
    value_new = key_value_rows[:, 1].astype(jnp.bfloat16)
    grouped_queries = rotated_query.reshape(
        local_prompts, kv_heads, query_heads // kv_heads, HEAD_SIZE
    )
    attention_scale = HEAD_SIZE ** (-0.5)
    key_block = cached_rotated_keys[0]
    value_block = cached_values[0]
    scores = (
        jnp.einsum(
            "pkgd,pksd->pkgs", grouped_queries, key_block, preferred_element_type=jnp.float32
        )
        * attention_scale
    )
    self_score = (
        jnp.einsum("pkgd,pkd->pkg", grouped_queries, fresh_key, preferred_element_type=jnp.float32)
        * attention_scale
    )
    valid = jnp.arange(key_block.shape[2], dtype=jnp.int32)[None, :] < lengths[:, None]
    exps = jnp.where(valid[:, None, None, :], jnp.exp(scores), 0.0)
    own_exp = jnp.exp(self_score)
    denominator = jnp.sum(exps, -1) + own_exp
    weights = (exps / denominator[..., None]).astype(jnp.bfloat16)
    own_weight = (own_exp / denominator).astype(jnp.bfloat16)
    attended = jnp.einsum(
        "pkgs,pksd->pkgd", weights, value_block, preferred_element_type=jnp.float32
    )
    attended = (
        attended
        + own_weight.astype(jnp.float32)[..., None] * value_new.astype(jnp.float32)[:, :, None, :]
    )
    attended = attended.reshape(local_prompts, query_cols).astype(jnp.bfloat16)

    half = prompts // streams
    recent_mine = lax.dynamic_slice_in_dim(recent_ids, stream * half, half, 0)
    penalty = penalty_step * repeat_counts(recent_mine, column_base, vocab_local)
    attended, penalty = lax.optimization_barrier((attended, penalty))

    attended_blocks = gather_swapped(attended, "dp")
    w_output, _ = lax.optimization_barrier((w_output, attended))
    partial_out = split_matmul(attended_blocks, w_output, jnp.bfloat16)

    share = half // tensors

    def partial_rows(tensor_to):
        parts = []
        for other in range(streams):
            prompt = (stream ^ other) * half + tensor_to * share
            block = dps - 1 - (dp ^ (prompt // local_prompts))
            place = block * local_prompts + prompt % local_prompts
            parts.append(lax.dynamic_slice_in_dim(partial_out, place, share, 0))
        return jnp.concatenate(parts, axis=0)

    def hidden_rows(stream_to):
        place = hidden_place(stream_to * half + tensor * share)
        return lax.dynamic_slice_in_dim(all_rows, place, share, 0).astype(jnp.float32)

    summed = jnp.concatenate([hidden_rows(stream ^ other) for other in range(streams)], axis=0)
    for distance in far_first("tensor"):
        arrived = swap(partial_rows(tensor ^ distance), "tensor", distance)
        summed = summed + arrived.astype(jnp.float32)
    residuals = summed.astype(jnp.bfloat16).reshape(streams, share, local_width)
    pair = [swap(residuals[other], "stream", other) for other in range(streams)]
    pair = jnp.concatenate(pair, axis=0)

    whole = jnp.zeros((streams * share, local_width * dps), jnp.bfloat16)
    for distance, block in zip(far_first("dp"), gather_swapped(pair, "dp")):
        whole = lax.dynamic_update_slice_in_dim(whole, block, (dp ^ distance) * local_width, 1)
    whole = whole.reshape(streams, share, -1).astype(jnp.float32)
    inverse = lax.rsqrt(jnp.sum(whole * whole, 2) / MODEL_WIDTH + norm_eps)
    guide = lax.dynamic_slice_in_dim(guidance, stream * half + tensor * share, share, 0)
    own_guide = jnp.where(stream == 0, guide, 1.0 - guide)
    factors = inverse * jnp.stack([own_guide, 1.0 - own_guide])
    mixed = jnp.sum(whole * factors[:, :, None], 0) * gain.astype(jnp.float32)
    mixed = mixed.astype(jnp.bfloat16)

    mixed_blocks = gather_swapped(mixed, "tensor")
    w_head, _ = lax.optimization_barrier((w_head, mixed))
    places = jnp.stack([(tensor ^ distance) * share for distance in far_first("tensor")])
    guided = head(places.astype(jnp.int32), mixed_blocks, load_to_vmem(w_head, w_head.shape[0]), penalty)
    totals = sum_totals(jnp.sum(jnp.exp(guided), 1), ("dp", "tensor"))
    return guided - jnp.log(totals)[:, None]


def solution(mesh):
    return jax.shard_map(
        body,
        mesh=mesh,
        in_specs=(
            P("stream", "tensor", "dp"),
            P("stream", "dp", "tensor", None, None),
            P("stream", "dp", "tensor", None, None),
            P("stream", "dp"),
            P(),
            P(),
            P("dp", "tensor"),
            P("dp", None, "tensor"),
            P("tensor", "dp"),
            P("dp"),
            P(None, ("dp", "tensor")),
        ),
        out_specs=P("stream", ("dp", "tensor")),
        check_vma=False,
    )
```

```python
import math

import jax
import jax.numpy as jnp
import numpy as np
from jax import lax
from jax.experimental import pallas as pl
from jax.experimental.pallas import tpu as pltpu
from jax.sharding import PartitionSpec as P

MODEL_WIDTH = 8192
HEAD_SIZE = 128


rope_theta = 500000.0
penalty_step = 1.5
norm_eps = 1e-05


def swap(value, axis, distance):
    if distance == 0:
        return value
    pairs = [(source, source ^ distance) for source in range(lax.axis_size(axis))]
    return lax.ppermute(value, axis, pairs)


def far_first(axis):
    return range(lax.axis_size(axis) - 1, -1, -1)


def gather_swapped(value, axis):
    return [swap(value, axis, distance) for distance in far_first(axis)]


def sum_totals(value, axes):
    count = lax.axis_size(axes)
    copies = jnp.broadcast_to(value[None], (count,) + value.shape)
    return jnp.sum(lax.all_to_all(copies, axes, 0, 0, tiled=True), 0)


def matmul_kernel(row_blocks, *refs):
    blocks, weights, out_ref = refs[:row_blocks], refs[row_blocks:-1], refs[-1]
    rows = jnp.concatenate([block[...] for block in blocks], axis=0)
    first = 0
    for weight in weights:
        last = first + weight.shape[1]
        product = jnp.dot(rows, weight[...], preferred_element_type=jnp.float32)
        out_ref[:, first:last] = product.astype(out_ref.dtype)
        first = last


def matmul(blocks, weights, dtype):
    rows = sum(block.shape[0] for block in blocks)
    cols = sum(weight.shape[1] for weight in weights)
    depth = weights[0].shape[0]
    whole = pl.BlockSpec(memory_space=pltpu.VMEM)
    return pl.pallas_call(
        lambda *refs: matmul_kernel(len(blocks), *refs),
        out_shape=jax.ShapeDtypeStruct((rows, cols), dtype),
        in_specs=[whole] * (len(blocks) + len(weights)),
        out_specs=whole,
        compiler_params=pltpu.CompilerParams(vmem_limit_bytes=8 * 1024 * 1024),
        cost_estimate=pl.CostEstimate(
            flops=2 * rows * cols * depth,
            bytes_accessed=2 * (depth * (rows + cols) + rows * cols),
            transcendentals=0,
        ),
    )(*blocks, *[pltpu.with_memory_space_constraint(weight, pltpu.VMEM) for weight in weights])


def head_kernel(places_ref, *refs):
    blocks, (weight_ref, penalty_ref, out_ref) = refs[:-3], refs[-3:]
    rows = jnp.concatenate([block[...] for block in blocks], axis=0)
    logits = jnp.dot(rows, weight_ref[...], preferred_element_type=jnp.float32)
    share = blocks[0].shape[0]
    for i in range(len(blocks)):
        place = pl.ds(pl.multiple_of(places_ref[i], 8), share)
        out_ref[place, :] = logits[i * share : (i + 1) * share] - penalty_ref[place, :]


def head(places, blocks, weight, penalty):
    whole = pl.BlockSpec(memory_space=pltpu.VMEM)
    rows, cols = penalty.shape
    depth = weight.shape[0]
    return pl.pallas_call(
        head_kernel,
        out_shape=jax.ShapeDtypeStruct((rows, cols), jnp.float32),
        in_specs=[pl.BlockSpec(memory_space=pltpu.SMEM)] + [whole] * (len(blocks) + 2),
        out_specs=whole,
        compiler_params=pltpu.CompilerParams(vmem_limit_bytes=8 * 1024 * 1024),
        cost_estimate=pl.CostEstimate(
            flops=2 * rows * cols * depth,
            bytes_accessed=2 * depth * (rows + cols) + 8 * rows * cols,
            transcendentals=0,
        ),
    )(places, *blocks, pltpu.with_memory_space_constraint(weight, pltpu.VMEM), penalty)


def load_kernel(weight_ref, out_ref, sems):
    pieces = sems.shape[0]
    rows = out_ref.shape[0] // pieces
    copies = []
    for piece in range(pieces):
        part = pl.ds(piece * rows, rows)
        copy = pltpu.make_async_copy(weight_ref.at[part], out_ref.at[part], sems.at[piece])
        copy.start()
        copies.append(copy)
    for copy in copies:
        copy.wait()


def load_to_vmem(weight):
    return pl.pallas_call(
        load_kernel,
        out_shape=pltpu.VMEM(weight.shape, weight.dtype),
        in_specs=[pl.BlockSpec(memory_space=pltpu.HBM)],
        out_specs=pl.BlockSpec(memory_space=pltpu.VMEM),
        scratch_shapes=[pltpu.SemaphoreType.DMA((4,))],
        compiler_params=pltpu.CompilerParams(vmem_limit_bytes=8 * 1024 * 1024),
        cost_estimate=pl.CostEstimate(
            flops=0, bytes_accessed=4 * weight.size, transcendentals=0
        ),
    )(pltpu.with_memory_space_constraint(weight, pltpu.HBM))


def load_projections_kernel(query_ref, pair_ref, query_out, pair_out, pair_raw, sems):
    pieces = sems.shape[0] - 1
    depth, members, cols = pair_raw.shape
    rows = depth // pieces
    step = math.gcd(rows, 256)
    copies = []
    for piece in range(pieces):
        part = pl.ds(piece * rows, rows)
        copy = pltpu.make_async_copy(pair_ref.at[part], pair_raw.at[part], sems.at[piece])
        copy.start()
        copies.append(copy)
    query_copy = pltpu.make_async_copy(query_ref, query_out, sems.at[pieces])
    query_copy.start()
    for piece in range(pieces):
        copies[piece].wait()

        def relayout(index, carry, first=piece * rows):
            part = pl.ds(pl.multiple_of(first + index * step, step), step)
            for member in range(members):
                pair_out[part, member * cols : (member + 1) * cols] = pair_raw[part, member, :]
            return carry

        lax.fori_loop(0, rows // step, relayout, 0)
    query_copy.wait()


def load_projections(query, pair):
    depth, members, cols = pair.shape
    arrays = [pltpu.with_memory_space_constraint(array, pltpu.HBM) for array in (query, pair)]
    return pl.pallas_call(
        load_projections_kernel,
        out_shape=(
            pltpu.VMEM(query.shape, query.dtype),
            pltpu.VMEM((depth, members * cols), pair.dtype),
        ),
        in_specs=[pl.BlockSpec(memory_space=pltpu.HBM)] * 2,
        out_specs=[pl.BlockSpec(memory_space=pltpu.VMEM)] * 2,
        scratch_shapes=[pltpu.VMEM(pair.shape, pair.dtype), pltpu.SemaphoreType.DMA((5,))],
        compiler_params=pltpu.CompilerParams(vmem_limit_bytes=16 * 1024 * 1024),
        cost_estimate=pl.CostEstimate(
            flops=0, bytes_accessed=4 * (query.size + pair.size), transcendentals=0
        ),
    )(*arrays)


def rotation(positions):
    halfway = HEAD_SIZE // 2
    frequency = np.asarray(rope_theta ** (-np.arange(halfway) * 2.0 / HEAD_SIZE), np.float32)
    angles = positions.astype(jnp.float32)[:, None, None] * frequency
    return jnp.cos(angles), jnp.sin(angles)


def rotate(values, cosine_term, sine_term):
    halfway = values.shape[-1] // 2
    first_half = values[..., :halfway]
    second_half = values[..., halfway:]
    return jnp.concatenate(
        [
            first_half * cosine_term - second_half * sine_term,
            second_half * cosine_term + first_half * sine_term,
        ],
        axis=-1,
    )


def repeat_counts(recent_ids, first_column, width):
    columns = first_column + jnp.arange(width, dtype=jnp.int32)
    return jnp.sum((recent_ids[:, :, None] == columns[None, None, :]).astype(jnp.float32), 1)


def body(
    hidden,
    cached_rotated_keys,
    cached_values,
    cache_lengths,
    recent_ids,
    guidance,
    w_query,
    key_value_weight,
    w_output,
    norm_gain,
    w_head,
):
    streams, dps, tensors = (lax.axis_size(axis) for axis in ("stream", "dp", "tensor"))
    stream, dp, tensor = (lax.axis_index(axis) for axis in ("stream", "dp", "tensor"))
    local_width = hidden.shape[2]
    query_cols = w_query.shape[1]
    kv_cols = key_value_weight.shape[2]
    local_prompts = cache_lengths.shape[1]
    hidden_prompts = hidden.shape[1]
    prompts = recent_ids.shape[0]
    lengths = cache_lengths[0]
    vocab_local = w_head.shape[1]

    hidden_blocks = gather_swapped(hidden[0], "tensor")
    all_rows = jnp.concatenate(hidden_blocks, axis=0)
    w_query, key_value_weight, stream, dp, tensor = lax.optimization_barrier(
        (w_query, key_value_weight, stream, dp, tensor)
    )
    projected_parts = matmul(
        hidden_blocks, load_projections(w_query, key_value_weight), jnp.bfloat16
    )
    (projected_parts, lengths, recent_ids, guidance, norm_gain, stream, dp, tensor) = (
        lax.optimization_barrier(
            (projected_parts, lengths, recent_ids, guidance, norm_gain, stream, dp, tensor)
        )
    )
    column_base = (dp * tensors + tensor) * vocab_local
    cosine_term, sine_term = rotation(lengths)

    def hidden_place(prompt):
        block = prompt // hidden_prompts
        return (tensors - 1 - (tensor ^ block)) * hidden_prompts + prompt % hidden_prompts

    gain_rows = norm_gain.reshape(local_prompts, -1)
    total_cols = query_cols + 2 * kv_cols
    projected, gain_blocks = 0.0, []
    for distance in far_first("dp"):
        sending = lax.dynamic_slice_in_dim(
            projected_parts, hidden_place((dp ^ distance) * local_prompts), local_prompts, 0
        )
        arrived = swap(jnp.concatenate([sending, gain_rows], axis=1), "dp", distance)
        projected = projected + arrived[:, :total_cols].astype(jnp.float32)
        gain_blocks.append(arrived[:, total_cols:].reshape(local_width))
    gain = jnp.zeros((local_width * dps,), norm_gain.dtype)
    for distance, block in zip(far_first("dp"), gain_blocks):
        gain = lax.dynamic_update_slice_in_dim(gain, block, (dp ^ distance) * local_width, 0)

    query_heads = query_cols // HEAD_SIZE
    kv_heads = kv_cols // HEAD_SIZE
    rotated_query = rotate(
        projected[:, :query_cols].reshape(local_prompts, query_heads, HEAD_SIZE),
        cosine_term,
        sine_term,
    ).astype(jnp.bfloat16)
    key_value_rows = projected[:, query_cols:].reshape(local_prompts, 2, kv_heads, HEAD_SIZE)
    fresh_key = rotate(key_value_rows[:, 0], cosine_term, sine_term).astype(jnp.bfloat16)
    value_new = key_value_rows[:, 1].astype(jnp.bfloat16)
    grouped_queries = rotated_query.reshape(
        local_prompts, kv_heads, query_heads // kv_heads, HEAD_SIZE
    )
    attention_scale = HEAD_SIZE ** (-0.5)
    key_block = cached_rotated_keys[0]
    value_block = cached_values[0]
    scores = (
        jnp.einsum(
            "pkgd,pksd->pkgs", grouped_queries, key_block, preferred_element_type=jnp.float32
        )
        * attention_scale
    )
    self_score = (
        jnp.einsum("pkgd,pkd->pkg", grouped_queries, fresh_key, preferred_element_type=jnp.float32)
        * attention_scale
    )
    valid = jnp.arange(key_block.shape[2], dtype=jnp.int32)[None, :] < lengths[:, None]
    exps = jnp.where(valid[:, None, None, :], jnp.exp(scores), 0.0)
    own_exp = jnp.exp(self_score)
    denominator = jnp.sum(exps, -1) + own_exp
    weights = (exps / denominator[..., None]).astype(jnp.bfloat16)
    own_weight = (own_exp / denominator).astype(jnp.bfloat16)
    attended = jnp.einsum(
        "pkgs,pksd->pkgd", weights, value_block, preferred_element_type=jnp.float32
    )
    attended = (
        attended
        + own_weight.astype(jnp.float32)[..., None] * value_new.astype(jnp.float32)[:, :, None, :]
    )
    attended = attended.reshape(local_prompts, query_cols).astype(jnp.bfloat16)

    half = prompts // streams
    recent_mine = lax.dynamic_slice_in_dim(recent_ids, stream * half, half, 0)
    penalty = penalty_step * repeat_counts(recent_mine, column_base, vocab_local)
    attended, penalty = lax.optimization_barrier((attended, penalty))

    attended_blocks = gather_swapped(attended, "dp")
    w_output, _ = lax.optimization_barrier((w_output, attended))
    partial_out = matmul(attended_blocks, [load_to_vmem(w_output)], jnp.bfloat16)

    share = half // tensors

    def partial_rows(tensor_to):
        parts = []
        for other in range(streams):
            prompt = (stream ^ other) * half + tensor_to * share
            block = dps - 1 - (dp ^ (prompt // local_prompts))
            place = block * local_prompts + prompt % local_prompts
            parts.append(lax.dynamic_slice_in_dim(partial_out, place, share, 0))
        return jnp.concatenate(parts, axis=0)

    def hidden_rows(stream_to):
        place = hidden_place(stream_to * half + tensor * share)
        return lax.dynamic_slice_in_dim(all_rows, place, share, 0).astype(jnp.float32)

    summed = jnp.concatenate([hidden_rows(stream ^ other) for other in range(streams)], axis=0)
    for distance in far_first("tensor"):
        arrived = swap(partial_rows(tensor ^ distance), "tensor", distance)
        summed = summed + arrived.astype(jnp.float32)
    residuals = summed.astype(jnp.bfloat16).reshape(streams, share, local_width)
    pair = [swap(residuals[other], "stream", other) for other in range(streams)]
    pair = jnp.concatenate(pair, axis=0)

    whole = jnp.zeros((streams * share, local_width * dps), jnp.bfloat16)
    for distance, block in zip(far_first("dp"), gather_swapped(pair, "dp")):
        whole = lax.dynamic_update_slice_in_dim(whole, block, (dp ^ distance) * local_width, 1)
    whole = whole.reshape(streams, share, -1).astype(jnp.float32)
    inverse = lax.rsqrt(jnp.sum(whole * whole, 2) / MODEL_WIDTH + norm_eps)
    guide = lax.dynamic_slice_in_dim(guidance, stream * half + tensor * share, share, 0)
    own_guide = jnp.where(stream == 0, guide, 1.0 - guide)
    factors = inverse * jnp.stack([own_guide, 1.0 - own_guide])
    mixed = jnp.sum(whole * factors[:, :, None], 0) * gain.astype(jnp.float32)
    mixed = mixed.astype(jnp.bfloat16)

    mixed_blocks = [swap(mixed, "tensor", distance) for distance in range(tensors)]
    w_head, _ = lax.optimization_barrier((w_head, mixed))
    places = jnp.stack([(tensor ^ distance) * share for distance in range(tensors)])
    guided = head(places.astype(jnp.int32), mixed_blocks, load_to_vmem(w_head), penalty)
    totals = sum_totals(jnp.sum(jnp.exp(guided), 1), ("dp", "tensor"))
    return guided - jnp.log(totals)[:, None]


def solution(mesh):
    return jax.shard_map(
        body,
        mesh=mesh,
        in_specs=(
            P("stream", "tensor", "dp"),
            P("stream", "dp", "tensor", None, None),
            P("stream", "dp", "tensor", None, None),
            P("stream", "dp"),
            P(),
            P(),
            P("dp", "tensor"),
            P("dp", None, "tensor"),
            P("tensor", "dp"),
            P("dp"),
            P(None, ("dp", "tensor")),
        ),
        out_specs=P("stream", ("dp", "tensor")),
        check_vma=False,
    )
```

```python
import math

import jax
import jax.numpy as jnp
import numpy as np
from jax import lax
from jax.experimental import pallas as pl
from jax.experimental.pallas import tpu as pltpu
from jax.sharding import PartitionSpec as P

MODEL_WIDTH = 8192
HEAD_SIZE = 128


rope_theta = 500000.0
penalty_step = 1.5
norm_eps = 1e-05


def swap(value, axis, distance):
    if distance == 0:
        return value
    pairs = [(source, source ^ distance) for source in range(lax.axis_size(axis))]
    return lax.ppermute(value, axis, pairs)


def far_first(axis):
    return range(lax.axis_size(axis) - 1, -1, -1)


def gather_swapped(value, axis):
    return [swap(value, axis, distance) for distance in far_first(axis)]


def sum_totals(value, axes):
    count = lax.axis_size(axes)
    copies = jnp.broadcast_to(value[None], (count,) + value.shape)
    return jnp.sum(lax.all_to_all(copies, axes, 0, 0, tiled=True), 0)


def matmul_kernel(row_blocks, *refs):
    blocks, weights, out_ref = refs[:row_blocks], refs[row_blocks:-1], refs[-1]
    rows = jnp.concatenate([block[...] for block in blocks], axis=0)
    first = 0
    for weight in weights:
        last = first + weight.shape[1]
        product = jnp.dot(rows, weight[...], preferred_element_type=jnp.float32)
        out_ref[:, first:last] = product.astype(out_ref.dtype)
        first = last


def matmul(blocks, weights, dtype):
    rows = sum(block.shape[0] for block in blocks)
    cols = sum(weight.shape[1] for weight in weights)
    depth = weights[0].shape[0]
    whole = pl.BlockSpec(memory_space=pltpu.VMEM)
    return pl.pallas_call(
        lambda *refs: matmul_kernel(len(blocks), *refs),
        out_shape=jax.ShapeDtypeStruct((rows, cols), dtype),
        in_specs=[whole] * (len(blocks) + len(weights)),
        out_specs=whole,
        compiler_params=pltpu.CompilerParams(vmem_limit_bytes=8 * 1024 * 1024),
        cost_estimate=pl.CostEstimate(
            flops=2 * rows * cols * depth,
            bytes_accessed=2 * (depth * (rows + cols) + rows * cols),
            transcendentals=0,
        ),
    )(*blocks, *[pltpu.with_memory_space_constraint(weight, pltpu.VMEM) for weight in weights])


def head_kernel(places_ref, *refs):
    blocks, (weight_ref, penalty_ref, out_ref) = refs[:-3], refs[-3:]
    rows = jnp.concatenate([block[...] for block in blocks], axis=0)
    logits = jnp.dot(rows, weight_ref[...], preferred_element_type=jnp.float32)
    share = blocks[0].shape[0]
    for i in range(len(blocks)):
        place = pl.ds(pl.multiple_of(places_ref[i], 8), share)
        out_ref[place, :] = logits[i * share : (i + 1) * share] - penalty_ref[place, :]


def head(places, blocks, weight, penalty):
    whole = pl.BlockSpec(memory_space=pltpu.VMEM)
    rows, cols = penalty.shape
    depth = weight.shape[0]
    return pl.pallas_call(
        head_kernel,
        out_shape=jax.ShapeDtypeStruct((rows, cols), jnp.float32),
        in_specs=[pl.BlockSpec(memory_space=pltpu.SMEM)] + [whole] * (len(blocks) + 2),
        out_specs=whole,
        compiler_params=pltpu.CompilerParams(vmem_limit_bytes=8 * 1024 * 1024),
        cost_estimate=pl.CostEstimate(
            flops=2 * rows * cols * depth,
            bytes_accessed=2 * depth * (rows + cols) + 8 * rows * cols,
            transcendentals=0,
        ),
    )(places, *blocks, pltpu.with_memory_space_constraint(weight, pltpu.VMEM), penalty)


def load_kernel(weight_ref, out_ref, sems):
    pieces = sems.shape[0]
    rows = out_ref.shape[0] // pieces
    copies = []
    for piece in range(pieces):
        part = pl.ds(piece * rows, rows)
        copy = pltpu.make_async_copy(weight_ref.at[part], out_ref.at[part], sems.at[piece])
        copy.start()
        copies.append(copy)
    for copy in copies:
        copy.wait()


def load_to_vmem(weight):
    return pl.pallas_call(
        load_kernel,
        out_shape=pltpu.VMEM(weight.shape, weight.dtype),
        in_specs=[pl.BlockSpec(memory_space=pltpu.HBM)],
        out_specs=pl.BlockSpec(memory_space=pltpu.VMEM),
        scratch_shapes=[pltpu.SemaphoreType.DMA((4,))],
        compiler_params=pltpu.CompilerParams(vmem_limit_bytes=8 * 1024 * 1024),
        cost_estimate=pl.CostEstimate(
            flops=0, bytes_accessed=4 * weight.size, transcendentals=0
        ),
    )(pltpu.with_memory_space_constraint(weight, pltpu.HBM))


def load_in_turn(weight, stream, turn, held=None):
    def kernel(stream_ref, weight_ref, *refs):
        out_ref, sems = refs[-2:]

        @pl.when(stream_ref[0] == turn)
        def _():
            load_kernel(weight_ref, out_ref, sems)

    operands = [stream.reshape(1), pltpu.with_memory_space_constraint(weight, pltpu.HBM)]
    specs = [pl.BlockSpec(memory_space=pltpu.SMEM), pl.BlockSpec(memory_space=pltpu.HBM)]
    if held is not None:
        operands.append(pltpu.with_memory_space_constraint(held, pltpu.VMEM))
        specs.append(pl.BlockSpec(memory_space=pltpu.VMEM))
    return pl.pallas_call(
        kernel,
        out_shape=pltpu.VMEM(weight.shape, weight.dtype),
        in_specs=specs,
        out_specs=pl.BlockSpec(memory_space=pltpu.VMEM),
        scratch_shapes=[pltpu.SemaphoreType.DMA((4,))],
        input_output_aliases={} if held is None else {2: 0},
        compiler_params=pltpu.CompilerParams(vmem_limit_bytes=8 * 1024 * 1024),
        cost_estimate=pl.CostEstimate(
            flops=0, bytes_accessed=4 * weight.size, transcendentals=0
        ),
    )(*operands)


def load_projections_kernel(query_ref, pair_ref, query_out, pair_out, pair_raw, sems):
    pieces = sems.shape[0] - 1
    depth, members, cols = pair_raw.shape
    rows = depth // pieces
    step = math.gcd(rows, 256)
    copies = []
    for piece in range(pieces):
        part = pl.ds(piece * rows, rows)
        copy = pltpu.make_async_copy(pair_ref.at[part], pair_raw.at[part], sems.at[piece])
        copy.start()
        copies.append(copy)
    query_copy = pltpu.make_async_copy(query_ref, query_out, sems.at[pieces])
    query_copy.start()
    for piece in range(pieces):
        copies[piece].wait()

        def relayout(index, carry, first=piece * rows):
            part = pl.ds(pl.multiple_of(first + index * step, step), step)
            for member in range(members):
                pair_out[part, member * cols : (member + 1) * cols] = pair_raw[part, member, :]
            return carry

        lax.fori_loop(0, rows // step, relayout, 0)
    query_copy.wait()


def load_projections(query, pair):
    depth, members, cols = pair.shape
    arrays = [pltpu.with_memory_space_constraint(array, pltpu.HBM) for array in (query, pair)]
    return pl.pallas_call(
        load_projections_kernel,
        out_shape=(
            pltpu.VMEM(query.shape, query.dtype),
            pltpu.VMEM((depth, members * cols), pair.dtype),
        ),
        in_specs=[pl.BlockSpec(memory_space=pltpu.HBM)] * 2,
        out_specs=[pl.BlockSpec(memory_space=pltpu.VMEM)] * 2,
        scratch_shapes=[pltpu.VMEM(pair.shape, pair.dtype), pltpu.SemaphoreType.DMA((5,))],
        compiler_params=pltpu.CompilerParams(vmem_limit_bytes=16 * 1024 * 1024),
        cost_estimate=pl.CostEstimate(
            flops=0, bytes_accessed=4 * (query.size + pair.size), transcendentals=0
        ),
    )(*arrays)


def rotation(positions):
    halfway = HEAD_SIZE // 2
    frequency = np.asarray(rope_theta ** (-np.arange(halfway) * 2.0 / HEAD_SIZE), np.float32)
    angles = positions.astype(jnp.float32)[:, None, None] * frequency
    return jnp.cos(angles), jnp.sin(angles)


def rotate(values, cosine_term, sine_term):
    halfway = values.shape[-1] // 2
    first_half = values[..., :halfway]
    second_half = values[..., halfway:]
    return jnp.concatenate(
        [
            first_half * cosine_term - second_half * sine_term,
            second_half * cosine_term + first_half * sine_term,
        ],
        axis=-1,
    )


def repeat_counts(recent_ids, first_column, width):
    columns = first_column + jnp.arange(width, dtype=jnp.int32)
    return jnp.sum((recent_ids[:, :, None] == columns[None, None, :]).astype(jnp.float32), 1)


def body(
    hidden,
    cached_rotated_keys,
    cached_values,
    cache_lengths,
    recent_ids,
    guidance,
    w_query,
    key_value_weight,
    w_output,
    norm_gain,
    w_head,
):
    streams, dps, tensors = (lax.axis_size(axis) for axis in ("stream", "dp", "tensor"))
    stream, dp, tensor = (lax.axis_index(axis) for axis in ("stream", "dp", "tensor"))
    local_width = hidden.shape[2]
    query_cols = w_query.shape[1]
    kv_cols = key_value_weight.shape[2]
    local_prompts = cache_lengths.shape[1]
    hidden_prompts = hidden.shape[1]
    prompts = recent_ids.shape[0]
    lengths = cache_lengths[0]
    vocab_local = w_head.shape[1]

    hidden_blocks = gather_swapped(hidden[0], "tensor")
    all_rows = jnp.concatenate(hidden_blocks, axis=0)
    w_query, key_value_weight, stream, dp, tensor = lax.optimization_barrier(
        (w_query, key_value_weight, stream, dp, tensor)
    )
    projected_parts = matmul(
        hidden_blocks, load_projections(w_query, key_value_weight), jnp.bfloat16
    )
    (projected_parts, lengths, recent_ids, guidance, norm_gain, stream, dp, tensor) = (
        lax.optimization_barrier(
            (projected_parts, lengths, recent_ids, guidance, norm_gain, stream, dp, tensor)
        )
    )
    column_base = (dp * tensors + tensor) * vocab_local
    cosine_term, sine_term = rotation(lengths)

    def hidden_place(prompt):
        block = prompt // hidden_prompts
        return (tensors - 1 - (tensor ^ block)) * hidden_prompts + prompt % hidden_prompts

    gain_rows = norm_gain.reshape(local_prompts, -1)
    total_cols = query_cols + 2 * kv_cols
    projected, gain_blocks = 0.0, []
    for distance in far_first("dp"):
        sending = lax.dynamic_slice_in_dim(
            projected_parts, hidden_place((dp ^ distance) * local_prompts), local_prompts, 0
        )
        arrived = swap(jnp.concatenate([sending, gain_rows], axis=1), "dp", distance)
        projected = projected + arrived[:, :total_cols].astype(jnp.float32)
        gain_blocks.append(arrived[:, total_cols:].reshape(local_width))
    gain = jnp.zeros((local_width * dps,), norm_gain.dtype)
    for distance, block in zip(far_first("dp"), gain_blocks):
        gain = lax.dynamic_update_slice_in_dim(gain, block, (dp ^ distance) * local_width, 0)

    query_heads = query_cols // HEAD_SIZE
    kv_heads = kv_cols // HEAD_SIZE
    rotated_query = rotate(
        projected[:, :query_cols].reshape(local_prompts, query_heads, HEAD_SIZE),
        cosine_term,
        sine_term,
    ).astype(jnp.bfloat16)
    key_value_rows = projected[:, query_cols:].reshape(local_prompts, 2, kv_heads, HEAD_SIZE)
    fresh_key = rotate(key_value_rows[:, 0], cosine_term, sine_term).astype(jnp.bfloat16)
    value_new = key_value_rows[:, 1].astype(jnp.bfloat16)
    grouped_queries = rotated_query.reshape(
        local_prompts, kv_heads, query_heads // kv_heads, HEAD_SIZE
    )
    attention_scale = HEAD_SIZE ** (-0.5)
    key_block = cached_rotated_keys[0]
    value_block = cached_values[0]
    scores = (
        jnp.einsum(
            "pkgd,pksd->pkgs", grouped_queries, key_block, preferred_element_type=jnp.float32
        )
        * attention_scale
    )
    self_score = (
        jnp.einsum("pkgd,pkd->pkg", grouped_queries, fresh_key, preferred_element_type=jnp.float32)
        * attention_scale
    )
    valid = jnp.arange(key_block.shape[2], dtype=jnp.int32)[None, :] < lengths[:, None]
    exps = jnp.where(valid[:, None, None, :], jnp.exp(scores), 0.0)
    own_exp = jnp.exp(self_score)
    denominator = jnp.sum(exps, -1) + own_exp
    weights = (exps / denominator[..., None]).astype(jnp.bfloat16)
    own_weight = (own_exp / denominator).astype(jnp.bfloat16)
    attended = jnp.einsum(
        "pkgs,pksd->pkgd", weights, value_block, preferred_element_type=jnp.float32
    )
    attended = (
        attended
        + own_weight.astype(jnp.float32)[..., None] * value_new.astype(jnp.float32)[:, :, None, :]
    )
    attended = attended.reshape(local_prompts, query_cols).astype(jnp.bfloat16)

    half = prompts // streams
    recent_mine = lax.dynamic_slice_in_dim(recent_ids, stream * half, half, 0)
    penalty = penalty_step * repeat_counts(recent_mine, column_base, vocab_local)
    attended, penalty = lax.optimization_barrier((attended, penalty))

    attended_blocks = gather_swapped(attended, "dp")
    w_output, _ = lax.optimization_barrier((w_output, attended))
    partial_out = matmul(attended_blocks, [load_to_vmem(w_output)], jnp.bfloat16)

    share = half // tensors

    def partial_rows(tensor_to):
        parts = []
        for other in range(streams):
            prompt = (stream ^ other) * half + tensor_to * share
            block = dps - 1 - (dp ^ (prompt // local_prompts))
            place = block * local_prompts + prompt % local_prompts
            parts.append(lax.dynamic_slice_in_dim(partial_out, place, share, 0))
        return jnp.concatenate(parts, axis=0)

    def hidden_rows(stream_to):
        place = hidden_place(stream_to * half + tensor * share)
        return lax.dynamic_slice_in_dim(all_rows, place, share, 0).astype(jnp.float32)

    summed = jnp.concatenate([hidden_rows(stream ^ other) for other in range(streams)], axis=0)
    for distance in far_first("tensor"):
        arrived = swap(partial_rows(tensor ^ distance), "tensor", distance)
        summed = summed + arrived.astype(jnp.float32)
    residuals = summed.astype(jnp.bfloat16).reshape(streams, share, local_width)
    pair = [swap(residuals[other], "stream", other) for other in range(streams)]
    pair = jnp.concatenate(pair, axis=0)

    whole = jnp.zeros((streams * share, local_width * dps), jnp.bfloat16)
    for distance, block in zip(far_first("dp"), gather_swapped(pair, "dp")):
        whole = lax.dynamic_update_slice_in_dim(whole, block, (dp ^ distance) * local_width, 1)
    whole = whole.reshape(streams, share, -1).astype(jnp.float32)
    inverse = lax.rsqrt(jnp.sum(whole * whole, 2) / MODEL_WIDTH + norm_eps)
    guide = lax.dynamic_slice_in_dim(guidance, stream * half + tensor * share, share, 0)
    own_guide = jnp.where(stream == 0, guide, 1.0 - guide)
    factors = inverse * jnp.stack([own_guide, 1.0 - own_guide])
    mixed = jnp.sum(whole * factors[:, :, None], 0) * gain.astype(jnp.float32)
    mixed = mixed.astype(jnp.bfloat16)

    places = jnp.stack([(tensor ^ distance) * share for distance in range(tensors)])
    w_head, mixed, places = lax.optimization_barrier((w_head, mixed, places))
    held = load_in_turn(w_head, stream, streams - 1)
    held, mixed = lax.optimization_barrier((held, mixed))
    mixed_blocks = [swap(mixed, "tensor", distance) for distance in range(tensors)]
    held = load_in_turn(w_head, stream, 0, held)
    guided = head(places.astype(jnp.int32), mixed_blocks, held, penalty)
    totals = sum_totals(jnp.sum(jnp.exp(guided), 1), ("dp", "tensor"))
    return guided - jnp.log(totals)[:, None]


def solution(mesh):
    return jax.shard_map(
        body,
        mesh=mesh,
        in_specs=(
            P("stream", "tensor", "dp"),
            P("stream", "dp", "tensor", None, None),
            P("stream", "dp", "tensor", None, None),
            P("stream", "dp"),
            P(),
            P(),
            P("dp", "tensor"),
            P("dp", None, "tensor"),
            P("tensor", "dp"),
            P("dp"),
            P(None, ("dp", "tensor")),
        ),
        out_specs=P("stream", ("dp", "tensor")),
        check_vma=False,
    )
```

```python
import math

import jax
import jax.numpy as jnp
import numpy as np
from jax import lax
from jax.experimental import pallas as pl
from jax.experimental.pallas import tpu as pltpu
from jax.sharding import PartitionSpec as P

MODEL_WIDTH = 8192
HEAD_SIZE = 128


rope_theta = 500000.0
penalty_step = 1.5
norm_eps = 1e-05


def swap(value, axis, distance):
    if distance == 0:
        return value
    pairs = [(source, source ^ distance) for source in range(lax.axis_size(axis))]
    return lax.ppermute(value, axis, pairs)


def far_first(axis):
    return range(lax.axis_size(axis) - 1, -1, -1)


def gather_swapped(value, axis):
    return [swap(value, axis, distance) for distance in far_first(axis)]


def sum_totals(value, axes):
    count = lax.axis_size(axes)
    copies = jnp.broadcast_to(value[None], (count,) + value.shape)
    return jnp.sum(lax.all_to_all(copies, axes, 0, 0, tiled=True), 0)


def matmul_kernel(row_blocks, *refs):
    blocks, weights, out_ref = refs[:row_blocks], refs[row_blocks:-1], refs[-1]
    rows = jnp.concatenate([block[...] for block in blocks], axis=0)
    first = 0
    for weight in weights:
        last = first + weight.shape[1]
        product = jnp.dot(rows, weight[...], preferred_element_type=jnp.float32)
        out_ref[:, first:last] = product.astype(out_ref.dtype)
        first = last


def matmul(blocks, weights, dtype):
    rows = sum(block.shape[0] for block in blocks)
    cols = sum(weight.shape[1] for weight in weights)
    depth = weights[0].shape[0]
    whole = pl.BlockSpec(memory_space=pltpu.VMEM)
    return pl.pallas_call(
        lambda *refs: matmul_kernel(len(blocks), *refs),
        out_shape=jax.ShapeDtypeStruct((rows, cols), dtype),
        in_specs=[whole] * (len(blocks) + len(weights)),
        out_specs=whole,
        compiler_params=pltpu.CompilerParams(vmem_limit_bytes=8 * 1024 * 1024),
        cost_estimate=pl.CostEstimate(
            flops=2 * rows * cols * depth,
            bytes_accessed=2 * (depth * (rows + cols) + rows * cols),
            transcendentals=0,
        ),
    )(*blocks, *[pltpu.with_memory_space_constraint(weight, pltpu.VMEM) for weight in weights])


def head_kernel(places_ref, *refs):
    blocks, (weight_ref, penalty_ref, out_ref) = refs[:-3], refs[-3:]
    rows = jnp.concatenate([block[...] for block in blocks], axis=0)
    logits = jnp.dot(rows, weight_ref[...], preferred_element_type=jnp.float32)
    share = blocks[0].shape[0]
    for i in range(len(blocks)):
        place = pl.ds(pl.multiple_of(places_ref[i], 8), share)
        out_ref[place, :] = logits[i * share : (i + 1) * share] - penalty_ref[place, :]


def head(places, blocks, weight, penalty):
    whole = pl.BlockSpec(memory_space=pltpu.VMEM)
    rows, cols = penalty.shape
    depth = weight.shape[0]
    return pl.pallas_call(
        head_kernel,
        out_shape=jax.ShapeDtypeStruct((rows, cols), jnp.float32),
        in_specs=[pl.BlockSpec(memory_space=pltpu.SMEM)] + [whole] * (len(blocks) + 2),
        out_specs=whole,
        compiler_params=pltpu.CompilerParams(vmem_limit_bytes=8 * 1024 * 1024),
        cost_estimate=pl.CostEstimate(
            flops=2 * rows * cols * depth,
            bytes_accessed=2 * depth * (rows + cols) + 8 * rows * cols,
            transcendentals=0,
        ),
    )(places, *blocks, pltpu.with_memory_space_constraint(weight, pltpu.VMEM), penalty)


def load_kernel(weight_ref, out_ref, sems):
    pieces = sems.shape[0]
    rows = out_ref.shape[0] // pieces
    copies = []
    for piece in range(pieces):
        part = pl.ds(piece * rows, rows)
        copy = pltpu.make_async_copy(weight_ref.at[part], out_ref.at[part], sems.at[piece])
        copy.start()
        copies.append(copy)
    for copy in copies:
        copy.wait()


def load_to_vmem(weight):
    return pl.pallas_call(
        load_kernel,
        out_shape=pltpu.VMEM(weight.shape, weight.dtype),
        in_specs=[pl.BlockSpec(memory_space=pltpu.HBM)],
        out_specs=pl.BlockSpec(memory_space=pltpu.VMEM),
        scratch_shapes=[pltpu.SemaphoreType.DMA((8,))],
        compiler_params=pltpu.CompilerParams(vmem_limit_bytes=8 * 1024 * 1024),
        cost_estimate=pl.CostEstimate(
            flops=0, bytes_accessed=4 * weight.size, transcendentals=0
        ),
    )(pltpu.with_memory_space_constraint(weight, pltpu.HBM))


def load_projections_kernel(query_ref, pair_ref, query_out, pair_out, pair_raw, sems):
    pieces = sems.shape[0] - 1
    depth, members, cols = pair_raw.shape
    rows = depth // pieces
    step = math.gcd(rows, 256)
    copies = []
    for piece in range(pieces):
        part = pl.ds(piece * rows, rows)
        copy = pltpu.make_async_copy(pair_ref.at[part], pair_raw.at[part], sems.at[piece])
        copy.start()
        copies.append(copy)
    query_copy = pltpu.make_async_copy(query_ref, query_out, sems.at[pieces])
    query_copy.start()
    for piece in range(pieces):
        copies[piece].wait()

        def relayout(index, carry, first=piece * rows):
            part = pl.ds(pl.multiple_of(first + index * step, step), step)
            both = pair_raw[part].astype(jnp.float32)
            for member in range(members):
                pair_out[part, member * cols : (member + 1) * cols] = both[:, member, :].astype(
                    pair_out.dtype
                )
            return carry

        lax.fori_loop(0, rows // step, relayout, 0)
    query_copy.wait()


def load_projections(query, pair):
    depth, members, cols = pair.shape
    arrays = [pltpu.with_memory_space_constraint(array, pltpu.HBM) for array in (query, pair)]
    return pl.pallas_call(
        load_projections_kernel,
        out_shape=(
            pltpu.VMEM(query.shape, query.dtype),
            pltpu.VMEM((depth, members * cols), pair.dtype),
        ),
        in_specs=[pl.BlockSpec(memory_space=pltpu.HBM)] * 2,
        out_specs=[pl.BlockSpec(memory_space=pltpu.VMEM)] * 2,
        scratch_shapes=[pltpu.VMEM(pair.shape, pair.dtype), pltpu.SemaphoreType.DMA((5,))],
        compiler_params=pltpu.CompilerParams(vmem_limit_bytes=16 * 1024 * 1024),
        cost_estimate=pl.CostEstimate(
            flops=0, bytes_accessed=4 * (query.size + pair.size), transcendentals=0
        ),
    )(*arrays)


def rotation(positions):
    halfway = HEAD_SIZE // 2
    frequency = np.asarray(rope_theta ** (-np.arange(halfway) * 2.0 / HEAD_SIZE), np.float32)
    angles = positions.astype(jnp.float32)[:, None, None] * frequency
    return jnp.cos(angles), jnp.sin(angles)


def rotate(values, cosine_term, sine_term):
    halfway = values.shape[-1] // 2
    first_half = values[..., :halfway]
    second_half = values[..., halfway:]
    return jnp.concatenate(
        [
            first_half * cosine_term - second_half * sine_term,
            second_half * cosine_term + first_half * sine_term,
        ],
        axis=-1,
    )


def repeat_counts(recent_ids, first_column, width):
    columns = first_column + jnp.arange(width, dtype=jnp.int32)
    return jnp.sum((recent_ids[:, :, None] == columns[None, None, :]).astype(jnp.float32), 1)


def body(
    hidden,
    cached_rotated_keys,
    cached_values,
    cache_lengths,
    recent_ids,
    guidance,
    w_query,
    key_value_weight,
    w_output,
    norm_gain,
    w_head,
):
    streams, dps, tensors = (lax.axis_size(axis) for axis in ("stream", "dp", "tensor"))
    stream, dp, tensor = (lax.axis_index(axis) for axis in ("stream", "dp", "tensor"))
    local_width = hidden.shape[2]
    query_cols = w_query.shape[1]
    kv_cols = key_value_weight.shape[2]
    local_prompts = cache_lengths.shape[1]
    hidden_prompts = hidden.shape[1]
    prompts = recent_ids.shape[0]
    lengths = cache_lengths[0]
    vocab_local = w_head.shape[1]

    hidden_blocks = gather_swapped(hidden[0], "tensor")
    all_rows = jnp.concatenate(hidden_blocks, axis=0)
    w_query, key_value_weight, stream, dp, tensor = lax.optimization_barrier(
        (w_query, key_value_weight, stream, dp, tensor)
    )
    projected_parts = matmul(
        hidden_blocks, load_projections(w_query, key_value_weight), jnp.bfloat16
    )
    (projected_parts, lengths, recent_ids, guidance, norm_gain, stream, dp, tensor) = (
        lax.optimization_barrier(
            (projected_parts, lengths, recent_ids, guidance, norm_gain, stream, dp, tensor)
        )
    )
    column_base = (dp * tensors + tensor) * vocab_local
    cosine_term, sine_term = rotation(lengths)

    def hidden_place(prompt):
        block = prompt // hidden_prompts
        return (tensors - 1 - (tensor ^ block)) * hidden_prompts + prompt % hidden_prompts

    gain_rows = norm_gain.reshape(local_prompts, -1)
    total_cols = query_cols + 2 * kv_cols
    projected, gain_blocks = 0.0, []
    for distance in far_first("dp"):
        sending = lax.dynamic_slice_in_dim(
            projected_parts, hidden_place((dp ^ distance) * local_prompts), local_prompts, 0
        )
        arrived = swap(jnp.concatenate([sending, gain_rows], axis=1), "dp", distance)
        projected = projected + arrived[:, :total_cols].astype(jnp.float32)
        gain_blocks.append(arrived[:, total_cols:].reshape(local_width))
    gain = jnp.zeros((local_width * dps,), norm_gain.dtype)
    for distance, block in zip(far_first("dp"), gain_blocks):
        gain = lax.dynamic_update_slice_in_dim(gain, block, (dp ^ distance) * local_width, 0)

    query_heads = query_cols // HEAD_SIZE
    kv_heads = kv_cols // HEAD_SIZE
    rotated_query = rotate(
        projected[:, :query_cols].reshape(local_prompts, query_heads, HEAD_SIZE),
        cosine_term,
        sine_term,
    ).astype(jnp.bfloat16)
    key_value_rows = projected[:, query_cols:].reshape(local_prompts, 2, kv_heads, HEAD_SIZE)
    fresh_key = rotate(key_value_rows[:, 0], cosine_term, sine_term).astype(jnp.bfloat16)
    value_new = key_value_rows[:, 1].astype(jnp.bfloat16)
    grouped_queries = rotated_query.reshape(
        local_prompts, kv_heads, query_heads // kv_heads, HEAD_SIZE
    )
    attention_scale = HEAD_SIZE ** (-0.5)
    key_block = cached_rotated_keys[0]
    value_block = cached_values[0]
    scores = (
        jnp.einsum(
            "pkgd,pksd->pkgs", grouped_queries, key_block, preferred_element_type=jnp.float32
        )
        * attention_scale
    )
    self_score = (
        jnp.einsum("pkgd,pkd->pkg", grouped_queries, fresh_key, preferred_element_type=jnp.float32)
        * attention_scale
    )
    valid = jnp.arange(key_block.shape[2], dtype=jnp.int32)[None, :] < lengths[:, None]
    exps = jnp.where(valid[:, None, None, :], jnp.exp(scores), 0.0)
    own_exp = jnp.exp(self_score)
    denominator = jnp.sum(exps, -1) + own_exp
    weights = (exps / denominator[..., None]).astype(jnp.bfloat16)
    own_weight = (own_exp / denominator).astype(jnp.bfloat16)
    attended = jnp.einsum(
        "pkgs,pksd->pkgd", weights, value_block, preferred_element_type=jnp.float32
    )
    attended = (
        attended
        + own_weight.astype(jnp.float32)[..., None] * value_new.astype(jnp.float32)[:, :, None, :]
    )
    attended = attended.reshape(local_prompts, query_cols).astype(jnp.bfloat16)

    half = prompts // streams
    recent_mine = lax.dynamic_slice_in_dim(recent_ids, stream * half, half, 0)
    penalty = penalty_step * repeat_counts(recent_mine, column_base, vocab_local)
    attended, penalty = lax.optimization_barrier((attended, penalty))

    attended_blocks = gather_swapped(attended, "dp")
    w_output, _ = lax.optimization_barrier((w_output, attended))
    partial_out = matmul(attended_blocks, [load_to_vmem(w_output)], jnp.bfloat16)

    share = half // tensors

    def partial_rows(tensor_to):
        parts = []
        for other in range(streams):
            prompt = (stream ^ other) * half + tensor_to * share
            block = dps - 1 - (dp ^ (prompt // local_prompts))
            place = block * local_prompts + prompt % local_prompts
            parts.append(lax.dynamic_slice_in_dim(partial_out, place, share, 0))
        return jnp.concatenate(parts, axis=0)

    def hidden_rows(stream_to):
        place = hidden_place(stream_to * half + tensor * share)
        return lax.dynamic_slice_in_dim(all_rows, place, share, 0).astype(jnp.float32)

    summed = jnp.concatenate([hidden_rows(stream ^ other) for other in range(streams)], axis=0)
    for distance in far_first("tensor"):
        arrived = swap(partial_rows(tensor ^ distance), "tensor", distance)
        summed = summed + arrived.astype(jnp.float32)
    residuals = summed.astype(jnp.bfloat16).reshape(streams, share, local_width)
    pair = [swap(residuals[other], "stream", other) for other in range(streams)]
    pair = jnp.concatenate(pair, axis=0)

    whole = jnp.zeros((streams * share, local_width * dps), jnp.bfloat16)
    for distance, block in zip(far_first("dp"), gather_swapped(pair, "dp")):
        whole = lax.dynamic_update_slice_in_dim(whole, block, (dp ^ distance) * local_width, 1)
    whole = whole.reshape(streams, share, -1).astype(jnp.float32)
    inverse = lax.rsqrt(jnp.sum(whole * whole, 2) / MODEL_WIDTH + norm_eps)
    guide = lax.dynamic_slice_in_dim(guidance, stream * half + tensor * share, share, 0)
    own_guide = jnp.where(stream == 0, guide, 1.0 - guide)
    factors = inverse * jnp.stack([own_guide, 1.0 - own_guide])
    mixed = jnp.sum(whole * factors[:, :, None], 0) * gain.astype(jnp.float32)
    mixed = mixed.astype(jnp.bfloat16)

    mixed_blocks = [swap(mixed, "tensor", distance) for distance in range(tensors)]
    w_head, _ = lax.optimization_barrier((w_head, mixed))
    places = jnp.stack([(tensor ^ distance) * share for distance in range(tensors)])
    guided = head(places.astype(jnp.int32), mixed_blocks, load_to_vmem(w_head), penalty)
    totals = sum_totals(jnp.sum(jnp.exp(guided), 1), ("dp", "tensor"))
    return guided - jnp.log(totals)[:, None]


def solution(mesh):
    return jax.shard_map(
        body,
        mesh=mesh,
        in_specs=(
            P("stream", "tensor", "dp"),
            P("stream", "dp", "tensor", None, None),
            P("stream", "dp", "tensor", None, None),
            P("stream", "dp"),
            P(),
            P(),
            P("dp", "tensor"),
            P("dp", None, "tensor"),
            P("tensor", "dp"),
            P("dp"),
            P(None, ("dp", "tensor")),
        ),
        out_specs=P("stream", ("dp", "tensor")),
        check_vma=False,
    )
```

```python
import math

import jax
import jax.numpy as jnp
import numpy as np
from jax import lax
from jax.experimental import pallas as pl
from jax.experimental.pallas import tpu as pltpu
from jax.sharding import PartitionSpec as P

MODEL_WIDTH = 8192
HEAD_SIZE = 128


rope_theta = 500000.0
penalty_step = 1.5
norm_eps = 1e-05


def swap(value, axis, distance):
    if distance == 0:
        return value
    pairs = [(source, source ^ distance) for source in range(lax.axis_size(axis))]
    return lax.ppermute(value, axis, pairs)


def far_first(axis):
    return range(lax.axis_size(axis) - 1, -1, -1)


def gather_swapped(value, axis):
    return [swap(value, axis, distance) for distance in far_first(axis)]


def sum_totals(value, axes):
    count = lax.axis_size(axes)
    copies = jnp.broadcast_to(value[None], (count,) + value.shape)
    return jnp.sum(lax.all_to_all(copies, axes, 0, 0, tiled=True), 0)


def matmul_kernel(row_blocks, *refs):
    blocks, weights, out_ref = refs[:row_blocks], refs[row_blocks:-1], refs[-1]
    rows = jnp.concatenate([block[...] for block in blocks], axis=0)
    first = 0
    for weight in weights:
        last = first + weight.shape[1]
        product = jnp.dot(rows, weight[...], preferred_element_type=jnp.float32)
        out_ref[:, first:last] = product.astype(out_ref.dtype)
        first = last


def matmul(blocks, weights, dtype):
    rows = sum(block.shape[0] for block in blocks)
    cols = sum(weight.shape[1] for weight in weights)
    depth = weights[0].shape[0]
    whole = pl.BlockSpec(memory_space=pltpu.VMEM)
    return pl.pallas_call(
        lambda *refs: matmul_kernel(len(blocks), *refs),
        out_shape=jax.ShapeDtypeStruct((rows, cols), dtype),
        in_specs=[whole] * (len(blocks) + len(weights)),
        out_specs=whole,
        compiler_params=pltpu.CompilerParams(vmem_limit_bytes=8 * 1024 * 1024),
        cost_estimate=pl.CostEstimate(
            flops=2 * rows * cols * depth,
            bytes_accessed=2 * (depth * (rows + cols) + rows * cols),
            transcendentals=0,
        ),
    )(*blocks, *[pltpu.with_memory_space_constraint(weight, pltpu.VMEM) for weight in weights])


def head_kernel(places_ref, *refs):
    blocks, (weight_ref, penalty_ref, out_ref) = refs[:-3], refs[-3:]
    rows = jnp.concatenate([block[...] for block in blocks], axis=0)
    logits = jnp.dot(rows, weight_ref[...], preferred_element_type=jnp.float32)
    share = blocks[0].shape[0]
    for i in range(len(blocks)):
        place = pl.ds(pl.multiple_of(places_ref[i], 8), share)
        out_ref[place, :] = logits[i * share : (i + 1) * share] - penalty_ref[place, :]


def head(places, blocks, weight, penalty):
    whole = pl.BlockSpec(memory_space=pltpu.VMEM)
    rows, cols = penalty.shape
    depth = weight.shape[0]
    return pl.pallas_call(
        head_kernel,
        out_shape=jax.ShapeDtypeStruct((rows, cols), jnp.float32),
        in_specs=[pl.BlockSpec(memory_space=pltpu.SMEM)] + [whole] * (len(blocks) + 2),
        out_specs=whole,
        compiler_params=pltpu.CompilerParams(vmem_limit_bytes=8 * 1024 * 1024),
        cost_estimate=pl.CostEstimate(
            flops=2 * rows * cols * depth,
            bytes_accessed=2 * depth * (rows + cols) + 8 * rows * cols,
            transcendentals=0,
        ),
    )(places, *blocks, pltpu.with_memory_space_constraint(weight, pltpu.VMEM), penalty)


def load_kernel(weight_ref, out_ref, sems):
    pieces = sems.shape[0]
    rows = out_ref.shape[0] // pieces
    copies = []
    for piece in range(pieces):
        part = pl.ds(piece * rows, rows)
        copy = pltpu.make_async_copy(weight_ref.at[part], out_ref.at[part], sems.at[piece])
        copy.start()
        copies.append(copy)
    for copy in copies:
        copy.wait()


def load_to_vmem(weight):
    return pl.pallas_call(
        load_kernel,
        out_shape=pltpu.VMEM(weight.shape, weight.dtype),
        in_specs=[pl.BlockSpec(memory_space=pltpu.HBM)],
        out_specs=pl.BlockSpec(memory_space=pltpu.VMEM),
        scratch_shapes=[pltpu.SemaphoreType.DMA((4,))],
        compiler_params=pltpu.CompilerParams(vmem_limit_bytes=8 * 1024 * 1024),
        cost_estimate=pl.CostEstimate(
            flops=0, bytes_accessed=4 * weight.size, transcendentals=0
        ),
    )(pltpu.with_memory_space_constraint(weight, pltpu.HBM))


LANES = 128


def load_projections_kernel(query_ref, pair_ref, query_out, pair_out, pair_raw, wide, sems):
    parts, depth, members, _ = pair_raw.shape
    cols = pair_ref.shape[2]
    step = wide.shape[0] // members
    copies = []
    for part in range(parts):
        lanes = pl.ds(part * LANES, LANES)
        copy = pltpu.make_async_copy(
            pair_ref.at[:, :, lanes], pair_raw.at[part], sems.at[part]
        )
        copy.start()
        copies.append(copy)
    query_copy = pltpu.make_async_copy(query_ref, query_out, sems.at[parts])
    query_copy.start()
    for part in range(parts):
        copies[part].wait()
        rows_in_turn = pair_raw.at[part].reshape(depth * members, LANES)

        def relayout(index, carry, rows_in_turn=rows_in_turn, part=part):
            source = pl.ds(pl.multiple_of(index * step * members, step * members), step * members)
            wide[...] = rows_in_turn[source, :].astype(jnp.float32)
            target = pl.ds(pl.multiple_of(index * step, step), step)
            for member in range(members):
                first = member * cols + part * LANES
                rows = wide[pl.ds(member, step, stride=members), :]
                pair_out[target, first : first + LANES] = rows.astype(pair_out.dtype)
            return carry

        lax.fori_loop(0, depth // step, relayout, 0)
    query_copy.wait()


def load_projections(query, pair):
    depth, members, cols = pair.shape
    parts = cols // LANES
    step = math.gcd(depth, 256)
    arrays = [pltpu.with_memory_space_constraint(array, pltpu.HBM) for array in (query, pair)]
    return pl.pallas_call(
        load_projections_kernel,
        out_shape=(
            pltpu.VMEM(query.shape, query.dtype),
            pltpu.VMEM((depth, members * cols), pair.dtype),
        ),
        in_specs=[pl.BlockSpec(memory_space=pltpu.HBM)] * 2,
        out_specs=[pl.BlockSpec(memory_space=pltpu.VMEM)] * 2,
        scratch_shapes=[
            pltpu.VMEM((parts, depth, members, LANES), pair.dtype),
            pltpu.VMEM((step * members, LANES), jnp.float32),
            pltpu.SemaphoreType.DMA((parts + 1,)),
        ],
        compiler_params=pltpu.CompilerParams(vmem_limit_bytes=16 * 1024 * 1024),
        cost_estimate=pl.CostEstimate(
            flops=0, bytes_accessed=4 * (query.size + pair.size), transcendentals=0
        ),
    )(*arrays)


def rotation(positions):
    halfway = HEAD_SIZE // 2
    frequency = np.asarray(rope_theta ** (-np.arange(halfway) * 2.0 / HEAD_SIZE), np.float32)
    angles = positions.astype(jnp.float32)[:, None, None] * frequency
    return jnp.cos(angles), jnp.sin(angles)


def rotate(values, cosine_term, sine_term):
    halfway = values.shape[-1] // 2
    first_half = values[..., :halfway]
    second_half = values[..., halfway:]
    return jnp.concatenate(
        [
            first_half * cosine_term - second_half * sine_term,
            second_half * cosine_term + first_half * sine_term,
        ],
        axis=-1,
    )


def repeat_counts(recent_ids, first_column, width):
    columns = first_column + jnp.arange(width, dtype=jnp.int32)
    return jnp.sum((recent_ids[:, :, None] == columns[None, None, :]).astype(jnp.float32), 1)


def body(
    hidden,
    cached_rotated_keys,
    cached_values,
    cache_lengths,
    recent_ids,
    guidance,
    w_query,
    key_value_weight,
    w_output,
    norm_gain,
    w_head,
):
    streams, dps, tensors = (lax.axis_size(axis) for axis in ("stream", "dp", "tensor"))
    stream, dp, tensor = (lax.axis_index(axis) for axis in ("stream", "dp", "tensor"))
    local_width = hidden.shape[2]
    query_cols = w_query.shape[1]
    kv_cols = key_value_weight.shape[2]
    local_prompts = cache_lengths.shape[1]
    hidden_prompts = hidden.shape[1]
    prompts = recent_ids.shape[0]
    lengths = cache_lengths[0]
    vocab_local = w_head.shape[1]

    hidden_blocks = gather_swapped(hidden[0], "tensor")
    all_rows = jnp.concatenate(hidden_blocks, axis=0)
    w_query, key_value_weight, stream, dp, tensor = lax.optimization_barrier(
        (w_query, key_value_weight, stream, dp, tensor)
    )
    projected_parts = matmul(
        hidden_blocks, load_projections(w_query, key_value_weight), jnp.bfloat16
    )
    (projected_parts, lengths, recent_ids, guidance, norm_gain, stream, dp, tensor) = (
        lax.optimization_barrier(
            (projected_parts, lengths, recent_ids, guidance, norm_gain, stream, dp, tensor)
        )
    )
    column_base = (dp * tensors + tensor) * vocab_local
    cosine_term, sine_term = rotation(lengths)

    def hidden_place(prompt):
        block = prompt // hidden_prompts
        return (tensors - 1 - (tensor ^ block)) * hidden_prompts + prompt % hidden_prompts

    gain_rows = norm_gain.reshape(local_prompts, -1)
    total_cols = query_cols + 2 * kv_cols
    projected, gain_blocks = 0.0, []
    for distance in far_first("dp"):
        sending = lax.dynamic_slice_in_dim(
            projected_parts, hidden_place((dp ^ distance) * local_prompts), local_prompts, 0
        )
        arrived = swap(jnp.concatenate([sending, gain_rows], axis=1), "dp", distance)
        projected = projected + arrived[:, :total_cols].astype(jnp.float32)
        gain_blocks.append(arrived[:, total_cols:].reshape(local_width))
    gain = jnp.zeros((local_width * dps,), norm_gain.dtype)
    for distance, block in zip(far_first("dp"), gain_blocks):
        gain = lax.dynamic_update_slice_in_dim(gain, block, (dp ^ distance) * local_width, 0)

    query_heads = query_cols // HEAD_SIZE
    kv_heads = kv_cols // HEAD_SIZE
    rotated_query = rotate(
        projected[:, :query_cols].reshape(local_prompts, query_heads, HEAD_SIZE),
        cosine_term,
        sine_term,
    ).astype(jnp.bfloat16)
    key_value_rows = projected[:, query_cols:].reshape(local_prompts, 2, kv_heads, HEAD_SIZE)
    fresh_key = rotate(key_value_rows[:, 0], cosine_term, sine_term).astype(jnp.bfloat16)
    value_new = key_value_rows[:, 1].astype(jnp.bfloat16)
    grouped_queries = rotated_query.reshape(
        local_prompts, kv_heads, query_heads // kv_heads, HEAD_SIZE
    )
    attention_scale = HEAD_SIZE ** (-0.5)
    key_block = cached_rotated_keys[0]
    value_block = cached_values[0]
    scores = (
        jnp.einsum(
            "pkgd,pksd->pkgs", grouped_queries, key_block, preferred_element_type=jnp.float32
        )
        * attention_scale
    )
    self_score = (
        jnp.einsum("pkgd,pkd->pkg", grouped_queries, fresh_key, preferred_element_type=jnp.float32)
        * attention_scale
    )
    valid = jnp.arange(key_block.shape[2], dtype=jnp.int32)[None, :] < lengths[:, None]
    exps = jnp.where(valid[:, None, None, :], jnp.exp(scores), 0.0)
    own_exp = jnp.exp(self_score)
    denominator = jnp.sum(exps, -1) + own_exp
    weights = (exps / denominator[..., None]).astype(jnp.bfloat16)
    own_weight = (own_exp / denominator).astype(jnp.bfloat16)
    attended = jnp.einsum(
        "pkgs,pksd->pkgd", weights, value_block, preferred_element_type=jnp.float32
    )
    attended = (
        attended
        + own_weight.astype(jnp.float32)[..., None] * value_new.astype(jnp.float32)[:, :, None, :]
    )
    attended = attended.reshape(local_prompts, query_cols).astype(jnp.bfloat16)

    half = prompts // streams
    recent_mine = lax.dynamic_slice_in_dim(recent_ids, stream * half, half, 0)
    penalty = penalty_step * repeat_counts(recent_mine, column_base, vocab_local)
    attended, penalty = lax.optimization_barrier((attended, penalty))

    attended_blocks = gather_swapped(attended, "dp")
    w_output, _ = lax.optimization_barrier((w_output, attended))
    partial_out = matmul(attended_blocks, [load_to_vmem(w_output)], jnp.bfloat16)

    share = half // tensors

    def partial_rows(tensor_to):
        parts = []
        for other in range(streams):
            prompt = (stream ^ other) * half + tensor_to * share
            block = dps - 1 - (dp ^ (prompt // local_prompts))
            place = block * local_prompts + prompt % local_prompts
            parts.append(lax.dynamic_slice_in_dim(partial_out, place, share, 0))
        return jnp.concatenate(parts, axis=0)

    def hidden_rows(stream_to):
        place = hidden_place(stream_to * half + tensor * share)
        return lax.dynamic_slice_in_dim(all_rows, place, share, 0).astype(jnp.float32)

    summed = jnp.concatenate([hidden_rows(stream ^ other) for other in range(streams)], axis=0)
    for distance in far_first("tensor"):
        arrived = swap(partial_rows(tensor ^ distance), "tensor", distance)
        summed = summed + arrived.astype(jnp.float32)
    residuals = summed.astype(jnp.bfloat16).reshape(streams, share, local_width)
    pair = [swap(residuals[other], "stream", other) for other in range(streams)]
    pair = jnp.concatenate(pair, axis=0)

    whole = jnp.zeros((streams * share, local_width * dps), jnp.bfloat16)
    for distance, block in zip(far_first("dp"), gather_swapped(pair, "dp")):
        whole = lax.dynamic_update_slice_in_dim(whole, block, (dp ^ distance) * local_width, 1)
    whole = whole.reshape(streams, share, -1).astype(jnp.float32)
    inverse = lax.rsqrt(jnp.sum(whole * whole, 2) / MODEL_WIDTH + norm_eps)
    guide = lax.dynamic_slice_in_dim(guidance, stream * half + tensor * share, share, 0)
    own_guide = jnp.where(stream == 0, guide, 1.0 - guide)
    factors = inverse * jnp.stack([own_guide, 1.0 - own_guide])
    mixed = jnp.sum(whole * factors[:, :, None], 0) * gain.astype(jnp.float32)
    mixed = mixed.astype(jnp.bfloat16)

    mixed_blocks = [swap(mixed, "tensor", distance) for distance in range(tensors)]
    w_head, _ = lax.optimization_barrier((w_head, mixed))
    places = jnp.stack([(tensor ^ distance) * share for distance in range(tensors)])
    guided = head(places.astype(jnp.int32), mixed_blocks, load_to_vmem(w_head), penalty)
    totals = sum_totals(jnp.sum(jnp.exp(guided), 1), ("dp", "tensor"))
    return guided - jnp.log(totals)[:, None]


def solution(mesh):
    return jax.shard_map(
        body,
        mesh=mesh,
        in_specs=(
            P("stream", "tensor", "dp"),
            P("stream", "dp", "tensor", None, None),
            P("stream", "dp", "tensor", None, None),
            P("stream", "dp"),
            P(),
            P(),
            P("dp", "tensor"),
            P("dp", None, "tensor"),
            P("tensor", "dp"),
            P("dp"),
            P(None, ("dp", "tensor")),
        ),
        out_specs=P("stream", ("dp", "tensor")),
        check_vma=False,
    )
```

```python
import math

import jax
import jax.numpy as jnp
import numpy as np
from jax import lax
from jax.experimental import pallas as pl
from jax.experimental.pallas import tpu as pltpu
from jax.sharding import PartitionSpec as P

MODEL_WIDTH = 8192
HEAD_SIZE = 128


rope_theta = 500000.0
penalty_step = 1.5
norm_eps = 1e-05


def swap(value, axis, distance):
    if distance == 0:
        return value
    pairs = [(source, source ^ distance) for source in range(lax.axis_size(axis))]
    return lax.ppermute(value, axis, pairs)


def far_first(axis):
    return range(lax.axis_size(axis) - 1, -1, -1)


def gather_swapped(value, axis):
    return [swap(value, axis, distance) for distance in far_first(axis)]


def sum_totals(value, axes):
    count = lax.axis_size(axes)
    copies = jnp.broadcast_to(value[None], (count,) + value.shape)
    return jnp.sum(lax.all_to_all(copies, axes, 0, 0, tiled=True), 0)


def matmul_kernel(row_blocks, *refs):
    blocks, weights, out_ref = refs[:row_blocks], refs[row_blocks:-1], refs[-1]
    rows = jnp.concatenate([block[...] for block in blocks], axis=0)
    first = 0
    for weight in weights:
        last = first + weight.shape[1]
        product = jnp.dot(rows, weight[...], preferred_element_type=jnp.float32)
        out_ref[:, first:last] = product.astype(out_ref.dtype)
        first = last


def matmul(blocks, weights, dtype):
    rows = sum(block.shape[0] for block in blocks)
    cols = sum(weight.shape[1] for weight in weights)
    depth = weights[0].shape[0]
    whole = pl.BlockSpec(memory_space=pltpu.VMEM)
    return pl.pallas_call(
        lambda *refs: matmul_kernel(len(blocks), *refs),
        out_shape=jax.ShapeDtypeStruct((rows, cols), dtype),
        in_specs=[whole] * (len(blocks) + len(weights)),
        out_specs=whole,
        compiler_params=pltpu.CompilerParams(vmem_limit_bytes=8 * 1024 * 1024),
        cost_estimate=pl.CostEstimate(
            flops=2 * rows * cols * depth,
            bytes_accessed=2 * (depth * (rows + cols) + rows * cols),
            transcendentals=0,
        ),
    )(*blocks, *[pltpu.with_memory_space_constraint(weight, pltpu.VMEM) for weight in weights])


def head_kernel(rows_ref, cols_ref, factor_ref, gain_ref, *refs):
    weight_ref, penalty_ref, out_ref, early, late = refs[-5:]
    tensors, dps = rows_ref.shape[0], cols_ref.shape[0]
    mixed, raw = refs[:tensors], refs[tensors : tensors + dps]
    part = mixed[0].shape[0]
    width = raw[0].shape[1]
    for i in range(tensors):
        early[i * part : (i + 1) * part, :] = mixed[i][...].astype(jnp.float32)
    for i in range(dps):
        late[:, pl.ds(pl.multiple_of(cols_ref[i], LANES), width)] = raw[i][...].astype(
            jnp.float32
        )
    values = late[...]
    squares = jnp.sum(values * values, axis=1, keepdims=True)
    values = values * (lax.rsqrt(squares / MODEL_WIDTH + norm_eps) * factor_ref[...])
    half = tensors * part
    second = (values[:half] + values[half:]) * gain_ref[...]
    rows = jnp.concatenate([early[...], second], axis=0).astype(weight_ref.dtype)
    logits = jnp.dot(rows, weight_ref[...], preferred_element_type=jnp.float32)
    for i in range(tensors):
        place = pl.ds(pl.multiple_of(rows_ref[i], 8), 2 * part)
        other = half + (tensors - 1 - i) * part
        both = jnp.concatenate(
            [logits[i * part : (i + 1) * part], logits[other : other + part]], axis=0
        )
        out_ref[place, :] = both - penalty_ref[place, :]


def head(row_places, col_places, factor, gain, mixed, raw, weight, penalty):
    whole = pl.BlockSpec(memory_space=pltpu.VMEM)
    places = pl.BlockSpec(memory_space=pltpu.SMEM)
    rows, cols = penalty.shape
    depth = weight.shape[0]
    return pl.pallas_call(
        head_kernel,
        out_shape=jax.ShapeDtypeStruct((rows, cols), jnp.float32),
        in_specs=[places] * 2 + [whole] * (len(mixed) + len(raw) + 4),
        out_specs=whole,
        scratch_shapes=[
            pltpu.VMEM((rows // 2, depth), jnp.float32),
            pltpu.VMEM((rows, depth), jnp.float32),
        ],
        compiler_params=pltpu.CompilerParams(vmem_limit_bytes=24 * 1024 * 1024),
        cost_estimate=pl.CostEstimate(
            flops=2 * rows * cols * depth,
            bytes_accessed=2 * depth * (rows + cols) + 8 * rows * cols,
            transcendentals=0,
        ),
    )(
        row_places,
        col_places,
        factor,
        gain,
        *mixed,
        *raw,
        pltpu.with_memory_space_constraint(weight, pltpu.VMEM),
        penalty,
    )


def load_kernel(weight_ref, out_ref, sems):
    pieces = sems.shape[0]
    rows = out_ref.shape[0] // pieces
    copies = []
    for piece in range(pieces):
        part = pl.ds(piece * rows, rows)
        copy = pltpu.make_async_copy(weight_ref.at[part], out_ref.at[part], sems.at[piece])
        copy.start()
        copies.append(copy)
    for copy in copies:
        copy.wait()


def load_to_vmem(weight):
    return pl.pallas_call(
        load_kernel,
        out_shape=pltpu.VMEM(weight.shape, weight.dtype),
        in_specs=[pl.BlockSpec(memory_space=pltpu.HBM)],
        out_specs=pl.BlockSpec(memory_space=pltpu.VMEM),
        scratch_shapes=[pltpu.SemaphoreType.DMA((4,))],
        compiler_params=pltpu.CompilerParams(vmem_limit_bytes=8 * 1024 * 1024),
        cost_estimate=pl.CostEstimate(
            flops=0, bytes_accessed=4 * weight.size, transcendentals=0
        ),
    )(pltpu.with_memory_space_constraint(weight, pltpu.HBM))


LANES = 128


def load_projections_kernel(query_ref, pair_ref, query_out, pair_out, pair_raw, wide, sems):
    parts, depth, members, _ = pair_raw.shape
    cols = pair_ref.shape[2]
    step = wide.shape[0] // members
    copies = []
    for part in range(parts):
        lanes = pl.ds(part * LANES, LANES)
        copy = pltpu.make_async_copy(
            pair_ref.at[:, :, lanes], pair_raw.at[part], sems.at[part]
        )
        copy.start()
        copies.append(copy)
    query_copy = pltpu.make_async_copy(query_ref, query_out, sems.at[parts])
    query_copy.start()
    for part in range(parts):
        copies[part].wait()
        rows_in_turn = pair_raw.at[part].reshape(depth * members, LANES)

        def relayout(index, carry, rows_in_turn=rows_in_turn, part=part):
            source = pl.ds(pl.multiple_of(index * step * members, step * members), step * members)
            wide[...] = rows_in_turn[source, :].astype(jnp.float32)
            target = pl.ds(pl.multiple_of(index * step, step), step)
            for member in range(members):
                first = member * cols + part * LANES
                rows = wide[pl.ds(member, step, stride=members), :]
                pair_out[target, first : first + LANES] = rows.astype(pair_out.dtype)
            return carry

        lax.fori_loop(0, depth // step, relayout, 0)
    query_copy.wait()


def load_projections(query, pair):
    depth, members, cols = pair.shape
    parts = cols // LANES
    step = math.gcd(depth, 256)
    arrays = [pltpu.with_memory_space_constraint(array, pltpu.HBM) for array in (query, pair)]
    return pl.pallas_call(
        load_projections_kernel,
        out_shape=(
            pltpu.VMEM(query.shape, query.dtype),
            pltpu.VMEM((depth, members * cols), pair.dtype),
        ),
        in_specs=[pl.BlockSpec(memory_space=pltpu.HBM)] * 2,
        out_specs=[pl.BlockSpec(memory_space=pltpu.VMEM)] * 2,
        scratch_shapes=[
            pltpu.VMEM((parts, depth, members, LANES), pair.dtype),
            pltpu.VMEM((step * members, LANES), jnp.float32),
            pltpu.SemaphoreType.DMA((parts + 1,)),
        ],
        compiler_params=pltpu.CompilerParams(vmem_limit_bytes=16 * 1024 * 1024),
        cost_estimate=pl.CostEstimate(
            flops=0, bytes_accessed=4 * (query.size + pair.size), transcendentals=0
        ),
    )(*arrays)


def rotation(positions):
    halfway = HEAD_SIZE // 2
    frequency = np.asarray(rope_theta ** (-np.arange(halfway) * 2.0 / HEAD_SIZE), np.float32)
    angles = positions.astype(jnp.float32)[:, None, None] * frequency
    return jnp.cos(angles), jnp.sin(angles)


def rotate(values, cosine_term, sine_term):
    halfway = values.shape[-1] // 2
    first_half = values[..., :halfway]
    second_half = values[..., halfway:]
    return jnp.concatenate(
        [
            first_half * cosine_term - second_half * sine_term,
            second_half * cosine_term + first_half * sine_term,
        ],
        axis=-1,
    )


def repeat_counts(recent_ids, first_column, width):
    columns = first_column + jnp.arange(width, dtype=jnp.int32)
    return jnp.sum((recent_ids[:, :, None] == columns[None, None, :]).astype(jnp.float32), 1)


def body(
    hidden,
    cached_rotated_keys,
    cached_values,
    cache_lengths,
    recent_ids,
    guidance,
    w_query,
    key_value_weight,
    w_output,
    norm_gain,
    w_head,
):
    streams, dps, tensors = (lax.axis_size(axis) for axis in ("stream", "dp", "tensor"))
    stream, dp, tensor = (lax.axis_index(axis) for axis in ("stream", "dp", "tensor"))
    local_width = hidden.shape[2]
    query_cols = w_query.shape[1]
    kv_cols = key_value_weight.shape[2]
    local_prompts = cache_lengths.shape[1]
    hidden_prompts = hidden.shape[1]
    prompts = recent_ids.shape[0]
    lengths = cache_lengths[0]
    vocab_local = w_head.shape[1]

    hidden_blocks = gather_swapped(hidden[0], "tensor")
    all_rows = jnp.concatenate(hidden_blocks, axis=0)
    w_query, key_value_weight, stream, dp, tensor = lax.optimization_barrier(
        (w_query, key_value_weight, stream, dp, tensor)
    )
    projected_parts = matmul(
        hidden_blocks, load_projections(w_query, key_value_weight), jnp.bfloat16
    )
    (projected_parts, lengths, recent_ids, guidance, norm_gain, stream, dp, tensor) = (
        lax.optimization_barrier(
            (projected_parts, lengths, recent_ids, guidance, norm_gain, stream, dp, tensor)
        )
    )
    column_base = (dp * tensors + tensor) * vocab_local
    cosine_term, sine_term = rotation(lengths)

    def hidden_place(prompt):
        block = prompt // hidden_prompts
        return (tensors - 1 - (tensor ^ block)) * hidden_prompts + prompt % hidden_prompts

    gain_rows = norm_gain.reshape(local_prompts, -1)
    total_cols = query_cols + 2 * kv_cols
    projected, gain_blocks = 0.0, []
    for distance in far_first("dp"):
        sending = lax.dynamic_slice_in_dim(
            projected_parts, hidden_place((dp ^ distance) * local_prompts), local_prompts, 0
        )
        arrived = swap(jnp.concatenate([sending, gain_rows], axis=1), "dp", distance)
        projected = projected + arrived[:, :total_cols].astype(jnp.float32)
        gain_blocks.append(arrived[:, total_cols:].reshape(local_width))
    gain = jnp.zeros((local_width * dps,), norm_gain.dtype)
    for distance, block in zip(far_first("dp"), gain_blocks):
        gain = lax.dynamic_update_slice_in_dim(gain, block, (dp ^ distance) * local_width, 0)

    query_heads = query_cols // HEAD_SIZE
    kv_heads = kv_cols // HEAD_SIZE
    rotated_query = rotate(
        projected[:, :query_cols].reshape(local_prompts, query_heads, HEAD_SIZE),
        cosine_term,
        sine_term,
    ).astype(jnp.bfloat16)
    key_value_rows = projected[:, query_cols:].reshape(local_prompts, 2, kv_heads, HEAD_SIZE)
    fresh_key = rotate(key_value_rows[:, 0], cosine_term, sine_term).astype(jnp.bfloat16)
    value_new = key_value_rows[:, 1].astype(jnp.bfloat16)
    grouped_queries = rotated_query.reshape(
        local_prompts, kv_heads, query_heads // kv_heads, HEAD_SIZE
    )
    attention_scale = HEAD_SIZE ** (-0.5)
    key_block = cached_rotated_keys[0]
    value_block = cached_values[0]
    scores = (
        jnp.einsum(
            "pkgd,pksd->pkgs", grouped_queries, key_block, preferred_element_type=jnp.float32
        )
        * attention_scale
    )
    self_score = (
        jnp.einsum("pkgd,pkd->pkg", grouped_queries, fresh_key, preferred_element_type=jnp.float32)
        * attention_scale
    )
    valid = jnp.arange(key_block.shape[2], dtype=jnp.int32)[None, :] < lengths[:, None]
    exps = jnp.where(valid[:, None, None, :], jnp.exp(scores), 0.0)
    own_exp = jnp.exp(self_score)
    denominator = jnp.sum(exps, -1) + own_exp
    weights = (exps / denominator[..., None]).astype(jnp.bfloat16)
    own_weight = (own_exp / denominator).astype(jnp.bfloat16)
    attended = jnp.einsum(
        "pkgs,pksd->pkgd", weights, value_block, preferred_element_type=jnp.float32
    )
    attended = (
        attended
        + own_weight.astype(jnp.float32)[..., None] * value_new.astype(jnp.float32)[:, :, None, :]
    )
    attended = attended.reshape(local_prompts, query_cols).astype(jnp.bfloat16)

    half = prompts // streams
    recent_mine = lax.dynamic_slice_in_dim(recent_ids, stream * half, half, 0)
    penalty = penalty_step * repeat_counts(recent_mine, column_base, vocab_local)
    attended, penalty = lax.optimization_barrier((attended, penalty))

    attended_blocks = gather_swapped(attended, "dp")
    w_output, _ = lax.optimization_barrier((w_output, attended))
    partial_out = matmul(attended_blocks, [load_to_vmem(w_output)], jnp.bfloat16)

    share = half // tensors

    def partial_rows(tensor_to):
        parts = []
        for other in range(streams):
            prompt = (stream ^ other) * half + tensor_to * share
            block = dps - 1 - (dp ^ (prompt // local_prompts))
            place = block * local_prompts + prompt % local_prompts
            parts.append(lax.dynamic_slice_in_dim(partial_out, place, share, 0))
        return jnp.concatenate(parts, axis=0)

    def hidden_rows(stream_to):
        place = hidden_place(stream_to * half + tensor * share)
        return lax.dynamic_slice_in_dim(all_rows, place, share, 0).astype(jnp.float32)

    summed = jnp.concatenate([hidden_rows(stream ^ other) for other in range(streams)], axis=0)
    for distance in far_first("tensor"):
        arrived = swap(partial_rows(tensor ^ distance), "tensor", distance)
        summed = summed + arrived.astype(jnp.float32)
    residuals = summed.astype(jnp.bfloat16).reshape(streams, share, local_width)
    pair = [swap(residuals[other], "stream", other) for other in range(streams)]
    pair = jnp.concatenate(pair, axis=0)

    part = share // 2
    group = [
        jnp.concatenate([pair[at : at + part], pair[share + at : share + at + part]], axis=0)
        for at in (0, part)
    ]
    second_blocks = gather_swapped(group[1], "tensor")
    first_blocks = gather_swapped(group[0], "dp")
    guide = lax.dynamic_slice_in_dim(guidance, stream * half, half, 0)
    own_guide = jnp.where(stream == 0, guide, 1.0 - guide)

    def own_factors(tensor_of, at):
        return lax.dynamic_slice_in_dim(own_guide, tensor_of * share + at, part, 0)

    whole = jnp.zeros((streams * part, local_width * dps), jnp.bfloat16)
    for distance, block in zip(far_first("dp"), first_blocks):
        whole = lax.dynamic_update_slice_in_dim(whole, block, (dp ^ distance) * local_width, 1)
    whole = whole.reshape(streams, part, -1).astype(jnp.float32)
    inverse = lax.rsqrt(jnp.sum(whole * whole, 2) / MODEL_WIDTH + norm_eps)
    first_factor = own_factors(tensor, 0)
    factors = inverse * jnp.stack([first_factor, 1.0 - first_factor])
    gain = gain.astype(jnp.float32)
    mixed = jnp.sum(whole * factors[:, :, None], 0) * gain
    mixed = mixed.astype(jnp.bfloat16)

    second_rows = jnp.concatenate(
        [block[:part] for block in second_blocks] + [block[part:] for block in second_blocks],
        axis=0,
    )
    second_factor = jnp.concatenate(
        [own_factors(tensor ^ distance, part) for distance in far_first("tensor")]
    )
    second_factor = jnp.concatenate([second_factor, 1.0 - second_factor])[:, None]
    row_places = jnp.stack([(tensor ^ distance) * share for distance in range(tensors)])
    col_places = jnp.stack([(dp ^ distance) * local_width for distance in far_first("dp")])
    gain = gain[None]
    w_head, mixed, second_rows, second_factor, row_places, col_places, gain = (
        lax.optimization_barrier(
            (w_head, mixed, second_rows, second_factor, row_places, col_places, gain)
        )
    )
    mixed_blocks = [swap(mixed, "tensor", distance) for distance in range(tensors)]
    raw_blocks = gather_swapped(second_rows, "dp")
    guided = head(
        row_places,
        col_places,
        second_factor,
        gain,
        mixed_blocks,
        raw_blocks,
        load_to_vmem(w_head),
        penalty,
    )
    totals = sum_totals(jnp.sum(jnp.exp(guided), 1), ("dp", "tensor"))
    return guided - jnp.log(totals)[:, None]


def solution(mesh):
    return jax.shard_map(
        body,
        mesh=mesh,
        in_specs=(
            P("stream", "tensor", "dp"),
            P("stream", "dp", "tensor", None, None),
            P("stream", "dp", "tensor", None, None),
            P("stream", "dp"),
            P(),
            P(),
            P("dp", "tensor"),
            P("dp", None, "tensor"),
            P("tensor", "dp"),
            P("dp"),
            P(None, ("dp", "tensor")),
        ),
        out_specs=P("stream", ("dp", "tensor")),
        check_vma=False,
    )
```

```python
import math

import jax
import jax.numpy as jnp
import numpy as np
from jax import lax
from jax.experimental import pallas as pl
from jax.experimental.pallas import tpu as pltpu
from jax.sharding import PartitionSpec as P

MODEL_WIDTH = 8192
HEAD_SIZE = 128


rope_theta = 500000.0
penalty_step = 1.5
norm_eps = 1e-05


def swap(value, axis, distance):
    if distance == 0:
        return value
    pairs = [(source, source ^ distance) for source in range(lax.axis_size(axis))]
    return lax.ppermute(value, axis, pairs)


def far_first(axis):
    return range(lax.axis_size(axis) - 1, -1, -1)


def gather_swapped(value, axis):
    return [swap(value, axis, distance) for distance in far_first(axis)]


def sum_totals(value, axes):
    count = lax.axis_size(axes)
    copies = jnp.broadcast_to(value[None], (count,) + value.shape)
    return jnp.sum(lax.all_to_all(copies, axes, 0, 0, tiled=True), 0)


def matmul_kernel(row_blocks, *refs):
    blocks, weights, out_ref = refs[:row_blocks], refs[row_blocks:-1], refs[-1]
    rows = jnp.concatenate([block[...] for block in blocks], axis=0)
    first = 0
    for weight in weights:
        last = first + weight.shape[1]
        product = jnp.dot(rows, weight[...], preferred_element_type=jnp.float32)
        out_ref[:, first:last] = product.astype(out_ref.dtype)
        first = last


def matmul(blocks, weights, dtype):
    rows = sum(block.shape[0] for block in blocks)
    cols = sum(weight.shape[1] for weight in weights)
    depth = weights[0].shape[0]
    whole = pl.BlockSpec(memory_space=pltpu.VMEM)
    return pl.pallas_call(
        lambda *refs: matmul_kernel(len(blocks), *refs),
        out_shape=jax.ShapeDtypeStruct((rows, cols), dtype),
        in_specs=[whole] * (len(blocks) + len(weights)),
        out_specs=whole,
        compiler_params=pltpu.CompilerParams(vmem_limit_bytes=8 * 1024 * 1024),
        cost_estimate=pl.CostEstimate(
            flops=2 * rows * cols * depth,
            bytes_accessed=2 * (depth * (rows + cols) + rows * cols),
            transcendentals=0,
        ),
    )(*blocks, *[pltpu.with_memory_space_constraint(weight, pltpu.VMEM) for weight in weights])


def head_kernel(*refs):
    blocks, (weight_ref, penalty_ref, out_ref) = refs[:-3], refs[-3:]
    rows = jnp.concatenate([block[...] for block in blocks], axis=0)
    logits = jnp.dot(rows, weight_ref[...], preferred_element_type=jnp.float32)
    share = blocks[0].shape[0]
    tensor = lax.axis_index("tensor")
    for i in range(len(blocks)):
        place = pl.ds(pl.multiple_of((tensor ^ i) * share, 8), share)
        out_ref[place, :] = logits[i * share : (i + 1) * share] - penalty_ref[place, :]


def head(blocks, weight, penalty):
    whole = pl.BlockSpec(memory_space=pltpu.VMEM)
    rows, cols = penalty.shape
    depth = weight.shape[0]
    return pl.pallas_call(
        head_kernel,
        out_shape=jax.ShapeDtypeStruct((rows, cols), jnp.float32),
        in_specs=[whole] * (len(blocks) + 2),
        out_specs=whole,
        compiler_params=pltpu.CompilerParams(vmem_limit_bytes=8 * 1024 * 1024),
        cost_estimate=pl.CostEstimate(
            flops=2 * rows * cols * depth,
            bytes_accessed=2 * depth * (rows + cols) + 8 * rows * cols,
            transcendentals=0,
        ),
    )(*blocks, pltpu.with_memory_space_constraint(weight, pltpu.VMEM), penalty)


def load_kernel(weight_ref, out_ref, sems):
    pieces = sems.shape[0]
    rows = out_ref.shape[0] // pieces
    copies = []
    for piece in range(pieces):
        part = pl.ds(piece * rows, rows)
        copy = pltpu.make_async_copy(weight_ref.at[part], out_ref.at[part], sems.at[piece])
        copy.start()
        copies.append(copy)
    for copy in copies:
        copy.wait()


def load_to_vmem(weight):
    return pl.pallas_call(
        load_kernel,
        out_shape=pltpu.VMEM(weight.shape, weight.dtype),
        in_specs=[pl.BlockSpec(memory_space=pltpu.HBM)],
        out_specs=pl.BlockSpec(memory_space=pltpu.VMEM),
        scratch_shapes=[pltpu.SemaphoreType.DMA((4,))],
        compiler_params=pltpu.CompilerParams(vmem_limit_bytes=8 * 1024 * 1024),
        cost_estimate=pl.CostEstimate(
            flops=0, bytes_accessed=4 * weight.size, transcendentals=0
        ),
    )(pltpu.with_memory_space_constraint(weight, pltpu.HBM))


LANES = 128


def load_projections_kernel(query_ref, pair_ref, query_out, pair_out, pair_raw, wide, sems):
    parts, depth, members, _ = pair_raw.shape
    cols = pair_ref.shape[2]
    step = wide.shape[0] // members
    copies = []
    for part in range(parts):
        lanes = pl.ds(part * LANES, LANES)
        copy = pltpu.make_async_copy(
            pair_ref.at[:, :, lanes], pair_raw.at[part], sems.at[part]
        )
        copy.start()
        copies.append(copy)
    query_copy = pltpu.make_async_copy(query_ref, query_out, sems.at[parts])
    query_copy.start()
    for part in range(parts):
        copies[part].wait()
        rows_in_turn = pair_raw.at[part].reshape(depth * members, LANES)

        def relayout(index, carry, rows_in_turn=rows_in_turn, part=part):
            source = pl.ds(pl.multiple_of(index * step * members, step * members), step * members)
            wide[...] = rows_in_turn[source, :].astype(jnp.float32)
            target = pl.ds(pl.multiple_of(index * step, step), step)
            for member in range(members):
                first = member * cols + part * LANES
                rows = wide[pl.ds(member, step, stride=members), :]
                pair_out[target, first : first + LANES] = rows.astype(pair_out.dtype)
            return carry

        lax.fori_loop(0, depth // step, relayout, 0)
    query_copy.wait()


def load_projections(query, pair):
    depth, members, cols = pair.shape
    parts = cols // LANES
    step = math.gcd(depth, 256)
    arrays = [pltpu.with_memory_space_constraint(array, pltpu.HBM) for array in (query, pair)]
    return pl.pallas_call(
        load_projections_kernel,
        out_shape=(
            pltpu.VMEM(query.shape, query.dtype),
            pltpu.VMEM((depth, members * cols), pair.dtype),
        ),
        in_specs=[pl.BlockSpec(memory_space=pltpu.HBM)] * 2,
        out_specs=[pl.BlockSpec(memory_space=pltpu.VMEM)] * 2,
        scratch_shapes=[
            pltpu.VMEM((parts, depth, members, LANES), pair.dtype),
            pltpu.VMEM((step * members, LANES), jnp.float32),
            pltpu.SemaphoreType.DMA((parts + 1,)),
        ],
        compiler_params=pltpu.CompilerParams(vmem_limit_bytes=16 * 1024 * 1024),
        cost_estimate=pl.CostEstimate(
            flops=0, bytes_accessed=4 * (query.size + pair.size), transcendentals=0
        ),
    )(*arrays)


def rotation(positions):
    halfway = HEAD_SIZE // 2
    frequency = np.asarray(rope_theta ** (-np.arange(halfway) * 2.0 / HEAD_SIZE), np.float32)
    angles = positions.astype(jnp.float32)[:, None, None] * frequency
    return jnp.cos(angles), jnp.sin(angles)


def rotate(values, cosine_term, sine_term):
    halfway = values.shape[-1] // 2
    first_half = values[..., :halfway]
    second_half = values[..., halfway:]
    return jnp.concatenate(
        [
            first_half * cosine_term - second_half * sine_term,
            second_half * cosine_term + first_half * sine_term,
        ],
        axis=-1,
    )


def repeat_counts(recent_ids, first_column, width):
    columns = first_column + jnp.arange(width, dtype=jnp.int32)
    return jnp.sum((recent_ids[:, :, None] == columns[None, None, :]).astype(jnp.float32), 1)


def body(
    hidden,
    cached_rotated_keys,
    cached_values,
    cache_lengths,
    recent_ids,
    guidance,
    w_query,
    key_value_weight,
    w_output,
    norm_gain,
    w_head,
):
    streams, dps, tensors = (lax.axis_size(axis) for axis in ("stream", "dp", "tensor"))
    stream, dp, tensor = (lax.axis_index(axis) for axis in ("stream", "dp", "tensor"))
    local_width = hidden.shape[2]
    query_cols = w_query.shape[1]
    kv_cols = key_value_weight.shape[2]
    local_prompts = cache_lengths.shape[1]
    hidden_prompts = hidden.shape[1]
    prompts = recent_ids.shape[0]
    lengths = cache_lengths[0]
    vocab_local = w_head.shape[1]

    hidden_blocks = gather_swapped(hidden[0], "tensor")
    all_rows = jnp.concatenate(hidden_blocks, axis=0)
    w_query, key_value_weight, stream, dp, tensor = lax.optimization_barrier(
        (w_query, key_value_weight, stream, dp, tensor)
    )
    projected_parts = matmul(
        hidden_blocks, load_projections(w_query, key_value_weight), jnp.bfloat16
    )
    (projected_parts, lengths, recent_ids, guidance, norm_gain, stream, dp, tensor) = (
        lax.optimization_barrier(
            (projected_parts, lengths, recent_ids, guidance, norm_gain, stream, dp, tensor)
        )
    )
    column_base = (dp * tensors + tensor) * vocab_local
    cosine_term, sine_term = rotation(lengths)

    def hidden_place(prompt):
        block = prompt // hidden_prompts
        return (tensors - 1 - (tensor ^ block)) * hidden_prompts + prompt % hidden_prompts

    gain_rows = norm_gain.reshape(local_prompts, -1)
    total_cols = query_cols + 2 * kv_cols
    projected, gain_blocks = 0.0, []
    for distance in far_first("dp"):
        sending = lax.dynamic_slice_in_dim(
            projected_parts, hidden_place((dp ^ distance) * local_prompts), local_prompts, 0
        )
        arrived = swap(jnp.concatenate([sending, gain_rows], axis=1), "dp", distance)
        projected = projected + arrived[:, :total_cols].astype(jnp.float32)
        gain_blocks.append(arrived[:, total_cols:].reshape(local_width))
    gain = jnp.zeros((local_width * dps,), norm_gain.dtype)
    for distance, block in zip(far_first("dp"), gain_blocks):
        gain = lax.dynamic_update_slice_in_dim(gain, block, (dp ^ distance) * local_width, 0)

    query_heads = query_cols // HEAD_SIZE
    kv_heads = kv_cols // HEAD_SIZE
    rotated_query = rotate(
        projected[:, :query_cols].reshape(local_prompts, query_heads, HEAD_SIZE),
        cosine_term,
        sine_term,
    ).astype(jnp.bfloat16)
    key_value_rows = projected[:, query_cols:].reshape(local_prompts, 2, kv_heads, HEAD_SIZE)
    fresh_key = rotate(key_value_rows[:, 0], cosine_term, sine_term).astype(jnp.bfloat16)
    value_new = key_value_rows[:, 1].astype(jnp.bfloat16)
    grouped_queries = rotated_query.reshape(
        local_prompts, kv_heads, query_heads // kv_heads, HEAD_SIZE
    )
    attention_scale = HEAD_SIZE ** (-0.5)
    key_block = cached_rotated_keys[0]
    value_block = cached_values[0]
    scores = (
        jnp.einsum(
            "pkgd,pksd->pkgs", grouped_queries, key_block, preferred_element_type=jnp.float32
        )
        * attention_scale
    )
    self_score = (
        jnp.einsum("pkgd,pkd->pkg", grouped_queries, fresh_key, preferred_element_type=jnp.float32)
        * attention_scale
    )
    valid = jnp.arange(key_block.shape[2], dtype=jnp.int32)[None, :] < lengths[:, None]
    exps = jnp.where(valid[:, None, None, :], jnp.exp(scores), 0.0)
    own_exp = jnp.exp(self_score)
    denominator = jnp.sum(exps, -1) + own_exp
    weights = (exps / denominator[..., None]).astype(jnp.bfloat16)
    own_weight = (own_exp / denominator).astype(jnp.bfloat16)
    attended = jnp.einsum(
        "pkgs,pksd->pkgd", weights, value_block, preferred_element_type=jnp.float32
    )
    attended = (
        attended
        + own_weight.astype(jnp.float32)[..., None] * value_new.astype(jnp.float32)[:, :, None, :]
    )
    attended = attended.reshape(local_prompts, query_cols).astype(jnp.bfloat16)

    half = prompts // streams
    recent_mine = lax.dynamic_slice_in_dim(recent_ids, stream * half, half, 0)
    penalty = penalty_step * repeat_counts(recent_mine, column_base, vocab_local)
    attended, penalty = lax.optimization_barrier((attended, penalty))

    attended_blocks = gather_swapped(attended, "dp")
    w_output, _ = lax.optimization_barrier((w_output, attended))
    partial_out = matmul(attended_blocks, [load_to_vmem(w_output)], jnp.bfloat16)

    share = half // tensors

    def partial_rows(tensor_to):
        parts = []
        for other in range(streams):
            prompt = (stream ^ other) * half + tensor_to * share
            block = dps - 1 - (dp ^ (prompt // local_prompts))
            place = block * local_prompts + prompt % local_prompts
            parts.append(lax.dynamic_slice_in_dim(partial_out, place, share, 0))
        return jnp.concatenate(parts, axis=0)

    def hidden_rows(stream_to):
        place = hidden_place(stream_to * half + tensor * share)
        return lax.dynamic_slice_in_dim(all_rows, place, share, 0).astype(jnp.float32)

    summed = jnp.concatenate([hidden_rows(stream ^ other) for other in range(streams)], axis=0)
    for distance in far_first("tensor"):
        arrived = swap(partial_rows(tensor ^ distance), "tensor", distance)
        summed = summed + arrived.astype(jnp.float32)
    residuals = summed.astype(jnp.bfloat16).reshape(streams, share, local_width)
    pair = [swap(residuals[other], "stream", other) for other in range(streams)]
    pair = jnp.concatenate(pair, axis=0)

    whole = jnp.zeros((streams * share, local_width * dps), jnp.bfloat16)
    for distance, block in zip(far_first("dp"), gather_swapped(pair, "dp")):
        whole = lax.dynamic_update_slice_in_dim(whole, block, (dp ^ distance) * local_width, 1)
    whole = whole.reshape(streams, share, -1).astype(jnp.float32)
    inverse = lax.rsqrt(jnp.sum(whole * whole, 2) / MODEL_WIDTH + norm_eps)
    guide = lax.dynamic_slice_in_dim(guidance, stream * half + tensor * share, share, 0)
    own_guide = jnp.where(stream == 0, guide, 1.0 - guide)
    factors = inverse * jnp.stack([own_guide, 1.0 - own_guide])
    mixed = jnp.sum(whole * factors[:, :, None], 0) * gain.astype(jnp.float32)
    mixed = mixed.astype(jnp.bfloat16)

    mixed_blocks = [swap(mixed, "tensor", distance) for distance in range(tensors)]
    w_head, _ = lax.optimization_barrier((w_head, mixed))
    guided = head(mixed_blocks, load_to_vmem(w_head), penalty)
    totals = sum_totals(jnp.sum(jnp.exp(guided), 1), ("dp", "tensor"))
    return guided - jnp.log(totals)[:, None]


def solution(mesh):
    return jax.shard_map(
        body,
        mesh=mesh,
        in_specs=(
            P("stream", "tensor", "dp"),
            P("stream", "dp", "tensor", None, None),
            P("stream", "dp", "tensor", None, None),
            P("stream", "dp"),
            P(),
            P(),
            P("dp", "tensor"),
            P("dp", None, "tensor"),
            P("tensor", "dp"),
            P("dp"),
            P(None, ("dp", "tensor")),
        ),
        out_specs=P("stream", ("dp", "tensor")),
        check_vma=False,
    )
```

```python
import math

import jax
import jax.numpy as jnp
import numpy as np
from jax import lax
from jax.experimental import pallas as pl
from jax.experimental.pallas import tpu as pltpu
from jax.sharding import PartitionSpec as P

MODEL_WIDTH = 8192
HEAD_SIZE = 128


rope_theta = 500000.0
penalty_step = 1.5
norm_eps = 1e-05


def swap(value, axis, distance):
    if distance == 0:
        return value
    pairs = [(source, source ^ distance) for source in range(lax.axis_size(axis))]
    return lax.ppermute(value, axis, pairs)


def far_first(axis):
    return range(lax.axis_size(axis) - 1, -1, -1)


def gather_swapped(value, axis):
    return [swap(value, axis, distance) for distance in far_first(axis)]


def sum_totals(value, axes):
    count = lax.axis_size(axes)
    copies = jnp.broadcast_to(value[None], (count,) + value.shape)
    return jnp.sum(lax.all_to_all(copies, axes, 0, 0, tiled=True), 0)


def matmul_kernel(row_blocks, *refs):
    blocks, weights, out_ref = refs[:row_blocks], refs[row_blocks:-1], refs[-1]
    rows = jnp.concatenate([block[...] for block in blocks], axis=0)
    first = 0
    for weight in weights:
        last = first + weight.shape[1]
        product = jnp.dot(rows, weight[...], preferred_element_type=jnp.float32)
        out_ref[:, first:last] = product.astype(out_ref.dtype)
        first = last


def matmul(blocks, weights, dtype):
    rows = sum(block.shape[0] for block in blocks)
    cols = sum(weight.shape[1] for weight in weights)
    depth = weights[0].shape[0]
    whole = pl.BlockSpec(memory_space=pltpu.VMEM)
    return pl.pallas_call(
        lambda *refs: matmul_kernel(len(blocks), *refs),
        out_shape=jax.ShapeDtypeStruct((rows, cols), dtype),
        in_specs=[whole] * (len(blocks) + len(weights)),
        out_specs=whole,
        compiler_params=pltpu.CompilerParams(vmem_limit_bytes=8 * 1024 * 1024),
        cost_estimate=pl.CostEstimate(
            flops=2 * rows * cols * depth,
            bytes_accessed=2 * (depth * (rows + cols) + rows * cols),
            transcendentals=0,
        ),
    )(*blocks, *[pltpu.with_memory_space_constraint(weight, pltpu.VMEM) for weight in weights])


def head_kernel(*refs):
    blocks, (weight_ref, penalty_ref, out_ref) = refs[:-3], refs[-3:]
    rows = jnp.concatenate([block[...] for block in blocks], axis=0)
    logits = jnp.dot(rows, weight_ref[...], preferred_element_type=jnp.float32)
    share = blocks[0].shape[0]
    tensor = lax.axis_index("tensor")
    for i in range(len(blocks)):
        place = pl.ds(pl.multiple_of((tensor ^ (len(blocks) - 1 - i)) * share, 8), share)
        out_ref[place, :] = logits[i * share : (i + 1) * share] - penalty_ref[place, :]


def head(blocks, weight, penalty):
    whole = pl.BlockSpec(memory_space=pltpu.VMEM)
    rows, cols = penalty.shape
    depth = weight.shape[0]
    return pl.pallas_call(
        head_kernel,
        out_shape=jax.ShapeDtypeStruct((rows, cols), jnp.float32),
        in_specs=[whole] * (len(blocks) + 2),
        out_specs=whole,
        compiler_params=pltpu.CompilerParams(vmem_limit_bytes=8 * 1024 * 1024),
        cost_estimate=pl.CostEstimate(
            flops=2 * rows * cols * depth,
            bytes_accessed=2 * depth * (rows + cols) + 8 * rows * cols,
            transcendentals=0,
        ),
    )(*blocks, pltpu.with_memory_space_constraint(weight, pltpu.VMEM), penalty)


def load_kernel(weight_ref, out_ref, sems):
    pieces = sems.shape[0]
    rows = out_ref.shape[0] // pieces
    copies = []
    for piece in range(pieces):
        part = pl.ds(piece * rows, rows)
        copy = pltpu.make_async_copy(weight_ref.at[part], out_ref.at[part], sems.at[piece])
        copy.start()
        copies.append(copy)
    for copy in copies:
        copy.wait()


def load_to_vmem(weight):
    return pl.pallas_call(
        load_kernel,
        out_shape=pltpu.VMEM(weight.shape, weight.dtype),
        in_specs=[pl.BlockSpec(memory_space=pltpu.HBM)],
        out_specs=pl.BlockSpec(memory_space=pltpu.VMEM),
        scratch_shapes=[pltpu.SemaphoreType.DMA((4,))],
        compiler_params=pltpu.CompilerParams(vmem_limit_bytes=8 * 1024 * 1024),
        cost_estimate=pl.CostEstimate(
            flops=0, bytes_accessed=4 * weight.size, transcendentals=0
        ),
    )(pltpu.with_memory_space_constraint(weight, pltpu.HBM))


LANES = 128


def load_projections_kernel(query_ref, pair_ref, query_out, pair_out, pair_raw, wide, sems):
    parts, depth, members, _ = pair_raw.shape
    cols = pair_ref.shape[2]
    step = wide.shape[0] // members
    copies = []
    for part in range(parts):
        lanes = pl.ds(part * LANES, LANES)
        copy = pltpu.make_async_copy(
            pair_ref.at[:, :, lanes], pair_raw.at[part], sems.at[part]
        )
        copy.start()
        copies.append(copy)
    query_copy = pltpu.make_async_copy(query_ref, query_out, sems.at[parts])
    query_copy.start()
    for part in range(parts):
        copies[part].wait()
        rows_in_turn = pair_raw.at[part].reshape(depth * members, LANES)

        def relayout(index, carry, rows_in_turn=rows_in_turn, part=part):
            source = pl.ds(pl.multiple_of(index * step * members, step * members), step * members)
            wide[...] = rows_in_turn[source, :].astype(jnp.float32)
            target = pl.ds(pl.multiple_of(index * step, step), step)
            for member in range(members):
                first = member * cols + part * LANES
                rows = wide[pl.ds(member, step, stride=members), :]
                pair_out[target, first : first + LANES] = rows.astype(pair_out.dtype)
            return carry

        lax.fori_loop(0, depth // step, relayout, 0)
    query_copy.wait()


def load_projections(query, pair):
    depth, members, cols = pair.shape
    parts = cols // LANES
    step = math.gcd(depth, 256)
    arrays = [pltpu.with_memory_space_constraint(array, pltpu.HBM) for array in (query, pair)]
    return pl.pallas_call(
        load_projections_kernel,
        out_shape=(
            pltpu.VMEM(query.shape, query.dtype),
            pltpu.VMEM((depth, members * cols), pair.dtype),
        ),
        in_specs=[pl.BlockSpec(memory_space=pltpu.HBM)] * 2,
        out_specs=[pl.BlockSpec(memory_space=pltpu.VMEM)] * 2,
        scratch_shapes=[
            pltpu.VMEM((parts, depth, members, LANES), pair.dtype),
            pltpu.VMEM((step * members, LANES), jnp.float32),
            pltpu.SemaphoreType.DMA((parts + 1,)),
        ],
        compiler_params=pltpu.CompilerParams(vmem_limit_bytes=16 * 1024 * 1024),
        cost_estimate=pl.CostEstimate(
            flops=0, bytes_accessed=4 * (query.size + pair.size), transcendentals=0
        ),
    )(*arrays)


def rotation(positions):
    halfway = HEAD_SIZE // 2
    frequency = np.asarray(rope_theta ** (-np.arange(halfway) * 2.0 / HEAD_SIZE), np.float32)
    angles = positions.astype(jnp.float32)[:, None, None] * frequency
    return jnp.cos(angles), jnp.sin(angles)


def rotate(values, cosine_term, sine_term):
    halfway = values.shape[-1] // 2
    first_half = values[..., :halfway]
    second_half = values[..., halfway:]
    return jnp.concatenate(
        [
            first_half * cosine_term - second_half * sine_term,
            second_half * cosine_term + first_half * sine_term,
        ],
        axis=-1,
    )


def repeat_counts(recent_ids, first_column, width):
    columns = first_column + jnp.arange(width, dtype=jnp.int32)
    return jnp.sum((recent_ids[:, :, None] == columns[None, None, :]).astype(jnp.float32), 1)


def body(
    hidden,
    cached_rotated_keys,
    cached_values,
    cache_lengths,
    recent_ids,
    guidance,
    w_query,
    key_value_weight,
    w_output,
    norm_gain,
    w_head,
):
    streams, dps, tensors = (lax.axis_size(axis) for axis in ("stream", "dp", "tensor"))
    stream, dp, tensor = (lax.axis_index(axis) for axis in ("stream", "dp", "tensor"))
    local_width = hidden.shape[2]
    query_cols = w_query.shape[1]
    kv_cols = key_value_weight.shape[2]
    local_prompts = cache_lengths.shape[1]
    hidden_prompts = hidden.shape[1]
    prompts = recent_ids.shape[0]
    lengths = cache_lengths[0]
    vocab_local = w_head.shape[1]

    hidden_blocks = gather_swapped(hidden[0], "tensor")
    all_rows = jnp.concatenate(hidden_blocks, axis=0)
    w_query, key_value_weight, stream, dp, tensor = lax.optimization_barrier(
        (w_query, key_value_weight, stream, dp, tensor)
    )
    projected_parts = matmul(
        hidden_blocks, load_projections(w_query, key_value_weight), jnp.bfloat16
    )
    (projected_parts, lengths, recent_ids, guidance, norm_gain, stream, dp, tensor) = (
        lax.optimization_barrier(
            (projected_parts, lengths, recent_ids, guidance, norm_gain, stream, dp, tensor)
        )
    )
    column_base = (dp * tensors + tensor) * vocab_local
    cosine_term, sine_term = rotation(lengths)

    def hidden_place(prompt):
        block = prompt // hidden_prompts
        return (tensors - 1 - (tensor ^ block)) * hidden_prompts + prompt % hidden_prompts

    gain_rows = norm_gain.reshape(local_prompts, -1)
    total_cols = query_cols + 2 * kv_cols
    projected, gain_blocks = 0.0, []
    for distance in far_first("dp"):
        sending = lax.dynamic_slice_in_dim(
            projected_parts, hidden_place((dp ^ distance) * local_prompts), local_prompts, 0
        )
        arrived = swap(jnp.concatenate([sending, gain_rows], axis=1), "dp", distance)
        projected = projected + arrived[:, :total_cols].astype(jnp.float32)
        gain_blocks.append(arrived[:, total_cols:].reshape(local_width))
    gain = jnp.zeros((local_width * dps,), norm_gain.dtype)
    for distance, block in zip(far_first("dp"), gain_blocks):
        gain = lax.dynamic_update_slice_in_dim(gain, block, (dp ^ distance) * local_width, 0)

    query_heads = query_cols // HEAD_SIZE
    kv_heads = kv_cols // HEAD_SIZE
    rotated_query = rotate(
        projected[:, :query_cols].reshape(local_prompts, query_heads, HEAD_SIZE),
        cosine_term,
        sine_term,
    ).astype(jnp.bfloat16)
    key_value_rows = projected[:, query_cols:].reshape(local_prompts, 2, kv_heads, HEAD_SIZE)
    fresh_key = rotate(key_value_rows[:, 0], cosine_term, sine_term).astype(jnp.bfloat16)
    value_new = key_value_rows[:, 1].astype(jnp.bfloat16)
    grouped_queries = rotated_query.reshape(
        local_prompts, kv_heads, query_heads // kv_heads, HEAD_SIZE
    )
    attention_scale = HEAD_SIZE ** (-0.5)
    key_block = cached_rotated_keys[0]
    value_block = cached_values[0]
    scores = (
        jnp.einsum(
            "pkgd,pksd->pkgs", grouped_queries, key_block, preferred_element_type=jnp.float32
        )
        * attention_scale
    )
    self_score = (
        jnp.einsum("pkgd,pkd->pkg", grouped_queries, fresh_key, preferred_element_type=jnp.float32)
        * attention_scale
    )
    valid = jnp.arange(key_block.shape[2], dtype=jnp.int32)[None, :] < lengths[:, None]
    exps = jnp.where(valid[:, None, None, :], jnp.exp(scores), 0.0)
    own_exp = jnp.exp(self_score)
    denominator = jnp.sum(exps, -1) + own_exp
    weights = (exps / denominator[..., None]).astype(jnp.bfloat16)
    own_weight = (own_exp / denominator).astype(jnp.bfloat16)
    attended = jnp.einsum(
        "pkgs,pksd->pkgd", weights, value_block, preferred_element_type=jnp.float32
    )
    attended = (
        attended
        + own_weight.astype(jnp.float32)[..., None] * value_new.astype(jnp.float32)[:, :, None, :]
    )
    attended = attended.reshape(local_prompts, query_cols).astype(jnp.bfloat16)

    half = prompts // streams
    recent_mine = lax.dynamic_slice_in_dim(recent_ids, stream * half, half, 0)
    penalty = penalty_step * repeat_counts(recent_mine, column_base, vocab_local)
    attended, penalty = lax.optimization_barrier((attended, penalty))

    attended_blocks = gather_swapped(attended, "dp")
    w_output, _ = lax.optimization_barrier((w_output, attended))
    partial_out = matmul(attended_blocks, [load_to_vmem(w_output)], jnp.bfloat16)

    share = half // tensors

    def partial_rows(tensor_to):
        parts = []
        for other in range(streams):
            prompt = (stream ^ other) * half + tensor_to * share
            block = dps - 1 - (dp ^ (prompt // local_prompts))
            place = block * local_prompts + prompt % local_prompts
            parts.append(lax.dynamic_slice_in_dim(partial_out, place, share, 0))
        return jnp.concatenate(parts, axis=0)

    def hidden_rows(stream_to):
        place = hidden_place(stream_to * half + tensor * share)
        return lax.dynamic_slice_in_dim(all_rows, place, share, 0).astype(jnp.float32)

    summed = jnp.concatenate([hidden_rows(stream ^ other) for other in range(streams)], axis=0)
    for distance in far_first("tensor"):
        arrived = swap(partial_rows(tensor ^ distance), "tensor", distance)
        summed = summed + arrived.astype(jnp.float32)
    residuals = summed.astype(jnp.bfloat16).reshape(streams, share, local_width)
    pair = [swap(residuals[other], "stream", other) for other in range(streams)]
    pair = jnp.concatenate(pair, axis=0)

    whole = jnp.zeros((streams * share, local_width * dps), jnp.bfloat16)
    for distance, block in zip(far_first("dp"), gather_swapped(pair, "dp")):
        whole = lax.dynamic_update_slice_in_dim(whole, block, (dp ^ distance) * local_width, 1)
    whole = whole.reshape(streams, share, -1).astype(jnp.float32)
    inverse = lax.rsqrt(jnp.sum(whole * whole, 2) / MODEL_WIDTH + norm_eps)
    guide = lax.dynamic_slice_in_dim(guidance, stream * half + tensor * share, share, 0)
    own_guide = jnp.where(stream == 0, guide, 1.0 - guide)
    factors = inverse * jnp.stack([own_guide, 1.0 - own_guide])
    mixed = jnp.sum(whole * factors[:, :, None], 0) * gain.astype(jnp.float32)
    mixed = mixed.astype(jnp.bfloat16)

    mixed_blocks = gather_swapped(mixed, "tensor")
    w_head, _ = lax.optimization_barrier((w_head, mixed))
    guided = head(mixed_blocks, load_to_vmem(w_head), penalty)
    totals = sum_totals(jnp.sum(jnp.exp(guided), 1), ("dp", "tensor"))
    return guided - jnp.log(totals)[:, None]


def solution(mesh):
    return jax.shard_map(
        body,
        mesh=mesh,
        in_specs=(
            P("stream", "tensor", "dp"),
            P("stream", "dp", "tensor", None, None),
            P("stream", "dp", "tensor", None, None),
            P("stream", "dp"),
            P(),
            P(),
            P("dp", "tensor"),
            P("dp", None, "tensor"),
            P("tensor", "dp"),
            P("dp"),
            P(None, ("dp", "tensor")),
        ),
        out_specs=P("stream", ("dp", "tensor")),
        check_vma=False,
    )
```
